32 devices in a mesh: fsdp: 8 (over z, y), tp: 4 (over x, core).
Axes of the slice: x: 2, y: 2, z: 4, core: 2. Of those that a mesh axis runs over, the one named last changes fastest.
Arguments:
- tokens: bfloat16 [2, 16384, 768], P(None, ('fsdp', 'tp')), may hold values from -6 to 6
- cotangent: bfloat16 [2, 16384, 768], P(None, ('fsdp', 'tp')), may hold values from -6 to 6
- gain_attn: float32 [768], replicated, may hold values from 0.5 to 1.5
- gain_moe: float32 [768], replicated, may hold values from 0.5 to 1.5
- qkv_weight: bfloat16 [768, 2304], P('fsdp', 'tp'), may hold values from -0.21875 to 0.21875
- out_weight: bfloat16 [768, 768], P('tp', 'fsdp'), may hold values from -3.5 to 3.5
- router: bfloat16 [768, 8], replicated, may hold values from -0.15625 to 0.15625
- w_in: bfloat16 [8, 768, 3072], P(None, 'fsdp', 'tp'), may hold values from -0.21875 to 0.21875
- w_out: bfloat16 [8, 3072, 768], P(None, 'tp', 'fsdp'), may hold values from -0.109375 to 0.109375
- doc_lengths: int32 [2, 8, 4], P(None, 'fsdp'), may hold values from 1 to 1792, 2048 in all within a row
- routes: int32 [2, 16384, 2], P(None, 'fsdp'), may hold values from 0 to 7, all different within a row; in each aligned block of 2048 rows (0 to 2047, 2048 to 4095, ..., all dimensions but the last counted through in order) at most 768 rows name the same one
- capacity: int32 [8], replicated, may hold values from 384 to 768, as said below
Outputs:
- output: bfloat16 [2, 16384, 768], P(None, ('fsdp', 'tp'))
- grad_tokens: bfloat16 [2, 16384, 768], P(None, ('fsdp', 'tp'))
- grad_gain_attn: float32 [768], replicated
- grad_gain_moe: float32 [768], replicated
- grad_qkv: float32 [768, 2304], P('fsdp', 'tp')
- grad_out: float32 [768, 768], P('tp', 'fsdp')
- grad_router: float32 [768, 8], replicated
- grad_w_in: float32 [8, 768, 3072], P(None, 'fsdp', 'tp')
- grad_w_out: float32 [8, 3072, 768], P(None, 'tp', 'fsdp')
The draws below stay inside these ranges and needn't reach their ends.
Inputs may be any that keep to these rules, and one draw needn't show every extreme that they name: `routes`: each row names two different experts. In each aligned block of 2048 rows (one sequence) no expert is named by more than 768 rows, a bound that some block reaches. `capacity`: each is at least 384, and one expert's is exactly 768. `doc_lengths`: the 4 lengths of a sequence sum to 2048; the longest is exactly 1792.
All inputs are finite; a program needn't handle non-finite values.
Results may differ from the reference program's by a relative error of at most 0.02.
Values may be sent and summed in bfloat16 or wider, within the bound.
A program may use at most 256 MiB of HBM per device.

```python
import math
import jax
import jax.numpy as jnp
import numpy as np
from jax import lax

D = 768
HEADS = 12
HEAD_DIM = 64
FF = 3072
EXPERTS = 8
SEQ = 2048
WINDOW = 1024
QBLOCK = 512
DOCS = 4
MICRO = 2
SEQS_DEV = 1
TOKENS = 16384
MOST = 1792
CAP = 768
N_FSDP = 8


def draw_capacity(key, part):
    key = jax.random.fold_in(key, 11)
    first_key, second_key = jax.random.split(key)
    values = jax.random.randint(first_key, (EXPERTS,), CAP // 2, CAP + 1)
    chosen = jax.random.randint(second_key, (), 0, EXPERTS)
    return jnp.where(jnp.arange(EXPERTS) == chosen, CAP, values).astype(jnp.int32)


def level_of(stream_key, shape, cuts, smallest, largest):
    def one(axis_at, parts):
        draws = jax.random.uniform(jax.random.fold_in(jax.random.fold_in(stream_key, 6), axis_at), (parts,), jnp.float32, smallest / len(cuts), largest / len(cuts))
        return jnp.repeat(jnp.exp(draws), shape[axis_at] // parts).reshape((-1,) + (1,) * (len(shape) - axis_at - 1))

    level = one(*cuts[0])
    for cut in cuts[1:]:
        level = level * one(*cut)
    return level


def profile(count, total, most, lean):
    portions = [(1 << 20) // math.isqrt(standing ** lean) + 1 for standing in range(2, count + 1)]
    spare, given = total - most - (count - 1), [1] * (count - 1)
    while spare > 0:
        candidates = [i for i in range(count - 1) if given[i] < most]
        mass, left = sum([portions[i] for i in candidates]), spare
        for i in candidates:
            addition = min(most - given[i], max(1, left * portions[i] // mass), spare)
            given[i] = given[i] + addition
            spare = spare - addition
    return np.array([most] + given)


def uneven(key, number_of, total, most, lean):
    if number_of == 2:
        one = jax.random.randint(key, (), max(1, total - most), min(most, total - 1) + 1)
        return jnp.stack([one, total - one])
    sizes = jnp.asarray(profile(number_of, total, most, lean), jnp.int32)
    couples = (number_of - 1) // 2
    source_of, sink = sizes[1:1 + 2 * couples:2], sizes[2:2 + 2 * couples:2]
    margin = jnp.minimum(source_of - 1, most - sink)
    shifted = jax.random.randint(jax.random.fold_in(key, 1), (couples,), 0, 1 << 20) % (margin + 1)
    sizes = sizes.at[1:1 + 2 * couples:2].set(source_of - shifted).at[2:2 + 2 * couples:2].set(sink + shifted)
    return sizes[jax.random.permutation(jax.random.fold_in(key, 2), number_of)]


def shared_out(stream_key, own, number, rows, amount, top, bound, slope):
    sequence = jax.random.permutation(stream_key, amount)
    crowded, common = portions_of(amount, rows * top, bound, slope, True), portions_of(amount, rows * top, bound, slope, False)
    places = jnp.arange(amount)

    def named(tallies, turn):
        used = int((tallies > 0).sum())
        fixed = max(1, used // 4)
        shifted = fixed + (places - fixed + turn * (used - fixed)) % max(1, amount - fixed)
        return jnp.zeros((amount,), jnp.int32).at[sequence[jnp.where(places < fixed, places, shifted)]].set(jnp.asarray(tallies, jnp.int32))

    tallies = jnp.where(number % 4 == 0, named(crowded, number // 4), named(common, number - number // 4 - 1))
    mixed = jax.random.permutation(jax.random.fold_in(own, 3), amount)
    source_of, receiver = mixed[0:amount // 2 * 2:2], mixed[1:amount // 2 * 2:2]
    room = jnp.minimum(tallies[source_of] - 1, bound - tallies[receiver]) // 2
    room = jnp.where((source_of == sequence[0]) | (receiver == sequence[0]) | (tallies[receiver] == 0), 0, jnp.maximum(room, 0))
    shifted = jax.random.randint(jax.random.fold_in(own, 4), (amount // 2,), 0, 1 << 20) % (room + 1)
    tallies = tallies.at[source_of].add(-shifted).at[receiver].add(shifted)
    labels = jnp.searchsorted(jnp.cumsum(tallies), jnp.arange(rows * top), side="right").astype(jnp.int32)
    listing = labels.reshape(top, rows).T
    listing = listing[jax.random.permutation(jax.random.fold_in(own, 1), rows)]
    turn = jax.random.randint(jax.random.fold_in(own, 2), (rows, 1), 0, top)
    return jnp.take_along_axis(listing, (jnp.arange(top)[None, :] + turn) % top, axis=1)


def portions_of(number_of, total, reach, skew, full):
    loads = [(1 << 20) // math.isqrt(standing ** skew) + 1 for standing in range(1, number_of + 1)]
    largest = reach if full else min(reach, max(-(-total // number_of), total * loads[0] // sum(loads)))
    least = 1 if total - largest >= number_of - 1 else 0
    holding, surplus = [largest] + [least] * (number_of - 1), total - largest - least * (number_of - 1)
    while surplus > 0:
        free = [i for i in range(1, number_of) if holding[i] < largest] or [i for i in range(1, number_of) if holding[i] < reach]
        whole, left = sum([loads[i] for i in free]), surplus
        for i in free:
            addition = min(reach - holding[i], max(1, left * loads[i] // whole), surplus)
            holding[i] = holding[i] + addition
            surplus = surplus - addition
    return np.array(holding)


def gaussian(key, dims, deviation, most, pieces=(), held_as=jnp.bfloat16):
    entries = deviation * jax.random.normal(key, dims, jnp.float32)
    if pieces:
        entries = entries * level_of(key, dims, pieces, -0.22, 0.18)
    return jnp.clip(entries, -most, most).astype(held_as)


def setup_inputs(seed: int = 0) -> dict:
    splits = jax.random.split(jax.random.key(seed), 13)
    tokens = gaussian(splits[0], (MICRO, TOKENS, D), 1.0, 6.0, ((1, 32),))
    cotangent = gaussian(splits[1], (MICRO, TOKENS, D), 1.0, 6.0, ((1, 32),))
    gain_attn = jnp.clip(1.0 + 0.1 * jax.random.normal(splits[2], (D,), jnp.float32), 0.5, 1.5)
    gain_moe = jnp.clip(1.0 + 0.1 * jax.random.normal(splits[3], (D,), jnp.float32), 0.5, 1.5)
    qkv_weight = gaussian(splits[4], (D, 3 * D), D ** -0.5, 0.21875, ((0, 8), (1, 4)))
    out_weight = gaussian(splits[5], (D, D), (max(D // 256, 1)) ** -0.5, 3.5, ((0, 4), (1, 8)))
    router = gaussian(splits[6], (D, EXPERTS), (2 * D) ** -0.5, 0.15625)
    w_in = gaussian(splits[7], (EXPERTS, D, FF), D ** -0.5, 0.21875, ((1, 8), (2, 4)))
    w_out = gaussian(splits[8], (EXPERTS, FF, D), FF ** -0.5, 0.109375, ((1, 4), (2, 8)))
    doc_lengths = jax.vmap(lambda own: uneven(own, DOCS, SEQ, MOST, 2))(jax.random.split(splits[9], MICRO * (N_FSDP * SEQS_DEV))).reshape((MICRO, N_FSDP * SEQS_DEV, DOCS)).astype(jnp.int32)
    routes_keys = jax.random.split(jax.random.fold_in(splits[10], 1), MICRO * TOKENS // SEQ)
    routes_turns = jax.random.permutation(jax.random.fold_in(splits[10], 3), MICRO * TOKENS // SEQ)
    routes = jax.vmap(lambda own, number: shared_out(jax.random.fold_in(splits[10], 2), own, number, SEQ, EXPERTS, 2, CAP, 1))(routes_keys, routes_turns).reshape((MICRO, TOKENS, 2))
    capacity = draw_capacity(jax.random.fold_in(splits[12], 71), 0)
    return {"tokens": tokens, "cotangent": cotangent, "gain_attn": gain_attn, "gain_moe": gain_moe, "qkv_weight": qkv_weight, "out_weight": out_weight, "router": router, "w_in": w_in, "w_out": w_out, "doc_lengths": doc_lengths, "routes": routes, "capacity": capacity}


epsilon = 1e-06
neg_big = -1e+30
highest = lax.Precision.HIGHEST

@jax.custom_vjp
def low(v):
    return lax.optimization_barrier(v.astype(jnp.bfloat16)).astype(jnp.float32)

@jax.custom_vjp
def low_back(v):
    return v

def low_keep(v):
    return (low(v), None)

def low_pass(kept, grad):
    return (grad,)

def back_keep(v):
    return (v, None)

def back_low(kept, grad):
    return (low(grad),)
low.defvjp(low_keep, low_pass)
low_back.defvjp(back_keep, back_low)

def matmul(left, right):
    return jnp.dot(left, right, precision=highest, preferred_element_type=jnp.float32)

def norm_scaled(values, gain):
    return values * lax.rsqrt(lax.optimization_barrier(jnp.mean(values * values, axis=-1, keepdims=True)) + epsilon) * gain

def doc_numbers(lengths, seq_len):
    ends = jnp.cumsum(lengths)
    places = jnp.arange(seq_len, dtype=jnp.int32)
    return lax.optimization_barrier(jnp.sum((places[:, None] >= ends[None, :]).astype(jnp.int32), axis=1))

def block_mask(start, docs_pad):
    q_place = start + jnp.arange(QBLOCK, dtype=jnp.int32)
    k_place = start - WINDOW + jnp.arange(QBLOCK + WINDOW, dtype=jnp.int32)
    q_doc = lax.dynamic_slice_in_dim(docs_pad, start + WINDOW, QBLOCK, 0)
    k_doc = lax.dynamic_slice_in_dim(docs_pad, start, QBLOCK + WINDOW, 0)
    causal = k_place[None, :] <= q_place[:, None]
    inside = q_place[:, None] - k_place[None, :] < WINDOW
    return causal & inside & (q_doc[:, None] == k_doc[None, :])

def dispatch(picks, capacity, experts, seq_len):
    onehot = (picks[:, :, None] == jnp.arange(experts, dtype=jnp.int32)[None, None, :]).astype(jnp.int32)
    per_token = lax.optimization_barrier(jnp.sum(onehot, axis=1))
    before = jnp.cumsum(per_token, axis=0) - per_token
    rank = lax.optimization_barrier(jnp.sum(before[:, None, :] * onehot, axis=2))
    limit = lax.optimization_barrier(jnp.sum(capacity[None, None, :] * onehot, axis=2))
    slot = jnp.where(rank < limit, picks * CAP + rank, experts * CAP).astype(jnp.int32)
    owner = jnp.broadcast_to(jnp.arange(seq_len, dtype=jnp.int32)[:, None], (seq_len, 2))
    token_of_slot = jnp.full((experts * CAP,), seq_len, jnp.int32).at[slot.reshape(-1)].set(owner.reshape(-1), mode='drop')
    return (slot, token_of_slot)

def layer(weights, row_in, lengths, picks, capacity):
    gain_attn, gain_moe, qkv_w, attn_w, router_w, in_w, back_w = weights
    experts = in_w.shape[0]
    scale = 1.0 / math.sqrt(HEAD_DIM)
    normed = low(norm_scaled(row_in, gain_attn))
    proj = low_back(low(matmul(normed, qkv_w))).reshape(SEQ, HEADS, 3, HEAD_DIM)
    queries = proj[:, :, 0]
    pad = jnp.zeros((WINDOW, HEADS, HEAD_DIM), jnp.float32)
    keys_pad = jnp.concatenate([pad, proj[:, :, 1]], axis=0)
    values_pad = jnp.concatenate([pad, proj[:, :, 2]], axis=0)
    docs = doc_numbers(lengths, SEQ)
    docs_pad = jnp.concatenate([jnp.full((WINDOW,), -1, jnp.int32), docs])

    def attend_block(start):
        q_blk = lax.dynamic_slice_in_dim(queries, start, QBLOCK, 0)
        k_blk = lax.dynamic_slice_in_dim(keys_pad, start, QBLOCK + WINDOW, 0)
        v_blk = lax.dynamic_slice_in_dim(values_pad, start, QBLOCK + WINDOW, 0)
        raw = jnp.einsum('qhd,khd->hqk', q_blk, k_blk, precision=highest, preferred_element_type=jnp.float32)
        scores = low_back(raw * scale)
        mask = block_mask(start, docs_pad)
        probs = jax.nn.softmax(jnp.where(mask[None], scores, neg_big), axis=-1)
        return jnp.einsum('hqk,khd->qhd', low(probs), v_blk, precision=highest, preferred_element_type=jnp.float32)
    starts = jnp.arange(SEQ // QBLOCK, dtype=jnp.int32) * QBLOCK
    mixed = lax.map(jax.checkpoint(attend_block), starts)
    mixed = low_back(low(mixed.reshape(SEQ, D)))
    hidden = row_in + low_back(matmul(mixed, attn_w))
    normed_moe = low(norm_scaled(hidden, gain_moe))
    logits = matmul(normed_moe, router_w)
    onehot = (picks[:, :, None] == jnp.arange(experts, dtype=jnp.int32)[None, None, :]).astype(jnp.float32)
    chosen = lax.optimization_barrier(jnp.sum(logits[:, None, :] * onehot, axis=2))
    gates = jax.nn.softmax(chosen, axis=-1)
    slot, token_of_slot = dispatch(picks, capacity, experts, SEQ)
    normed_pad = jnp.concatenate([normed_moe, jnp.zeros((1, D), jnp.float32)], axis=0)
    buffer = normed_pad[token_of_slot].reshape(experts, CAP, D)
    pre = low_back(jnp.einsum('ecd,edf->ecf', buffer, in_w, precision=highest, preferred_element_type=jnp.float32))
    act = low(jax.nn.gelu(pre))
    expert_out = low_back(jnp.einsum('ecf,efd->ecd', act, back_w, precision=highest, preferred_element_type=jnp.float32))
    out_pad = jnp.concatenate([expert_out.reshape(experts * CAP, D), jnp.zeros((1, D), jnp.float32)], axis=0)
    picked = out_pad[slot]
    return hidden + lax.optimization_barrier(jnp.sum(gates[:, :, None] * picked, axis=1))

def reference(tokens, cotangent, gain_attn, gain_moe, qkv_weight, out_weight, router, w_in, w_out, doc_lengths, routes, capacity):
    count = MICRO * N_FSDP * SEQS_DEV
    weights = tuple((w.astype(jnp.float32) for w in (gain_attn, gain_moe, qkv_weight, out_weight, router, w_in, w_out)))
    rows_in = tokens.astype(jnp.float32).reshape(count, SEQ, D)
    lens = doc_lengths.reshape(count, DOCS).astype(jnp.int32)
    picks = routes.reshape(count, SEQ, 2).astype(jnp.int32)
    checked = jax.checkpoint(layer)

    def forward(weights, rows_in):

        def step(carry, item):
            return (carry, checked(weights, item[0], item[1], item[2], capacity))
        _, outs = lax.scan(step, jnp.zeros((), jnp.float32), (rows_in, lens, picks))
        return outs
    outs, pull = jax.vjp(forward, weights, rows_in)
    grads, grad_rows = pull(cotangent.astype(jnp.float32).reshape(count, SEQ, D))
    output = outs.reshape(MICRO, TOKENS, D).astype(jnp.bfloat16)
    grad_tokens = grad_rows.reshape(MICRO, TOKENS, D).astype(jnp.bfloat16)
    return (output, grad_tokens, grads[0], grads[1], grads[2], grads[3], grads[4], grads[5], grads[6])
```

```python
import math

import jax
import jax.numpy as jnp
from jax import lax
from jax.experimental import pallas as pl
from jax.experimental.pallas import tpu as pltpu
from jax.sharding import PartitionSpec as P

HEAD_DIM = 64
WINDOW = 1024
CAP = 768
ROW_TILE = 16
QB = 256
CHUNK = 256
EPS = 1e-06
NEG = -1e30
F32 = jnp.float32
BF16 = jnp.bfloat16
I32 = jnp.int32
VMEM_LIMIT = 56 * 1024 * 1024
GELU_A = math.sqrt(2.0 / math.pi)
GELU_B = 0.044715
SIZES = (512, 256, 128, 64, 32, 16)


def dot_nn(a, b):
    return lax.dot_general(a, b, (((1,), (0,)), ((), ())), preferred_element_type=F32)


def dot_nt(a, b):
    return lax.dot_general(a, b, (((1,), (1,)), ((), ())), preferred_element_type=F32)


def dot_tn(a, b):
    return lax.dot_general(a, b, (((0,), (0,)), ((), ())), preferred_element_type=F32)


def params(*semantics):
    return pltpu.CompilerParams(dimension_semantics=semantics, vmem_limit_bytes=VMEM_LIMIT)


def whole(shape):
    zeros = (0,) * len(shape)
    return pl.BlockSpec(shape, lambda *_: zeros)


def attn_fwd_kernel(heads, me_ref, x0, x1, x2, x3, w_ref, lo_ref, proj_ref, mixed_ref, lse_ref,
                    send_ref, keep_ref, x_s, k_s, vt_s, q_s):
    me = me_ref[0]
    step = pl.program_id(0)
    part = x0.shape[0]
    seq = x_s.shape[0]
    nq = seq // QB
    per = part // QB

    @pl.when(step == 0)
    def _():
        for s, ref in enumerate((x0, x1, x2, x3)):
            x_s[pl.ds(pl.multiple_of((me ^ s) * part, part), part), :] = ref[...]

    @pl.when(step < nq)
    def _():
        rows = pl.ds(pl.multiple_of(step * QB, QB), QB)
        proj = dot_nn(x_s[rows, :], w_ref[:, : heads * 3 * HEAD_DIM]).astype(BF16)
        proj_ref[...] = proj
        for h in range(heads):
            base = h * 3 * HEAD_DIM
            q_s[h, rows, :] = proj[:, base : base + HEAD_DIM] * 0.125
            k_s[h, rows, :] = proj[:, base + HEAD_DIM : base + 2 * HEAD_DIM]
            vt_s[h, :, rows] = proj[:, base + 2 * HEAD_DIM : base + 3 * HEAD_DIM].T

    at = step - nq
    turn = at // per
    slot = jnp.where(turn == 0, 1, jnp.where(turn == 1, 3, jnp.where(turn == 2, 0, 2)))
    blk = (me ^ slot) * per + at % per

    def attend(nk):
        start = pl.multiple_of((blk - (nk - 1)) * QB, QB)
        rows = pl.ds(pl.multiple_of(blk * QB, QB), QB)
        keys = pl.ds(start, nk * QB)
        lo = lo_ref[:, rows]
        kpos = start + lax.broadcasted_iota(I32, (nk * QB, QB), 0)
        qpos = blk * QB + lax.broadcasted_iota(I32, (QB, QB), 1)
        outs = []
        for h in range(heads):
            s = dot_nt(k_s[h, keys, :], q_s[h, rows, :])
            s = jnp.where(kpos >= lo, s, NEG)
            last = jnp.where(kpos[(nk - 1) * QB :] <= qpos, s[(nk - 1) * QB :], NEG)
            s = last if nk == 1 else jnp.concatenate([s[: (nk - 1) * QB], last], axis=0)
            top = jnp.max(s, axis=0, keepdims=True)
            p = jnp.exp(s - top)
            total = jnp.sum(p, axis=0, keepdims=True)
            o = dot_nn(vt_s[h, :, keys], p.astype(BF16)) / total
            outs.append(o)
            lse_ref[h : h + 1, rows] = top + jnp.log(total)
        mixed_t = jnp.concatenate(outs, axis=0).astype(BF16)
        mixed_ref[:, rows] = mixed_t
        attn = dot_nt(mixed_t.T, w_ref[:, heads * 3 * HEAD_DIM :]).astype(BF16)

        @pl.when(at < nq // 2)
        def _():
            send_ref[...] = attn

        @pl.when(at >= nq // 2)
        def _():
            keep_ref[...] = attn

    most = WINDOW // QB + 1
    for nk in range(1, most + 1):
        cond = (blk == nk - 1) if nk < most else (blk >= most - 1)

        @pl.when((step >= nq) & cond)
        def _(nk=nk):
            attend(nk)


def attn_fwd(me, xs, w_cat, lo):
    part, width = xs[0].shape
    seq = part * 4
    heads = w_cat.shape[1] // (4 * HEAD_DIM)
    cols = heads * 3 * HEAD_DIM
    nq = seq // QB
    half = nq // 2
    spec = pltpu.PrefetchScalarGridSpec(
        num_scalar_prefetch=1,
        grid=(2 * nq,),
        in_specs=[whole((part, width))] * 4 + [
            whole(w_cat.shape), whole(lo.shape),
        ],
        out_specs=[
            pl.BlockSpec((QB, cols), lambda i, me: (jnp.minimum(i, nq - 1), 0)),
            whole((heads * HEAD_DIM, seq)),
            whole((8, seq)),
            pl.BlockSpec((QB, width), lambda i, me: (jnp.clip(i - nq, 0, half - 1), 0)),
            pl.BlockSpec((QB, width), lambda i, me: (jnp.clip(i - nq - half, 0, half - 1), 0)),
        ],
        scratch_shapes=[
            pltpu.VMEM((seq, width), BF16),
            pltpu.VMEM((heads, seq, HEAD_DIM), BF16),
            pltpu.VMEM((heads, HEAD_DIM, seq), BF16),
            pltpu.VMEM((heads, seq, HEAD_DIM), BF16),
        ],
    )
    return pl.pallas_call(
        lambda *refs: attn_fwd_kernel(heads, *refs),
        grid_spec=spec,
        out_shape=[
            jax.ShapeDtypeStruct((seq, cols), BF16),
            jax.ShapeDtypeStruct((heads * HEAD_DIM, seq), BF16),
            jax.ShapeDtypeStruct((8, seq), F32),
            jax.ShapeDtypeStruct((seq // 2, width), BF16),
            jax.ShapeDtypeStruct((seq // 2, width), BF16),
        ],
        compiler_params=params("arbitrary"),
        cost_estimate=pl.CostEstimate(flops=12_000_000_000, bytes_accessed=16_000_000, transcendentals=0),
        name="attn_fwd",
    )(me, *xs, w_cat, lo)


def attn_bwd_kernel(heads, me_ref, g0, g1, g2, g3, x0, x1, x2, x3, w_ref, lo_ref, proj_ref,
                    mixed_ref, lse_ref, dw_ref, send_ref, keep_ref, g_s, x_s, k_s, kt_s, v_s, dk_s, dv_s, dq_s,
                    dwo_s):
    me = me_ref[0]
    step = pl.program_id(0)
    part = x0.shape[0]
    seq = x_s.shape[0]
    nq = seq // QB
    per = part // QB
    cols = heads * 3 * HEAD_DIM

    @pl.when(step == 0)
    def _():
        for s, ref in enumerate((g0, g1, g2, g3)):
            g_s[pl.ds(pl.multiple_of((me ^ s) * part, part), part), :] = ref[...]
        for s, ref in enumerate((x0, x1, x2, x3)):
            x_s[pl.ds(pl.multiple_of((me ^ s) * part, part), part), :] = ref[...]
        dk_s[...] = jnp.zeros_like(dk_s)
        dv_s[...] = jnp.zeros_like(dv_s)
        dwo_s[...] = jnp.zeros_like(dwo_s)
        dw_ref[...] = jnp.zeros_like(dw_ref)

    def attend(nk):
        start = pl.multiple_of((step - (nk - 1)) * QB, QB)
        rows = pl.ds(pl.multiple_of(step * QB, QB), QB)
        keys = pl.ds(start, nk * QB)
        g = g_s[rows, :]
        gm_t = dot_nn(g, w_ref[:, cols:]).astype(BF16).T
        mixed_t = mixed_ref[:, rows]
        dwo_s[...] += dot_nn(mixed_t, g)
        prod = gm_t.astype(F32) * mixed_t.astype(F32)
        lo = lo_ref[:, rows]
        kpos = start + lax.broadcasted_iota(I32, (nk * QB, QB), 0)
        qpos = step * QB + lax.broadcasted_iota(I32, (QB, QB), 1)
        proj = proj_ref[...]
        for h in range(heads):
            base = h * 3 * HEAD_DIM
            here = slice(h * HEAD_DIM, (h + 1) * HEAD_DIM)
            q = proj[:, base : base + HEAD_DIM] * 0.125
            k_new = proj[:, base + HEAD_DIM : base + 2 * HEAD_DIM]
            k_s[h, rows, :] = k_new
            kt_s[h, :, rows] = k_new.T
            v_s[h, rows, :] = proj[:, base + 2 * HEAD_DIM : base + 3 * HEAD_DIM]
            drow = jnp.sum(prod[here], axis=0, keepdims=True)
            s = dot_nt(k_s[h, keys, :], q)
            s = jnp.where(kpos >= lo, s, NEG)
            last = jnp.where(kpos[(nk - 1) * QB :] <= qpos, s[(nk - 1) * QB :], NEG)
            s = last if nk == 1 else jnp.concatenate([s[: (nk - 1) * QB], last], axis=0)
            p = jnp.exp(s - lse_ref[h : h + 1, rows])
            dp = dot_nn(v_s[h, keys, :], gm_t[here])
            ds = (p * (dp - drow)).astype(BF16)
            dv_s[h, keys, :] += dot_nt(p.astype(BF16), gm_t[here])
            dk_s[h, keys, :] += dot_nn(ds, q)
            dq = dot_nn(kt_s[h, :, keys], ds) * 0.125
            dq_s[h, rows, :] = dq.astype(BF16).T

    most = WINDOW // QB + 1
    for nk in range(1, most + 1):
        cond = (step == nk - 1) if nk < most else ((step >= most - 1) & (step < nq))

        @pl.when(cond)
        def _(nk=nk):
            attend(nk)

    @pl.when(step >= nq)
    def _():
        at = step - nq
        turn = at // per
        slot = jnp.where(turn == 0, 1, jnp.where(turn == 1, 3, jnp.where(turn == 2, 0, 2)))
        blk = (me ^ slot) * per + at % per
        rows = pl.ds(pl.multiple_of(blk * QB, QB), QB)
        pieces = []
        for h in range(heads):
            pieces += [dq_s[h, rows, :], dk_s[h, rows, :].astype(BF16), dv_s[h, rows, :].astype(BF16)]
        dproj = jnp.concatenate(pieces, axis=1)
        dw_ref[:, :cols] += dot_tn(x_s[rows, :], dproj)
        gn = dot_nt(dproj, w_ref[:, :cols]).astype(BF16)

        @pl.when(at < nq // 2)
        def _():
            send_ref[...] = gn

        @pl.when(at >= nq // 2)
        def _():
            keep_ref[...] = gn

        @pl.when(at == nq - 1)
        def _():
            dw_ref[:, cols:] = dwo_s[...].T


def attn_bwd(me, gs, xs, w_cat, lo, proj, mixed_t, lse):
    part, width = xs[0].shape
    seq = part * 4
    heads = w_cat.shape[1] // (4 * HEAD_DIM)
    cols = heads * 3 * HEAD_DIM
    hc = heads * HEAD_DIM
    nq = seq // QB
    half = nq // 2
    spec = pltpu.PrefetchScalarGridSpec(
        num_scalar_prefetch=1,
        grid=(2 * nq,),
        in_specs=[whole((part, width))] * 8 + [
            whole(w_cat.shape), whole(lo.shape),
            pl.BlockSpec((QB, cols), lambda i, me: (jnp.minimum(i, nq - 1), 0)),
            whole((hc, seq)),
            whole((8, seq)),
        ],
        out_specs=[
            whole((width, cols + hc)),
            pl.BlockSpec((QB, width), lambda i, me: (jnp.clip(i - nq, 0, half - 1), 0)),
            pl.BlockSpec((QB, width), lambda i, me: (jnp.clip(i - nq - half, 0, half - 1), 0)),
        ],
        scratch_shapes=[
            pltpu.VMEM((seq, width), BF16),
            pltpu.VMEM((seq, width), BF16),
            pltpu.VMEM((heads, seq, HEAD_DIM), BF16),
            pltpu.VMEM((heads, HEAD_DIM, seq), BF16),
            pltpu.VMEM((heads, seq, HEAD_DIM), BF16),
            pltpu.VMEM((heads, seq, HEAD_DIM), F32),
            pltpu.VMEM((heads, seq, HEAD_DIM), F32),
            pltpu.VMEM((heads, seq, HEAD_DIM), BF16),
            pltpu.VMEM((hc, width), F32),
        ],
    )
    return pl.pallas_call(
        lambda *refs: attn_bwd_kernel(heads, *refs),
        grid_spec=spec,
        out_shape=[
            jax.ShapeDtypeStruct((width, cols + hc), F32),
            jax.ShapeDtypeStruct((seq // 2, width), BF16),
            jax.ShapeDtypeStruct((seq // 2, width), BF16),
        ],
        compiler_params=params("arbitrary"),
        cost_estimate=pl.CostEstimate(flops=40_000_000_000, bytes_accessed=20_000_000, transcendentals=0),
        name="attn_bwd",
    )(me, *gs, *xs, w_cat, lo, proj, mixed_t, lse)


def run_copies(n, src, src_at, dst, dst_at, sems, act):
    for i, size in enumerate(SIZES):
        done = n // (2 * size) * (2 * size)

        @pl.when((n // size) % 2 == 1)
        def _(i=i, size=size, done=done):
            copy = pltpu.make_async_copy(
                src.at[pl.ds(pl.multiple_of(src_at + done, ROW_TILE), size), :],
                dst.at[pl.ds(pl.multiple_of(dst_at + done, ROW_TILE), size), :],
                sems.at[i],
            )
            if act == "start":
                copy.start()
            else:
                copy.wait()


def dispatch_kernel(experts, n_ref, lo_ref, off_ref, x0, x1, x2, x3, c0, c1, c2, c3, rt_ref, pos_ref, *refs):
    xs_ref, gs_ref, meta_ref, x_s, c_s, xl, gl, in_sems, sems = refs[-9:]
    step = pl.program_id(0)
    slot = step % 2
    rows = xl.shape[1]
    part = x_s.shape[1]

    def load(s):
        for t, (x, c) in enumerate(((x0, c0), (x1, c1), (x2, c2), (x3, c3))):
            @pl.when(s == t)
            def _(x=x, c=c, t=t):
                pltpu.make_async_copy(x, x_s.at[t % 2], in_sems.at[t % 2, 0]).start()
                pltpu.make_async_copy(c, c_s.at[t % 2], in_sems.at[t % 2, 1]).start()

    def moves(at, slot, act):
        for e in range(experts):
            n, src, dst = n_ref[at, e], lo_ref[at, e], off_ref[at, e]
            run_copies(n, xl.at[slot], src, xs_ref.at[e], dst, sems.at[slot, 0, e], act)
            run_copies(n, gl.at[slot], src, gs_ref.at[e], dst, sems.at[slot, 1, e], act)

    @pl.when(step == 0)
    def _():
        load(0)

    @pl.when(step < 3)
    def _():
        load(step + 1)

    @pl.when(step >= 2)
    def _():
        moves(step - 2, slot, "wait")

    pltpu.make_async_copy(x0, x_s.at[slot], in_sems.at[slot, 0]).wait()
    pltpu.make_async_copy(c0, c_s.at[slot], in_sems.at[slot, 1]).wait()
    x = x_s[slot]
    logits = dot_nt(rt_ref[...], x)
    spots = pos_ref[0]
    p0, p1, r0, r1 = spots[0:1], spots[1:2], spots[2:3], spots[3:4]
    names = lax.broadcasted_iota(I32, logits.shape, 0)
    first = jnp.sum(jnp.where(names == r0, logits, 0.0), axis=0, keepdims=True)
    second = jnp.sum(jnp.where(names == r1, logits, 0.0), axis=0, keepdims=True)
    g0 = 1.0 / (1.0 + jnp.exp(second - first))
    g1 = 1.0 / (1.0 + jnp.exp(first - second))
    pick = lax.broadcasted_iota(I32, (8, part), 0)
    meta_ref[0] = jnp.where(
        pick == 0, p0.astype(F32), jnp.where(pick == 1, p1.astype(F32), jnp.where(pick == 2, g0, g1))
    )
    spot = lax.broadcasted_iota(I32, (rows, part), 0)
    is0 = spot == p0
    is1 = spot == p1
    plain = jnp.where(is0 | is1, 1.0, 0.0).astype(BF16)
    gated = jnp.where(is0, g0, jnp.where(is1, g1, 0.0)).astype(BF16)
    xl[slot] = dot_nn(plain, x).astype(BF16)
    gl[slot] = dot_nn(gated, c_s[slot]).astype(BF16)
    moves(step, slot, "start")

    @pl.when(step == 3)
    def _():
        moves(step - 1, 1 - slot, "wait")
        moves(step, slot, "wait")


def local_rows(part, experts):
    return -(-(2 * part + experts * (ROW_TILE - 1)) // 128) * 128


def dispatch(tables, xs, cs, router_t, spots, held, experts, most):
    part, width = xs[0].shape
    rows = local_rows(part, experts)
    anywhere = pl.BlockSpec(memory_space=pl.ANY)
    spec = pltpu.PrefetchScalarGridSpec(
        num_scalar_prefetch=3,
        grid=(4,),
        in_specs=[anywhere] * 8 + [
            whole(router_t.shape),
            pl.BlockSpec((1, 8, part), lambda i, *_: (i, 0, 0)),
        ] + [anywhere] * len(held),
        out_specs=[anywhere, anywhere, pl.BlockSpec((1, 8, part), lambda i, *_: (i, 0, 0))],
        scratch_shapes=[
            pltpu.VMEM((2, part, width), BF16),
            pltpu.VMEM((2, part, width), BF16),
            pltpu.VMEM((2, rows, width), BF16),
            pltpu.VMEM((2, rows, width), BF16),
            pltpu.SemaphoreType.DMA((2, 2)),
            pltpu.SemaphoreType.DMA((2, 2, experts, len(SIZES))),
        ],
    )
    return pl.pallas_call(
        lambda *refs: dispatch_kernel(experts, *refs),
        grid_spec=spec,
        out_shape=[
            jax.ShapeDtypeStruct((experts, most, width), BF16),
            jax.ShapeDtypeStruct((experts, most, width), BF16),
            jax.ShapeDtypeStruct((4, 8, part), F32),
        ],
        input_output_aliases={13: 0, 14: 1} if held else {},
        compiler_params=params("arbitrary"),
        cost_estimate=pl.CostEstimate(flops=10_000_000_000, bytes_accessed=20_000_000, transcendentals=0),
        name="dispatch",
    )(*tables, *xs, *cs, router_t, spots, *held)


def expert_kernel(first, tot_ref, xs_ref, gs_ref, w_ref, od_ref, dw_ref, din_s, dout_s):
    e = pl.program_id(0)
    c = pl.program_id(1)
    tot = tot_ref[first + e]
    width = xs_ref.shape[2]

    @pl.when(c == 0)
    def _():
        din_s[...] = jnp.zeros_like(din_s)
        dout_s[...] = jnp.zeros_like(dout_s)

    @pl.when(c * CHUNK < tot)
    def _():
        live = c * CHUNK + lax.broadcasted_iota(I32, (CHUNK, width), 0) < tot
        x = jnp.where(live, xs_ref[0], jnp.zeros((), BF16))
        g = jnp.where(live, gs_ref[0], jnp.zeros((), BF16))
        w_in = w_ref[0, 0]
        w_out_t = w_ref[0, 1]
        pre = dot_nn(x, w_in)
        dact = dot_nn(g, w_out_t)
        square = pre * pre
        t = jnp.tanh(GELU_A * pre * (1.0 + GELU_B * square))
        half = 0.5 * (1.0 + t)
        act = pre * half
        slope = half + (0.5 * GELU_A) * pre * (1.0 - t * t) * (1.0 + (3.0 * GELU_B) * square)
        act_low = act.astype(BF16)
        dpre = (slope * dact).astype(BF16)
        od_ref[0, :, :width] = dot_nt(act_low, w_out_t).astype(BF16)
        od_ref[0, :, width : 2 * width] = dot_nt(dpre, w_in).astype(BF16)
        dot_row = jnp.sum(act * dact, axis=1, keepdims=True)
        lane = lax.broadcasted_iota(I32, (CHUNK, 128), 1)
        od_ref[0, :, 2 * width :] = jnp.where(lane == first + e, dot_row, 0.0).astype(BF16)
        din_s[...] += dot_tn(x, dpre)
        dout_s[...] += dot_tn(g, act_low)

    @pl.when(c == pl.num_programs(1) - 1)
    def _():
        dw_ref[0, 0] = din_s[...].astype(BF16)
        dw_ref[0, 1] = dout_s[...].astype(BF16)


def run_experts(first, totals, xs, gs, weights):
    group, _, width, hidden = weights.shape
    most = xs.shape[1]
    chunks = most // CHUNK

    def rows_at(base):
        def index(e, c, tot):
            last = jnp.maximum((tot[first + e] + CHUNK - 1) // CHUNK - 1, 0)
            return (base + e, jnp.minimum(c, last), 0)

        return index

    spec = pltpu.PrefetchScalarGridSpec(
        num_scalar_prefetch=1,
        grid=(group, chunks),
        in_specs=[
            pl.BlockSpec((1, CHUNK, width), rows_at(first)),
            pl.BlockSpec((1, CHUNK, width), rows_at(first)),
            pl.BlockSpec((1, 2, width, hidden), lambda e, c, tot: (e, 0, 0, 0)),
        ],
        out_specs=[
            pl.BlockSpec((1, CHUNK, 2 * width + 128), rows_at(0)),
            pl.BlockSpec((1, 2, width, hidden), lambda e, c, tot: (e, 0, 0, 0)),
        ],
        scratch_shapes=[pltpu.VMEM((width, hidden), F32), pltpu.VMEM((width, hidden), F32)],
    )
    return pl.pallas_call(
        lambda *refs: expert_kernel(first, *refs),
        grid_spec=spec,
        out_shape=[
            jax.ShapeDtypeStruct((group, most, 2 * width + 128), BF16),
            jax.ShapeDtypeStruct((group, 2, width, hidden), BF16),
        ],
        compiler_params=params("arbitrary", "arbitrary"),
        cost_estimate=pl.CostEstimate(
            flops=group * 12 * 1024 * width * hidden, bytes_accessed=group * 20_000_000, transcendentals=0
        ),
        name="experts",
    )(totals, xs, gs, weights)


def combine_kernel(experts, groups, n_ref, lo_ref, off_ref, *refs):
    od_refs = refs[:groups]
    meta_ref, send_ref, keep_ref, od_l, sems = refs[groups:]
    step = pl.program_id(0)
    slot = step % 2
    rows = od_l.shape[1]
    each = experts // groups
    part = meta_ref.shape[2]
    width = (od_l.shape[2] - 128) // 2

    def moves(at, slot, act):
        for e in range(experts):
            n, dst, src = n_ref[at, e], lo_ref[at, e], off_ref[at, e]
            run_copies(n, od_refs[e // each].at[e % each], src, od_l.at[slot], dst, sems.at[slot, e], act)

    @pl.when(step == 0)
    def _():
        od_l[...] = jnp.zeros_like(od_l)
        moves(0, 0, "start")

    @pl.when(step < 3)
    def _():
        moves(step + 1, 1 - slot, "start")

    moves(step, slot, "wait")
    meta = meta_ref[0].T
    p0, p1, g0, g1 = (meta[:, i : i + 1] for i in range(4))
    spot = lax.broadcasted_iota(I32, (part, rows), 1).astype(F32)
    is0 = spot == p0
    is1 = spot == p1
    plain = jnp.where(is0 | is1, 1.0, 0.0).astype(BF16)
    gated = jnp.where(is0, g0, jnp.where(is1, g1, 0.0)).astype(BF16)
    out = dot_nn(gated, od_l[slot, :, :width]).astype(BF16)
    back = dot_nn(plain, od_l[slot, :, width:]).astype(BF16)

    @pl.when(step < 2)
    def _():
        send_ref[:, :width] = out
        send_ref[:, width:] = back

    @pl.when(step >= 2)
    def _():
        keep_ref[:, :width] = out
        keep_ref[:, width:] = back


def combine(tables, ods, meta):
    experts = sum(od.shape[0] for od in ods)
    groups = len(ods)
    wide = ods[0].shape[2]
    part = meta.shape[2]
    rows = local_rows(part, experts)
    anywhere = pl.BlockSpec(memory_space=pl.ANY)
    spec = pltpu.PrefetchScalarGridSpec(
        num_scalar_prefetch=3,
        grid=(4,),
        in_specs=[anywhere] * groups + [pl.BlockSpec((1, 8, part), lambda i, *_: (i, 0, 0))],
        out_specs=[
            pl.BlockSpec((part, wide), lambda i, *_: (jnp.minimum(i, 1), 0)),
            pl.BlockSpec((part, wide), lambda i, *_: (jnp.maximum(i - 2, 0), 0)),
        ],
        scratch_shapes=[
            pltpu.VMEM((2, rows, wide), BF16),
            pltpu.SemaphoreType.DMA((2, experts, len(SIZES))),
        ],
    )
    return pl.pallas_call(
        lambda *refs: combine_kernel(experts, groups, *refs),
        grid_spec=spec,
        out_shape=[jax.ShapeDtypeStruct((2 * part, wide), BF16)] * 2,
        compiler_params=params("arbitrary"),
        cost_estimate=pl.CostEstimate(flops=10_000_000_000, bytes_accessed=20_000_000, transcendentals=0),
        name="combine",
    )(*tables, *ods, meta)


def routing(routes, capacity, me, part):
    micro = routes.shape[0]
    experts = capacity.shape[0]
    picks = routes.reshape(micro, 4, part, 2).transpose(0, 1, 3, 2)
    names = jnp.arange(experts, dtype=I32)[:, None]
    named = picks[:, :, :, None, :] == names
    either = named[:, :, 0] | named[:, :, 1]
    earlier = jnp.arange(part)[:, None] < jnp.arange(part)[None, :]
    before = jnp.einsum("mbet,ts->mbes", either.astype(BF16), earlier.astype(BF16), preferred_element_type=F32)
    before = before.astype(I32)
    count = jnp.sum(either.astype(I32), axis=3)
    carry = jnp.cumsum(count, axis=1) - count
    kept = jnp.clip(capacity[None, None, :] - carry, 0, count)
    n = (kept + ROW_TILE - 1) // ROW_TILE * ROW_TILE
    lo = jnp.cumsum(n, axis=2) - n
    place = jnp.where(before < kept[..., None], lo[..., None] + before, -1)
    pos = jnp.max(jnp.where(named, place[:, :, None], -1), axis=3)
    order = me ^ jnp.array([1, 3, 0, 2], I32)
    spots = jnp.concatenate([pos, picks, jnp.zeros_like(pos), jnp.zeros_like(pos)], axis=2)
    spots = jnp.take(spots, order, axis=1)
    n = jnp.take(n, order, axis=1)
    lo = jnp.take(lo, order, axis=1)
    flat = n.reshape(micro * 4, experts)
    off = (jnp.cumsum(flat, axis=0) - flat).reshape(n.shape)
    return n, lo, off, jnp.sum(flat, axis=0), spots


def norm_scaled(values, gain):
    return values * lax.rsqrt(jnp.mean(values * values, axis=-1, keepdims=True) + EPS) * gain


def spread(rows):
    over = lax.ppermute(rows, "tp", [(i, i ^ 2) for i in range(4)])
    side = lax.ppermute(rows, "tp", [(i, i ^ 1) for i in range(4)])
    far = lax.ppermute(over, "tp", [(i, i ^ 1) for i in range(4)])
    return (side, far, rows, over)


def gather_sum(send, keep):
    part = keep.shape[0] // 2
    got = lax.ppermute(send, "tp", [(i, i ^ 1) for i in range(4)])
    both = keep.astype(F32) + got.astype(F32)
    away = lax.ppermute(both[part:].astype(BF16), "tp", [(i, i ^ 2) for i in range(4)])
    return both[:part] + away.astype(F32)


def local(tokens, cotangent, gain_attn, gain_moe, qkv_weight, out_weight, router, w_in, w_out, doc_lengths, routes,
          capacity):
    micro, part, width = tokens.shape
    seq = part * 4
    experts = w_in.shape[0]
    me = lax.axis_index("tp").astype(I32)
    me_arr = me.reshape(1)
    most = -(-micro * (CAP + 4 * ROW_TILE) // CHUNK) * CHUNK
    groups = 4
    each = experts // groups

    cat = jnp.concatenate([qkv_weight, out_weight.T], axis=1)
    w_cat = lax.all_gather(cat, "fsdp", axis=0, tiled=True)
    w_pair = jnp.stack([w_in, w_out.transpose(0, 2, 1)], axis=1)
    w_groups = [
        lax.all_gather(w_pair[g * each : (g + 1) * each], "fsdp", axis=2, tiled=True) for g in range(groups)
    ]

    n, lo_at, off, totals, spots = routing(routes, capacity, me, part)
    places = jnp.arange(seq, dtype=I32)
    ends = jnp.cumsum(doc_lengths.reshape(micro, -1), axis=1)
    begins = ends - doc_lengths.reshape(micro, -1)
    doc_start = jnp.max(jnp.where(places >= begins[:, :, None], begins[:, :, None], 0), axis=1)
    low = jnp.maximum(doc_start, places - (WINDOW - 1)).astype(I32)
    router_t = router.T
    router_float = router.astype(F32)

    x_float = [tokens[m].astype(F32) for m in range(micro)]
    normed_parts, cot_parts = [], []
    back_attn = []
    for m in range(micro):
        normed, back = jax.vjp(norm_scaled, x_float[m], gain_attn)
        back_attn.append(back)
        normed_parts.append(spread(normed.astype(BF16)))
    cot_parts = [spread(cotangent[m]) for m in range(micro)]

    fwd = []
    moe_rows, back_moe, hidden = [], [], []
    held = ()
    metas = []
    for m in range(micro):
        side, far, own, over = normed_parts[m]
        proj, mixed_t, lse, send, keep = attn_fwd(me_arr, (own, side, over, far), w_cat, low[m : m + 1])
        fwd.append((proj, mixed_t, lse))
        hid = x_float[m] + gather_sum(send, keep)
        hidden.append(hid)
        normed, back = jax.vjp(norm_scaled, hid, gain_moe)
        back_moe.append(back)
        moe_rows.append(normed.astype(BF16))
        xs, gs, meta = dispatch(
            (n[m], lo_at[m], off[m]), spread(moe_rows[m]), cot_parts[m], router_t, spots[m], held, experts, most
        )
        held = (xs, gs)
        metas.append(meta)

    ods, dws = [], []
    for g in range(groups):
        od, dw = run_experts(g * each, totals, xs, gs, w_groups[g])
        ods.append(od)
        dws.append(lax.psum_scatter(dw, "fsdp", scatter_dimension=2, tiled=True))

    outputs, grads_in = [], []
    grad_router = jnp.zeros(router.shape, F32)
    grad_gain_two = jnp.zeros(gain_moe.shape, F32)
    grad_gain_one = jnp.zeros(gain_attn.shape, F32)
    grad_cat = jnp.zeros((width, w_cat.shape[1]), F32)
    names = jnp.arange(experts, dtype=I32)
    for m in range(micro):
        send, keep = combine((n[m], lo_at[m], off[m]), ods, metas[m])
        summed = gather_sum(send, keep)
        outputs.append((hidden[m] + summed[:, :width]).astype(BF16))
        products = summed[:, 2 * width : 2 * width + experts]
        mine = lax.dynamic_slice_in_dim(routes[m], me * part, part, 0)
        gates = metas[m][2, 2:4].T
        full = jnp.sum(jnp.where(mine[:, :, None] == names, gates[:, :, None], 0.0), axis=1)
        grad_logits = products - full * jnp.sum(products, axis=1, keepdims=True)
        grad_router += jnp.einsum(
            "td,te->de", moe_rows[m].astype(F32), grad_logits, precision=lax.Precision.HIGHEST,
            preferred_element_type=F32,
        )
        grad_moe = summed[:, width : 2 * width] + jnp.einsum(
            "te,de->td", grad_logits, router_float, precision=lax.Precision.HIGHEST, preferred_element_type=F32
        )
        grad_norm, grad_gain = back_moe[m](grad_moe)
        grad_gain_two += grad_gain
        grad_hidden = cotangent[m].astype(F32) + grad_norm
        g_side, g_far, g_own, g_over = spread(grad_hidden.astype(BF16))
        side, far, own, over = normed_parts[m]
        proj, mixed_t, lse = fwd[m]
        dcat, send, keep = attn_bwd(
            me_arr, (g_own, g_side, g_over, g_far), (own, side, over, far), w_cat, low[m : m + 1], proj, mixed_t, lse
        )
        grad_cat += dcat
        grad_x, grad_gain = back_attn[m](gather_sum(send, keep))
        grad_gain_one += grad_gain
        grads_in.append((grad_hidden + grad_x).astype(BF16))

    grad_cat = lax.psum_scatter(grad_cat.astype(BF16), "fsdp", scatter_dimension=0, tiled=True).astype(F32)
    dw = jnp.concatenate(dws, axis=0).astype(F32)
    grad_router, grad_gain_one, grad_gain_two = lax.psum((grad_router, grad_gain_one, grad_gain_two), ("fsdp", "tp"))
    cols = qkv_weight.shape[1]
    return (
        jnp.stack(outputs),
        jnp.stack(grads_in),
        grad_gain_one,
        grad_gain_two,
        grad_cat[:, :cols],
        grad_cat[:, cols:].T,
        grad_router,
        dw[:, 0],
        dw[:, 1].transpose(0, 2, 1),
    )


def solution(mesh):
    rows = P(None, ("fsdp", "tp"), None)
    in_specs = (
        rows,
        rows,
        P(),
        P(),
        P("fsdp", "tp"),
        P("tp", "fsdp"),
        P(),
        P(None, "fsdp", "tp"),
        P(None, "tp", "fsdp"),
        P(None, "fsdp", None),
        P(None, "fsdp", None),
        P(),
    )
    out_specs = (
        rows,
        rows,
        P(),
        P(),
        P("fsdp", "tp"),
        P("tp", "fsdp"),
        P(),
        P(None, "fsdp", "tp"),
        P(None, "tp", "fsdp"),
    )
    return jax.shard_map(local, mesh=mesh, in_specs=in_specs, out_specs=out_specs, check_vma=False)
```

```python
import math

import jax
import jax.numpy as jnp
from jax import lax
from jax.experimental import pallas as pl
from jax.experimental.pallas import tpu as pltpu
from jax.sharding import PartitionSpec as P

HEAD_DIM = 64
WINDOW = 1024
CAP = 768
ROW_TILE = 16
QB = 256
CHUNK = 256
EPS = 1e-06
NEG = -1e30
F32 = jnp.float32
BF16 = jnp.bfloat16
I32 = jnp.int32
VMEM_LIMIT = 56 * 1024 * 1024
GELU_A = math.sqrt(2.0 / math.pi)
GELU_B = 0.044715
SIZES = (512, 256, 128, 64, 32, 16)


def dot_nn(a, b):
    return lax.dot_general(a, b, (((1,), (0,)), ((), ())), preferred_element_type=F32)


def dot_nt(a, b):
    return lax.dot_general(a, b, (((1,), (1,)), ((), ())), preferred_element_type=F32)


def dot_tn(a, b):
    return lax.dot_general(a, b, (((0,), (0,)), ((), ())), preferred_element_type=F32)


def params(*semantics):
    return pltpu.CompilerParams(dimension_semantics=semantics, vmem_limit_bytes=VMEM_LIMIT)


def whole(shape):
    zeros = (0,) * len(shape)
    return pl.BlockSpec(shape, lambda *_: zeros)


def next_on_cycle(i):
    y, z = i % 2, i // 2
    return jnp.where(y == 0, jnp.where(z < 3, i + 2, i + 1), jnp.where(z > 0, i - 2, i - 1))


def before_on_cycle(i):
    y, z = i % 2, i // 2
    return jnp.where(y == 0, jnp.where(z > 0, i - 2, i + 1), jnp.where(z < 3, i + 2, i - 1))


def remote(src, dst, sems, k, peer):
    send, recv = sems
    return pltpu.make_async_remote_copy(
        src_ref=src, dst_ref=dst, send_sem=send.at[k], recv_sem=recv.at[k], device_id=peer,
        device_id_type=pl.DeviceIdType.MESH,
    )


def greet(peers):
    barrier = pltpu.get_barrier_semaphore()
    for peer in peers:
        pl.semaphore_signal(barrier, inc=1, device_id=peer, device_id_type=pl.DeviceIdType.MESH)
    pl.semaphore_wait(barrier, len(peers))


def attend_rows(blk, lo_ref, q_s, k_s, vt_s, mixed_ref, lse_ref, finish):
    heads = q_s.shape[0]
    most = WINDOW // QB + 1

    def window(nk):
        start = pl.multiple_of((blk - (nk - 1)) * QB, QB)
        rows = pl.ds(pl.multiple_of(blk * QB, QB), QB)
        keys = pl.ds(start, nk * QB)
        lo = lo_ref[:, rows]
        kpos = start + lax.broadcasted_iota(I32, (nk * QB, QB), 0)
        qpos = blk * QB + lax.broadcasted_iota(I32, (QB, QB), 1)
        outs = []
        for h in range(heads):
            s = dot_nt(k_s[h, keys, :], q_s[h, rows, :])
            s = jnp.where(kpos >= lo, s, NEG)
            last = jnp.where(kpos[(nk - 1) * QB :] <= qpos, s[(nk - 1) * QB :], NEG)
            s = last if nk == 1 else jnp.concatenate([s[: (nk - 1) * QB], last], axis=0)
            top = jnp.max(s, axis=0, keepdims=True)
            p = jnp.exp(s - top)
            total = jnp.sum(p, axis=0, keepdims=True)
            outs.append(dot_nn(vt_s[h, :, keys], p.astype(BF16)) / total)
            lse_ref[h : h + 1, rows] = top + jnp.log(total)
        mixed_t = jnp.concatenate(outs, axis=0).astype(BF16)
        mixed_ref[:, rows] = mixed_t
        finish(mixed_t)

    for nk in range(1, most + 1):
        cond = (blk == nk - 1) if nk < most else (blk >= most - 1)

        @pl.when(cond)
        def _(nk=nk):
            window(nk)


SLOT_ORDER = (3, 2, 1, 0)
STEPS = 9
NAMES = (
    "n_over", "n_side", "n_far", "c_over", "c_side", "c_far", "m_over", "m_side", "m_far", "a_far", "a_own", "b_over"
)


def forward_kernel(heads, ring, tok_ref, cot_ref, gain1_ref, gain2_ref, cat_ref, lo_ref, xn_out, moe_out, cot_out,
                   mixed_ref, lse_ref, hid_ref, wcat_out, xn_s, q_s, k_s, vt_s, part_s, side_s, over_s, moe_s, wcat_ref, send_sem,
                   recv_sem, local_sem):
    micro, part, width = tok_ref.shape
    seq = part * 4
    cols = heads * 3 * HEAD_DIM
    per = part // QB
    nq = seq // QB
    step = pl.program_id(0)
    m = step // STEPS
    t = step % STEPS
    me = lax.axis_index("tp").astype(I32)
    side = {"tp": me ^ 1}
    over = {"tp": me ^ 2}
    sems = (send_sem, recv_sem)
    mine = pl.ds(pl.multiple_of(me * part, part), part)
    theirs = pl.ds(pl.multiple_of((me ^ 2) * part, part), part)

    def copy(name, k):
        table = {
            "n_over": (0, xn_s.at[k, mine], xn_s.at[k, mine], over),
            "n_side": (1, xn_s.at[k, mine], xn_s.at[k, mine], side),
            "n_far": (2, xn_s.at[k, theirs], xn_s.at[k, theirs], side),
            "c_over": (3, cot_ref.at[k], cot_out.at[k, 3], over),
            "c_side": (4, cot_ref.at[k], cot_out.at[k, 0], side),
            "c_far": (5, cot_out.at[k, 3], cot_out.at[k, 1], side),
            "m_over": (6, moe_s.at[k], moe_out.at[k, 3], over),
            "m_side": (7, moe_s.at[k], moe_out.at[k, 0], side),
            "m_far": (8, moe_out.at[k, 3], moe_out.at[k, 1], side),
            "a_far": (9, part_s.at[k, 3], side_s.at[k, 0], side),
            "a_own": (10, part_s.at[k, 1], side_s.at[k, 1], side),
            "b_over": (11, part_s.at[k, 2], over_s.at[k], over),
        }
        at, source, target, peer = table[name]
        return remote(source, target, sems, 12 * k + at, peer)

    def keep(at, k):
        source, target = ((cot_ref.at[k], cot_out.at[k, 2]), (moe_s.at[k], moe_out.at[k, 2]), (xn_s.at[k], xn_out.at[k]))[at]
        return pltpu.make_async_copy(source, target, local_sem.at[3 * k + at])

    if ring:
        here = lax.axis_index("fsdp").astype(I32)
        ahead, behind = next_on_cycle(here), before_on_cycle(here)
        rows = cat_ref.shape[0]

        def hop(k, source, peer):
            at = pl.ds(pl.multiple_of(source * rows, rows), rows)
            return remote(wcat_ref.at[at], wcat_ref.at[at], sems, 24 + k, peer)

    tiles = part // 128

    @pl.when(step == 0)
    def _():
        peers = [side, over]
        if ring:
            peers += [{"fsdp": ahead}, {"fsdp": behind}]
        greet(peers)
        if ring:
            wcat_ref[pl.ds(pl.multiple_of(here * rows, rows), rows), :] = cat_ref[...]
            hop(0, here, {"fsdp": ahead}).start()
            hop(1, here, {"fsdp": behind}).start()
        else:
            wcat_ref[...] = cat_ref[...]
        for k in range(micro):
            def body(i, _, k=k):
                at = pl.ds(pl.multiple_of(i * 128, 128), 128)
                x = tok_ref[k, at, :].astype(F32)
                r = lax.rsqrt(jnp.mean(x * x, axis=1, keepdims=True) + EPS)
                xn_s[k, pl.ds(pl.multiple_of(me * part + i * 128, 128), 128), :] = (x * r * gain1_ref[...]).astype(BF16)
                return 0

            lax.fori_loop(0, tiles, body, 0)
            if k == 0:
                c = 0
                copy("n_over", c).start()
                copy("n_side", c).start()
        if ring:
            one, two = here, here
            for k in range(1, 4):
                one, two = before_on_cycle(one), next_on_cycle(two)
                hop(2 * k - 2, one, {"fsdp": ahead}).wait_recv()
                hop(2 * k, one, {"fsdp": ahead}).start()
                hop(2 * k - 1, two, {"fsdp": behind}).wait_recv()
                if k < 3:
                    hop(2 * k + 1, two, {"fsdp": behind}).start()
            hop(6, before_on_cycle(one), {"fsdp": ahead}).wait_recv()
        c = 0
        copy("n_over", c).wait_recv()
        copy("n_far", c).start()
        copy("n_side", c).wait_recv()
        copy("n_far", c).wait_recv()
        c = 1
        copy("n_over", c).start()
        copy("n_side", c).start()

    @pl.when(step == STEPS)
    def _():
        c = 1
        copy("n_side", c).wait_recv()
        copy("n_far", c).wait_recv()

    @pl.when((t == 0) & (m < micro))
    def _():
        def body(i, _):
            at = pl.ds(pl.multiple_of(i * QB, QB), QB)
            proj = dot_nn(xn_s[m, at, :], wcat_ref[:, :cols]).astype(BF16)
            for h in range(heads):
                base = h * 3 * HEAD_DIM
                q_s[h, at, :] = proj[:, base : base + HEAD_DIM] * 0.125
                k_s[h, at, :] = proj[:, base + HEAD_DIM : base + 2 * HEAD_DIM]
                vt_s[h, :, at] = proj[:, base + 2 * HEAD_DIM : base + 3 * HEAD_DIM].T
            return 0

        lax.fori_loop(0, nq, body, 0)

    @pl.when((t > 0) & (m < micro))
    def _():
        at = t - 1
        slot = 3 - at // per
        blk = (me ^ slot) * per + at % per

        def finish(mixed_t):
            rows = pl.ds(pl.multiple_of(at % per * QB, QB), QB)
            part_s[m, slot, rows, :] = dot_nt(mixed_t.T, wcat_ref[:, cols:]).astype(BF16)

        attend_rows(blk, lo_ref.at[m], q_s, k_s, vt_s, mixed_ref.at[m], lse_ref.at[m], finish)

    for k in range(micro):
        first = k * STEPS
        c = k

        @pl.when(step == first + per)
        def _(c=c):
            copy("a_far", c).start()

        @pl.when(step == first + 2 * per)
        def _(c=c, k=k):
            copy("a_far", c).wait_recv()
            part_s[k, 2] = (part_s[k, 2].astype(F32) + side_s[k, 0].astype(F32)).astype(BF16)
            copy("b_over", c).start()
            if k == 0:
                d = 1
                copy("n_over", d).wait_recv()
                copy("n_far", d).start()
                keep(0, c).start()
                copy("c_side", c).start()
                copy("c_over", c).start()
            else:
                d = 0
                copy("m_over", d).wait_recv()
                copy("m_far", d).start()
                keep(0, c).start()
                copy("c_side", c).start()
                copy("c_over", c).start()

        @pl.when(step == first + 3 * per)
        def _(c=c, k=k):
            copy("a_own", c).start()
            if k == 1:
                d = 0
                copy("c_over", d).wait_recv()
                copy("c_far", d).start()

        @pl.when(step == first + 4 * per)
        def _(c=c, k=k):
            copy("a_own", c).wait_recv()
            copy("b_over", c).wait_recv()

            def body(i, _):
                at = pl.ds(pl.multiple_of(i * 128, 128), 128)
                hid = (
                    tok_ref[k, at, :].astype(F32) + part_s[k, 0, at, :].astype(F32)
                    + side_s[k, 1, at, :].astype(F32) + over_s[k, at, :].astype(F32)
                )
                hid_ref[k, at, :] = hid
                r = lax.rsqrt(jnp.mean(hid * hid, axis=1, keepdims=True) + EPS)
                moe_s[k, at, :] = (hid * r * gain2_ref[...]).astype(BF16)
                return 0

            lax.fori_loop(0, tiles, body, 0)
            copy("m_over", c).start()
            copy("m_side", c).start()
            keep(1, c).start()
            keep(2, c).start()

    def keep_w():
        return pltpu.make_async_copy(wcat_ref, wcat_out, local_sem.at[6])

    @pl.when(step == STEPS)
    def _():
        keep_w().start()

    @pl.when(step == 2 * STEPS)
    def _():
        c, d = 0, 1
        keep_w().wait()
        copy("m_over", d).wait_recv()
        copy("m_far", d).start()
        copy("c_over", d).wait_recv()
        copy("c_far", d).start()
        for e in (c, d):
            copy("c_side", e).wait_recv()
            copy("c_far", e).wait_recv()
            copy("m_side", e).wait_recv()
            copy("m_far", e).wait_recv()
            for name in NAMES:
                copy(name, e).wait_send()
            for at in range(3):
                keep(at, e).wait()
        if ring:
            one, two = here, here
            for k in range(4):
                hop(2 * k, one, {"fsdp": ahead}).wait_send()
                if k < 3:
                    hop(2 * k + 1, two, {"fsdp": behind}).wait_send()
                one, two = before_on_cycle(one), next_on_cycle(two)


def forward_half(tokens, cotangent, gain1, gain2, cat, low, ring):
    micro, part, width = tokens.shape
    seq = part * 4
    wide = cat.shape[1]
    heads = wide // (4 * HEAD_DIM)
    hc = heads * HEAD_DIM
    anywhere = pl.BlockSpec(memory_space=pl.ANY)
    return pl.pallas_call(
        lambda *refs: forward_kernel(heads, ring, *refs),
        grid=(2 * STEPS + 1,),
        in_specs=[whole(tokens.shape), anywhere, whole((1, width)), whole((1, width)), whole(cat.shape), whole(low.shape)],
        out_specs=[anywhere, anywhere, anywhere, whole((micro, hc, seq)), whole((micro, 8, seq)),
                   whole((micro, part, width)), anywhere],
        out_shape=[
            jax.ShapeDtypeStruct((micro, seq, width), BF16),
            jax.ShapeDtypeStruct((micro, 4, part, width), BF16),
            jax.ShapeDtypeStruct((micro, 4, part, width), BF16),
            jax.ShapeDtypeStruct((micro, hc, seq), BF16),
            jax.ShapeDtypeStruct((micro, 8, seq), F32),
            jax.ShapeDtypeStruct((micro, part, width), F32),
            jax.ShapeDtypeStruct((width, wide), BF16),
        ],
        scratch_shapes=[
            pltpu.VMEM((micro, seq, width), BF16),
            pltpu.VMEM((heads, seq, HEAD_DIM), BF16),
            pltpu.VMEM((heads, seq, HEAD_DIM), BF16),
            pltpu.VMEM((heads, HEAD_DIM, seq), BF16),
            pltpu.VMEM((micro, 4, part, width), BF16),
            pltpu.VMEM((micro, 2, part, width), BF16),
            pltpu.VMEM((micro, part, width), BF16),
            pltpu.VMEM((micro, part, width), BF16),
            pltpu.VMEM((width, wide), BF16),
            pltpu.SemaphoreType.DMA((31,)),
            pltpu.SemaphoreType.DMA((31,)),
            pltpu.SemaphoreType.DMA((7,)),
        ],
        compiler_params=pltpu.CompilerParams(
            dimension_semantics=("arbitrary",), vmem_limit_bytes=VMEM_LIMIT, collective_id=1, has_side_effects=True
        ),
        cost_estimate=pl.CostEstimate(flops=100_000_000_000, bytes_accessed=100_000_000, transcendentals=0),
        name="forward_half",
    )(tokens, cotangent, gain1, gain2, cat, low)


def attn_bwd_kernel(heads, held, me_ref, g0, g1, g2, g3, x_ref, w_ref, lo_ref, mixed_ref,
                    lse_ref, *refs):
    before = refs[:2] if held else ()
    (dw_ref, gain_ref, send_ref, keep_ref, g_s, k_s, kt_s, v_s, dk_s, dv_s, dq_s, dwo_s) = refs[-12:]
    x_s, mixed_ref, lse_ref, lo_ref = x_ref.at[0], mixed_ref.at[0], lse_ref.at[0], lo_ref.at[0]
    me = me_ref[0]
    step = pl.program_id(0)
    part = g0.shape[0]
    seq = x_s.shape[0]
    nq = seq // QB
    per = part // QB
    cols = heads * 3 * HEAD_DIM

    @pl.when(step == 0)
    def _():
        for s, ref in enumerate((g0, g1, g2, g3)):
            g_s[pl.ds(pl.multiple_of((me ^ s) * part, part), part), :] = ref[...]
        dk_s[...] = jnp.zeros_like(dk_s)
        dv_s[...] = jnp.zeros_like(dv_s)
        dwo_s[...] = jnp.zeros_like(dwo_s)
        if before:
            dw_ref[...] = before[0][...]
            gain_ref[...] = before[1][...]
        else:
            dw_ref[...] = jnp.zeros_like(dw_ref)
            gain_ref[...] = jnp.zeros_like(gain_ref)

    def attend(nk):
        start = pl.multiple_of((step - (nk - 1)) * QB, QB)
        rows = pl.ds(pl.multiple_of(step * QB, QB), QB)
        keys = pl.ds(start, nk * QB)
        g = g_s[rows, :]
        gm_t = dot_nn(g, w_ref[:, cols:]).astype(BF16).T
        mixed_t = mixed_ref[:, rows]
        dwo_s[...] += dot_nn(mixed_t, g)
        prod = gm_t.astype(F32) * mixed_t.astype(F32)
        lo = lo_ref[:, rows]
        kpos = start + lax.broadcasted_iota(I32, (nk * QB, QB), 0)
        qpos = step * QB + lax.broadcasted_iota(I32, (QB, QB), 1)
        proj = dot_nn(x_s[rows, :], w_ref[:, :cols]).astype(BF16)
        for h in range(heads):
            base = h * 3 * HEAD_DIM
            here = slice(h * HEAD_DIM, (h + 1) * HEAD_DIM)
            q = proj[:, base : base + HEAD_DIM] * 0.125
            k_new = proj[:, base + HEAD_DIM : base + 2 * HEAD_DIM]
            k_s[h, rows, :] = k_new
            kt_s[h, :, rows] = k_new.T
            v_s[h, rows, :] = proj[:, base + 2 * HEAD_DIM : base + 3 * HEAD_DIM]
            drow = jnp.sum(prod[here], axis=0, keepdims=True)
            s = dot_nt(k_s[h, keys, :], q)
            s = jnp.where(kpos >= lo, s, NEG)
            last = jnp.where(kpos[(nk - 1) * QB :] <= qpos, s[(nk - 1) * QB :], NEG)
            s = last if nk == 1 else jnp.concatenate([s[: (nk - 1) * QB], last], axis=0)
            p = jnp.exp(s - lse_ref[h : h + 1, rows])
            dp = dot_nn(v_s[h, keys, :], gm_t[here])
            ds = (p * (dp - drow)).astype(BF16)
            dv_s[h, keys, :] += dot_nt(p.astype(BF16), gm_t[here])
            dk_s[h, keys, :] += dot_nn(ds, q)
            dq = dot_nn(kt_s[h, :, keys], ds) * 0.125
            dq_s[h, rows, :] = dq.astype(BF16).T

    most = WINDOW // QB + 1
    for nk in range(1, most + 1):
        cond = (step == nk - 1) if nk < most else ((step >= most - 1) & (step < nq))

        @pl.when(cond)
        def _(nk=nk):
            attend(nk)

    @pl.when(step >= nq)
    def _():
        at = step - nq
        turn = at // per
        slot = jnp.where(turn == 0, 1, jnp.where(turn == 1, 3, jnp.where(turn == 2, 0, 2)))
        blk = (me ^ slot) * per + at % per
        rows = pl.ds(pl.multiple_of(blk * QB, QB), QB)
        pieces = []
        for h in range(heads):
            pieces += [dq_s[h, rows, :], dk_s[h, rows, :].astype(BF16), dv_s[h, rows, :].astype(BF16)]
        dproj = jnp.concatenate(pieces, axis=1)
        dw_ref[:, :cols] += dot_tn(x_s[rows, :], dproj)
        gn = dot_nt(dproj, w_ref[:, :cols])
        gain_ref[...] += jnp.sum((gn * x_s[rows, :].astype(F32)).reshape(QB // 8, 8, gn.shape[1]), axis=0)
        gn = gn.astype(BF16)

        @pl.when(at < nq // 2)
        def _():
            send_ref[...] = gn

        @pl.when(at >= nq // 2)
        def _():
            keep_ref[...] = gn

        @pl.when(at == nq - 1)
        def _():
            dw_ref[:, cols:] += dwo_s[...].T


def attn_bwd(m, me, gs, xn, w_cat, lo, mixed_t, lse, before, deps=()):
    part, width = gs[0].shape
    seq = part * 4
    heads = w_cat.shape[1] // (4 * HEAD_DIM)
    cols = heads * 3 * HEAD_DIM
    hc = heads * HEAD_DIM
    nq = seq // QB
    half = nq // 2
    spec = pltpu.PrefetchScalarGridSpec(
        num_scalar_prefetch=1,
        grid=(2 * nq,),
        in_specs=[whole((part, width))] * 4 + [
            pl.BlockSpec((1, seq, width), lambda i, me: (m, 0, 0)),
            whole(w_cat.shape),
            pl.BlockSpec((1, 1, seq), lambda i, me: (m, 0, 0)),
            pl.BlockSpec((1, hc, seq), lambda i, me: (m, 0, 0)),
            pl.BlockSpec((1, 8, seq), lambda i, me: (m, 0, 0)),
        ] + ([whole((width, cols + hc)), whole((8, width))] if before else [])
        + [pl.BlockSpec(memory_space=pl.ANY)] * len(deps),
        out_specs=[
            whole((width, cols + hc)),
            whole((8, width)),
            pl.BlockSpec((QB, width), lambda i, me: (jnp.clip(i - nq, 0, half - 1), 0)),
            pl.BlockSpec((QB, width), lambda i, me: (jnp.clip(i - nq - half, 0, half - 1), 0)),
        ],
        scratch_shapes=[
            pltpu.VMEM((seq, width), BF16),
            pltpu.VMEM((heads, seq, HEAD_DIM), BF16),
            pltpu.VMEM((heads, HEAD_DIM, seq), BF16),
            pltpu.VMEM((heads, seq, HEAD_DIM), BF16),
            pltpu.VMEM((heads, seq, HEAD_DIM), F32),
            pltpu.VMEM((heads, seq, HEAD_DIM), F32),
            pltpu.VMEM((heads, seq, HEAD_DIM), BF16),
            pltpu.VMEM((hc, width), F32),
        ],
    )
    return pl.pallas_call(
        lambda *refs: attn_bwd_kernel(heads, bool(before), *refs),
        grid_spec=spec,
        out_shape=[
            jax.ShapeDtypeStruct((width, cols + hc), F32),
            jax.ShapeDtypeStruct((8, width), F32),
            jax.ShapeDtypeStruct((seq // 2, width), BF16),
            jax.ShapeDtypeStruct((seq // 2, width), BF16),
        ],
        compiler_params=params("arbitrary"),
        cost_estimate=pl.CostEstimate(flops=40_000_000_000, bytes_accessed=20_000_000, transcendentals=0),
        name="attn_bwd",
    )(me, *gs, xn, w_cat, lo, mixed_t, lse, *before, *deps)


def run_copies(n, src, src_at, dst, dst_at, sems, act):
    for i, size in enumerate(SIZES):
        done = n // (2 * size) * (2 * size)

        @pl.when((n // size) % 2 == 1)
        def _(i=i, size=size, done=done):
            copy = pltpu.make_async_copy(
                src.at[pl.ds(pl.multiple_of(src_at + done, ROW_TILE), size), :],
                dst.at[pl.ds(pl.multiple_of(dst_at + done, ROW_TILE), size), :],
                sems.at[i],
            )
            if act == "start":
                copy.start()
            else:
                copy.wait()


def dispatch_kernel(m, experts, n_ref, lo_ref, off_ref, x_all, c_all, rt_ref, pos_ref, *refs):
    xs_ref, gs_ref, meta_ref, x_s, c_s, xl, gl, in_sems, sems = refs[-9:]
    step = pl.program_id(0)
    slot = step % 2
    rows = xl.shape[1]
    part = x_s.shape[1]

    def loads(s):
        at = s % 2
        return (
            pltpu.make_async_copy(x_all.at[m, s], x_s.at[at], in_sems.at[at, 0]),
            pltpu.make_async_copy(c_all.at[m, s], c_s.at[at], in_sems.at[at, 1]),
        )

    def moves(at, slot, act):
        for e in range(experts):
            n, src, dst = n_ref[at, e], lo_ref[at, e], off_ref[at, e]
            run_copies(n, xl.at[slot], src, xs_ref.at[e], dst, sems.at[slot, 0, e], act)
            run_copies(n, gl.at[slot], src, gs_ref.at[e], dst, sems.at[slot, 1, e], act)

    @pl.when(step == 0)
    def _():
        for copy in loads(0):
            copy.start()

    @pl.when(step < 3)
    def _():
        for copy in loads(step + 1):
            copy.start()

    @pl.when(step >= 2)
    def _():
        moves(step - 2, slot, "wait")

    for copy in loads(step):
        copy.wait()
    x = x_s[slot]
    logits = dot_nt(rt_ref[...], x)
    spots = pos_ref[0]
    p0, p1, r0, r1 = spots[0:1], spots[1:2], spots[2:3], spots[3:4]
    names = lax.broadcasted_iota(I32, logits.shape, 0)
    first = jnp.sum(jnp.where(names == r0, logits, 0.0), axis=0, keepdims=True)
    second = jnp.sum(jnp.where(names == r1, logits, 0.0), axis=0, keepdims=True)
    g0 = 1.0 / (1.0 + jnp.exp(second - first))
    g1 = 1.0 / (1.0 + jnp.exp(first - second))
    pick = lax.broadcasted_iota(I32, (8, part), 0)
    meta_ref[0] = jnp.where(
        pick == 0, p0.astype(F32), jnp.where(pick == 1, p1.astype(F32), jnp.where(pick == 2, g0, g1))
    )
    spot = lax.broadcasted_iota(I32, (rows, part), 0)
    is0 = spot == p0
    is1 = spot == p1
    plain = jnp.where(is0 | is1, 1.0, 0.0).astype(BF16)
    gated = jnp.where(is0, g0, jnp.where(is1, g1, 0.0)).astype(BF16)
    xl[slot] = dot_nn(plain, x).astype(BF16)
    gl[slot] = dot_nn(gated, c_s[slot]).astype(BF16)
    moves(step, slot, "start")

    @pl.when(step == 3)
    def _():
        moves(step - 1, 1 - slot, "wait")
        moves(step, slot, "wait")


def local_rows(part, experts):
    return -(-(2 * part + experts * (ROW_TILE - 1)) // 128) * 128


def dispatch(m, tables, xs, cs, router_t, spots, held, experts, most):
    part, width = xs.shape[2:]
    rows = local_rows(part, experts)
    anywhere = pl.BlockSpec(memory_space=pl.ANY)
    spec = pltpu.PrefetchScalarGridSpec(
        num_scalar_prefetch=3,
        grid=(4,),
        in_specs=[anywhere] * 2 + [
            whole(router_t.shape),
            pl.BlockSpec((1, 8, part), lambda i, *_: (i, 0, 0)),
        ] + [anywhere] * len(held),
        out_specs=[anywhere, anywhere, pl.BlockSpec((1, 8, part), lambda i, *_: (i, 0, 0))],
        scratch_shapes=[
            pltpu.VMEM((2, part, width), BF16),
            pltpu.VMEM((2, part, width), BF16),
            pltpu.VMEM((2, rows, width), BF16),
            pltpu.VMEM((2, rows, width), BF16),
            pltpu.SemaphoreType.DMA((2, 2)),
            pltpu.SemaphoreType.DMA((2, 2, experts, len(SIZES))),
        ],
    )
    return pl.pallas_call(
        lambda *refs: dispatch_kernel(m, experts, *refs),
        grid_spec=spec,
        out_shape=[
            jax.ShapeDtypeStruct((experts, most, width), BF16),
            jax.ShapeDtypeStruct((experts, most, width), BF16),
            jax.ShapeDtypeStruct((4, 8, part), F32),
        ],
        input_output_aliases={7: 0, 8: 1} if held else {},
        compiler_params=params("arbitrary"),
        cost_estimate=pl.CostEstimate(flops=10_000_000_000, bytes_accessed=20_000_000, transcendentals=0),
        name="dispatch",
    )(*tables, xs, cs, router_t, spots, *held)


def expert_kernel(first, shards, deps, split, tot_ref, src_ref, out_ref, xs_ref, gs_ref, *refs):
    w_refs = refs[:shards]
    refs = refs[shards + deps :]
    od_ref, dw_refs = refs[0], refs[1 : 3 if split else 2]
    w_s, din_s, dout_s = refs[-3:]
    e = pl.program_id(0)
    c = pl.program_id(1)
    tot = tot_ref[first + e]
    width = xs_ref.shape[2]

    @pl.when(c == 0)
    def _():
        din_s[...] = jnp.zeros_like(din_s)
        dout_s[...] = jnp.zeros_like(dout_s)
        for s, ref in enumerate(w_refs):
            rows = ref.shape[2]
            at = pl.ds(pl.multiple_of(src_ref[s] * rows, rows), rows)
            w_s[0, at, :] = ref[0, 0]
            w_s[1, at, :] = ref[0, 1]

    @pl.when(c * CHUNK < tot)
    def _():
        live = c * CHUNK + lax.broadcasted_iota(I32, (CHUNK, width), 0) < tot
        x = jnp.where(live, xs_ref[0], jnp.zeros((), BF16))
        g = jnp.where(live, gs_ref[0], jnp.zeros((), BF16))
        w_in = w_s[0]
        w_out_t = w_s[1]
        pre = dot_nn(x, w_in)
        dact = dot_nn(g, w_out_t)
        square = pre * pre
        t = jnp.tanh(GELU_A * pre * (1.0 + GELU_B * square))
        half = 0.5 * (1.0 + t)
        act = pre * half
        slope = half + (0.5 * GELU_A) * pre * (1.0 - t * t) * (1.0 + (3.0 * GELU_B) * square)
        act_low = act.astype(BF16)
        dpre = (slope * dact).astype(BF16)
        od_ref[0, :, :width] = dot_nt(act_low, w_out_t).astype(BF16)
        od_ref[0, :, width : 2 * width] = dot_nt(dpre, w_in).astype(BF16)
        dot_row = jnp.sum(act * dact, axis=1, keepdims=True)
        lane = lax.broadcasted_iota(I32, (CHUNK, 128), 1)
        od_ref[0, :, 2 * width :] = jnp.where(lane == first + e, dot_row, 0.0).astype(BF16)
        din_s[...] += dot_tn(x, dpre)
        dout_s[...] += dot_tn(g, act_low)

    @pl.when(c == pl.num_programs(1) - 1)
    def _():
        if not split:
            dw_refs[0][0, 0] = din_s[...].astype(BF16)
            dw_refs[0][0, 1] = dout_s[...].astype(BF16)
        else:
            count, rows = dw_refs[0].shape[2:4]
            for which, ref in enumerate(dw_refs):
                for k in range(count):
                    at = pl.ds(pl.multiple_of(out_ref[which * count + k] * rows, rows), rows)
                    ref[0, 0, k] = din_s[at, :].astype(BF16)
                    ref[0, 1, k] = dout_s[at, :].astype(BF16)


def run_experts(first, group, totals, xs, gs, w_shards, src, out_order, split, deps=()):
    arrays = [array for array, _ in w_shards]
    shards = len(arrays)
    rows, hidden = arrays[0].shape[2:]
    width = xs.shape[2]
    most = xs.shape[1]
    chunks = most // CHUNK

    def rows_at(base):
        def index(e, c, tot, *_):
            last = jnp.maximum((tot[first + e] + CHUNK - 1) // CHUNK - 1, 0)
            return (base + e, jnp.minimum(c, last), 0)

        return index

    def shard_at(base):
        return lambda e, c, *_: (first - base + e, 0, 0, 0)

    if split:
        half = (group, 2, out_order.shape[0] // 2, width // out_order.shape[0], hidden)
        dw_shapes = [half, half]
        dw_specs = [pl.BlockSpec((1,) + half[1:], lambda e, c, *_: (e, 0, 0, 0, 0))] * 2
    else:
        dw_shapes = [(group, 2, width, hidden)]
        dw_specs = [pl.BlockSpec((1, 2, width, hidden), lambda e, c, *_: (e, 0, 0, 0))]
    spec = pltpu.PrefetchScalarGridSpec(
        num_scalar_prefetch=3,
        grid=(group, chunks),
        in_specs=[
            pl.BlockSpec((1, CHUNK, width), rows_at(first)),
            pl.BlockSpec((1, CHUNK, width), rows_at(first)),
        ] + [pl.BlockSpec((1, 2, rows, hidden), shard_at(base)) for _, base in w_shards]
        + [pl.BlockSpec(memory_space=pl.ANY)] * len(deps),
        out_specs=[pl.BlockSpec((1, CHUNK, 2 * width + 128), rows_at(0))] + dw_specs,
        scratch_shapes=[
            pltpu.VMEM((2, width, hidden), BF16),
            pltpu.VMEM((width, hidden), F32),
            pltpu.VMEM((width, hidden), F32),
        ],
    )
    return pl.pallas_call(
        lambda *refs: expert_kernel(first, shards, len(deps), split, *refs),
        grid_spec=spec,
        out_shape=[jax.ShapeDtypeStruct((group, most, 2 * width + 128), BF16)]
        + [jax.ShapeDtypeStruct(shape, BF16) for shape in dw_shapes],
        compiler_params=params("arbitrary", "arbitrary"),
        cost_estimate=pl.CostEstimate(
            flops=group * 24 * 1024 * width * hidden, bytes_accessed=group * 20_000_000, transcendentals=0
        ),
        name="experts",
    )(totals, src, out_order, xs, gs, *arrays, *deps)


def combine_kernel(experts, groups, n_ref, lo_ref, off_ref, *refs):
    od_refs = refs[:groups]
    meta_ref = refs[groups]
    osend_ref, okeep_ref, bsend_ref, bkeep_ref, od_l, sems = refs[-6:]
    step = pl.program_id(0)
    slot = step % 2
    rows = od_l.shape[1]
    each = experts // groups
    part = meta_ref.shape[2]
    width = (od_l.shape[2] - 128) // 2

    def moves(at, slot, act):
        for e in range(experts):
            n, dst, src = n_ref[at, e], lo_ref[at, e], off_ref[at, e]
            run_copies(n, od_refs[e // each].at[e % each], src, od_l.at[slot], dst, sems.at[slot, e], act)

    @pl.when(step == 0)
    def _():
        od_l[...] = jnp.zeros_like(od_l)
        moves(0, 0, "start")

    @pl.when(step < 3)
    def _():
        moves(step + 1, 1 - slot, "start")

    moves(step, slot, "wait")
    meta = meta_ref[0].T
    p0, p1, g0, g1 = (meta[:, i : i + 1] for i in range(4))
    spot = lax.broadcasted_iota(I32, (part, rows), 1).astype(F32)
    is0 = spot == p0
    is1 = spot == p1
    plain = jnp.where(is0 | is1, 1.0, 0.0).astype(BF16)
    gated = jnp.where(is0, g0, jnp.where(is1, g1, 0.0)).astype(BF16)
    out = dot_nn(gated, od_l[slot, :, :width]).astype(BF16)
    back = dot_nn(plain, od_l[slot, :, width:]).astype(BF16)

    @pl.when(step < 2)
    def _():
        osend_ref[...] = out
        bsend_ref[...] = back

    @pl.when(step >= 2)
    def _():
        okeep_ref[...] = out
        bkeep_ref[...] = back


def combine(tables, ods, meta, deps=()):
    experts = sum(od.shape[0] for od in ods)
    groups = len(ods)
    wide = ods[0].shape[2]
    width = (wide - 128) // 2
    part = meta.shape[2]
    rows = local_rows(part, experts)
    anywhere = pl.BlockSpec(memory_space=pl.ANY)
    spec = pltpu.PrefetchScalarGridSpec(
        num_scalar_prefetch=3,
        grid=(4,),
        in_specs=[anywhere] * groups + [pl.BlockSpec((1, 8, part), lambda i, *_: (i, 0, 0))]
        + [anywhere] * len(deps),
        out_specs=[
            pl.BlockSpec((part, cols), index)
            for cols in (width, wide - width)
            for index in (lambda i, *_: (jnp.minimum(i, 1), 0), lambda i, *_: (jnp.maximum(i - 2, 0), 0))
        ],
        scratch_shapes=[
            pltpu.VMEM((2, rows, wide), BF16),
            pltpu.SemaphoreType.DMA((2, experts, len(SIZES))),
        ],
    )
    return pl.pallas_call(
        lambda *refs: combine_kernel(experts, groups, *refs),
        grid_spec=spec,
        out_shape=[jax.ShapeDtypeStruct((2 * part, cols), BF16) for cols in (width, width, wide - width, wide - width)],
        compiler_params=params("arbitrary"),
        cost_estimate=pl.CostEstimate(flops=10_000_000_000, bytes_accessed=20_000_000, transcendentals=0),
        name="combine",
    )(*tables, *ods, meta, *deps)


def routing(routes, capacity, me, part):
    micro = routes.shape[0]
    experts = capacity.shape[0]
    picks = routes.reshape(micro, 4, part, 2).transpose(0, 1, 3, 2)
    names = jnp.arange(experts, dtype=I32)[:, None]
    named = picks[:, :, :, None, :] == names
    either = named[:, :, 0] | named[:, :, 1]
    earlier = jnp.arange(part)[:, None] < jnp.arange(part)[None, :]
    before = jnp.einsum("mbet,ts->mbes", either.astype(BF16), earlier.astype(BF16), preferred_element_type=F32)
    before = before.astype(I32)
    count = jnp.sum(either.astype(I32), axis=3)
    carry = jnp.cumsum(count, axis=1) - count
    kept = jnp.clip(capacity[None, None, :] - carry, 0, count)
    n = (kept + ROW_TILE - 1) // ROW_TILE * ROW_TILE
    lo = jnp.cumsum(n, axis=2) - n
    place = jnp.where(before < kept[..., None], lo[..., None] + before, -1)
    pos = jnp.max(jnp.where(named, place[:, :, None], -1), axis=3)
    order = me ^ jnp.array([1, 3, 0, 2], I32)
    spots = jnp.concatenate([pos, picks, jnp.zeros_like(pos), jnp.zeros_like(pos)], axis=2)
    spots = jnp.take(spots, order, axis=1)
    n = jnp.take(n, order, axis=1)
    lo = jnp.take(lo, order, axis=1)
    flat = n.reshape(micro * 4, experts)
    off = (jnp.cumsum(flat, axis=0) - flat).reshape(n.shape)
    return n, lo, off, jnp.sum(flat, axis=0), spots


def norm_scaled(values, gain):
    return values * lax.rsqrt(jnp.mean(values * values, axis=-1, keepdims=True) + EPS) * gain


def spread(rows):
    over = lax.ppermute(rows, "tp", [(i, i ^ 2) for i in range(4)])
    side = lax.ppermute(rows, "tp", [(i, i ^ 1) for i in range(4)])
    far = lax.ppermute(over, "tp", [(i, i ^ 1) for i in range(4)])
    return (side, far, rows, over)


def pair_sum(send, keep):
    got = lax.ppermute(send, "tp", [(i, i ^ 1) for i in range(4)])
    return keep.astype(F32) + got.astype(F32)


def chip_sum(both):
    part = both.shape[0] // 2
    away = lax.ppermute(both[part:].astype(BF16), "tp", [(i, i ^ 2) for i in range(4)])
    return both[:part] + away.astype(F32)


def line_sum(send, keep):
    return line_finish(line_start(send, keep))


def line_start(send, keep):
    got = lax.ppermute(send, "fsdp", [(i, i ^ 1) for i in range(8)])
    return keep.astype(F32) + got.astype(F32)


def line_finish(both):
    total = both[..., 0, :, :]
    for k in range(1, 4):
        piece = both[..., k, :, :].astype(BF16)
        total += lax.ppermute(piece, "fsdp", [(i, i ^ (2 * k)) for i in range(8)]).astype(F32)
    return total


def sum_everywhere(values, axis, count):
    step = 1
    while step < count:
        values += lax.ppermute(values, axis, [(i, i ^ step) for i in range(count)])
        step *= 2
    return values


def local(tokens, cotangent, gain_attn, gain_moe, qkv_weight, out_weight, router, w_in, w_out, doc_lengths, routes,
          capacity):
    micro, part, width = tokens.shape
    seq = part * 4
    experts = w_in.shape[0]
    n_fsdp = lax.axis_size("fsdp")
    ring = n_fsdp == 8
    me = lax.axis_index("tp").astype(I32)
    me_arr = me.reshape(1)
    most = -(-micro * (CAP + 4 * ROW_TILE) // CHUNK) * CHUNK
    groups = 4
    each = experts // groups

    cat = jnp.concatenate([qkv_weight, out_weight.T], axis=1)
    w_pair = jnp.stack([w_in, w_out.transpose(0, 2, 1)], axis=1)
    if ring:
        row_index = lax.axis_index("fsdp").astype(I32)
        near = 2 * ((row_index // 2) ^ jnp.arange(4, dtype=I32))
        out_order = jnp.concatenate([near + row_index % 2, near + (1 - row_index % 2)])
    else:
        cat = lax.all_gather(cat, "fsdp", axis=0, tiled=True)
        out_order = jnp.zeros((1,), I32)
    w_groups = [
        lax.all_gather(w_pair[g * each : (g + 1) * each], "fsdp", axis=2, tiled=True) for g in range(groups)
    ]

    n, lo_at, off, totals, spots = routing(routes, capacity, me, part)
    places = jnp.arange(seq, dtype=I32)
    ends = jnp.cumsum(doc_lengths.reshape(micro, -1), axis=1)
    begins = ends - doc_lengths.reshape(micro, -1)
    doc_start = jnp.max(jnp.where(places >= begins[:, :, None], begins[:, :, None], 0), axis=1)
    low = jnp.maximum(doc_start, places - (WINDOW - 1)).astype(I32)
    router_t = router.T
    router_float = router.astype(F32)

    low = low[:, None, :]
    xn, moe, cot, mixed_t, lse, hidden, w_cat = forward_half(
        tokens, cotangent, gain_attn[None], gain_moe[None], cat, low, ring
    )
    metas, held = [], ()
    for m in range(micro):
        xs, gs, meta = dispatch(
            m, (n[m], lo_at[m], off[m]), moe, cot, router_t, spots[m], held, experts, most
        )
        held = (xs, gs)
        metas.append(meta)
    back_attn = [jax.vjp(norm_scaled, tokens[m].astype(F32), gain_attn)[1] for m in range(micro)]
    back_moe = [jax.vjp(norm_scaled, hidden[m], gain_moe)[1] for m in range(micro)]
    moe_rows = [moe[m, 2] for m in range(micro)]

    ods, dws, halves, deps = [], [], [], ()
    for g in range(groups):
        first = g * each
        split = ring and g < groups // 2
        od, *dw = run_experts(
            first, each, totals, xs, gs, [(w_groups[g], first)], jnp.zeros((1,), I32), out_order, split, deps
        )
        deps = (od,)
        ods.append(od)
        if split:
            halves.append(line_start(dw[1], dw[0]))
        else:
            dws.append(lax.psum_scatter(dw[0], "fsdp", scatter_dimension=2, tiled=True).astype(F32))

    outputs, grads_in = [], []
    grad_router = jnp.zeros(router.shape, F32)
    grad_gain_two = jnp.zeros(gain_moe.shape, F32)
    names = jnp.arange(experts, dtype=I32)
    before, deps = (), ()
    ready = [tuple(halves[m : m + 1]) for m in range(micro)]
    for m in range(micro):
        out_send, out_keep, send, keep = combine((n[m], lo_at[m], off[m]), ods, metas[m], deps + ready[m])
        both = pair_sum(send, keep)
        deps = (both,)
        summed = chip_sum(both)
        out_both = pair_sum(out_send, out_keep)
        outputs.append((hidden[m] + chip_sum(out_both)).astype(BF16))
        products = summed[:, width : width + experts]
        mine = lax.dynamic_slice_in_dim(routes[m], me * part, part, 0)
        gates = metas[m][2, 2:4].T
        full = jnp.sum(jnp.where(mine[:, :, None] == names, gates[:, :, None], 0.0), axis=1)
        grad_logits = products - full * jnp.sum(products, axis=1, keepdims=True)
        grad_router += jnp.einsum(
            "td,te->de", moe_rows[m].astype(F32), grad_logits, precision=lax.Precision.HIGHEST,
            preferred_element_type=F32,
        )
        grad_moe = summed[:, :width] + jnp.einsum(
            "te,de->td", grad_logits, router_float, precision=lax.Precision.HIGHEST, preferred_element_type=F32
        )
        grad_norm, grad_gain = back_moe[m](grad_moe)
        grad_gain_two += grad_gain
        grad_hidden = cotangent[m].astype(F32) + grad_norm
        g_side, g_far, g_own, g_over = spread(grad_hidden.astype(BF16))
        done = [line_finish(half) for half in halves[m : m + 1]]
        dws[m:m] = done
        done += [outputs[0]] if m == 1 else []
        dcat, gain_rows, send, keep = attn_bwd(
            m, me_arr, (g_own, g_side, g_over, g_far), xn, w_cat, low, mixed_t, lse, before, tuple(done)
        )
        before = (dcat, gain_rows)
        grad_x, _ = back_attn[m](chip_sum(pair_sum(send, keep)))
        grads_in.append((grad_hidden + grad_x).astype(BF16))

    cols = qkv_weight.shape[1]
    if ring:
        blocks = dcat.reshape(n_fsdp, width // n_fsdp, -1).astype(BF16)
        grad_cat = line_sum(jnp.take(blocks, out_order[4:], axis=0), jnp.take(blocks, out_order[:4], axis=0))
    else:
        grad_cat = lax.psum_scatter(dcat.astype(BF16), "fsdp", scatter_dimension=0, tiled=True).astype(F32)
    grad_gain_one = jnp.sum(gain_rows, axis=0) / gain_attn
    small = jnp.concatenate([grad_router.T, grad_gain_one[None], grad_gain_two[None]], axis=0)
    small = sum_everywhere(sum_everywhere(small, "tp", 4), "fsdp", n_fsdp)
    dw = jnp.concatenate(dws, axis=0)
    return (
        jnp.stack(outputs),
        jnp.stack(grads_in),
        small[experts],
        small[experts + 1],
        grad_cat[:, :cols],
        grad_cat[:, cols:].T,
        small[:experts].T,
        dw[:, 0],
        dw[:, 1].transpose(0, 2, 1),
    )


def solution(mesh):
    rows = P(None, ("fsdp", "tp"), None)
    in_specs = (
        rows,
        rows,
        P(),
        P(),
        P("fsdp", "tp"),
        P("tp", "fsdp"),
        P(),
        P(None, "fsdp", "tp"),
        P(None, "tp", "fsdp"),
        P(None, "fsdp", None),
        P(None, "fsdp", None),
        P(),
    )
    out_specs = (
        rows,
        rows,
        P(),
        P(),
        P("fsdp", "tp"),
        P("tp", "fsdp"),
        P(),
        P(None, "fsdp", "tp"),
        P(None, "tp", "fsdp"),
    )
    return jax.shard_map(local, mesh=mesh, in_specs=in_specs, out_specs=out_specs, check_vma=False)
```

```python
import math

import jax
import jax.numpy as jnp
from jax import lax
from jax.experimental import pallas as pl
from jax.experimental.pallas import tpu as pltpu
from jax.sharding import PartitionSpec as P

HEAD_DIM = 64
WINDOW = 1024
CAP = 768
ROW_TILE = 16
QB = 256
CHUNK = 256
EPS = 1e-06
NEG = -1e30
F32 = jnp.float32
BF16 = jnp.bfloat16
I32 = jnp.int32
VMEM_LIMIT = 56 * 1024 * 1024
GELU_A = math.sqrt(2.0 / math.pi)
GELU_B = 0.044715
NEAR = 2


def dot_nn(a, b):
    return lax.dot_general(a, b, (((1,), (0,)), ((), ())), preferred_element_type=F32)


def dot_nt(a, b):
    return lax.dot_general(a, b, (((1,), (1,)), ((), ())), preferred_element_type=F32)


def dot_tn(a, b):
    return lax.dot_general(a, b, (((0,), (0,)), ((), ())), preferred_element_type=F32)


def params(*semantics):
    return pltpu.CompilerParams(dimension_semantics=semantics, vmem_limit_bytes=VMEM_LIMIT)


def whole(shape):
    zeros = (0,) * len(shape)
    return pl.BlockSpec(shape, lambda *_: zeros)


def next_on_cycle(i):
    y, z = i % 2, i // 2
    return jnp.where(y == 0, jnp.where(z < 3, i + 2, i + 1), jnp.where(z > 0, i - 2, i - 1))


def before_on_cycle(i):
    y, z = i % 2, i // 2
    return jnp.where(y == 0, jnp.where(z > 0, i - 2, i + 1), jnp.where(z < 3, i + 2, i - 1))


def remote(src, dst, sems, k, peer):
    send, recv = sems
    return pltpu.make_async_remote_copy(
        src_ref=src, dst_ref=dst, send_sem=send.at[k], recv_sem=recv.at[k], device_id=peer,
        device_id_type=pl.DeviceIdType.MESH,
    )


def greet(peers):
    barrier = pltpu.get_barrier_semaphore()
    for peer in peers:
        pl.semaphore_signal(barrier, inc=1, device_id=peer, device_id_type=pl.DeviceIdType.MESH)
    pl.semaphore_wait(barrier, len(peers))


def attend_rows(blk, lo_ref, q_s, k_s, vt_s, mixed_ref, lse_ref, finish):
    heads = q_s.shape[0]
    most = WINDOW // QB + 1

    def window(nk):
        start = pl.multiple_of((blk - (nk - 1)) * QB, QB)
        rows = pl.ds(pl.multiple_of(blk * QB, QB), QB)
        keys = pl.ds(start, nk * QB)
        lo = lo_ref[:, rows]
        kpos = start + lax.broadcasted_iota(I32, (nk * QB, QB), 0)
        qpos = blk * QB + lax.broadcasted_iota(I32, (QB, QB), 1)
        outs = []
        for h in range(heads):
            s = dot_nt(k_s[h, keys, :], q_s[h, rows, :])
            s = jnp.where(kpos >= lo, s, NEG)
            last = jnp.where(kpos[(nk - 1) * QB :] <= qpos, s[(nk - 1) * QB :], NEG)
            s = last if nk == 1 else jnp.concatenate([s[: (nk - 1) * QB], last], axis=0)
            top = jnp.max(s, axis=0, keepdims=True)
            p = jnp.exp(s - top)
            total = jnp.sum(p, axis=0, keepdims=True)
            outs.append(dot_nn(vt_s[h, :, keys], p.astype(BF16)) / total)
            lse_ref[h : h + 1, rows] = top + jnp.log(total)
        mixed_t = jnp.concatenate(outs, axis=0).astype(BF16)
        mixed_ref[:, rows] = mixed_t
        finish(mixed_t)

    for nk in range(1, most + 1):
        cond = (blk == nk - 1) if nk < most else (blk >= most - 1)

        @pl.when(cond)
        def _(nk=nk):
            window(nk)


SLOT_ORDER = (3, 2, 1, 0)
STEPS = 9
NAMES = (
    "n_over", "n_side", "n_far", "m_over", "m_side", "m_far", "a_far", "a_own", "b_over"
)


def forward_kernel(heads, ring, tok_ref, cot_ref, gain1_ref, gain2_ref, cat_ref, lo_ref, far_ref, near_ref, xn_out, moe_out, cot_out,
                   mixed_ref, lse_ref, hid_ref, wcat_out, far_out, near_out, xn_s, q_s, k_s, vt_s, part_s, side_s, over_s, moe_s, wcat_ref, send_sem,
                   recv_sem, local_sem):
    micro, part, width = tok_ref.shape
    seq = part * 4
    cols = heads * 3 * HEAD_DIM
    per = part // QB
    nq = seq // QB
    step = pl.program_id(0)
    m = step // STEPS
    t = step % STEPS
    me = lax.axis_index("tp").astype(I32)
    side = {"tp": me ^ 1}
    over = {"tp": me ^ 2}
    sems = (send_sem, recv_sem)
    mine = pl.ds(pl.multiple_of(me * part, part), part)
    theirs = pl.ds(pl.multiple_of((me ^ 2) * part, part), part)

    def copy(name, k):
        table = {
            "n_over": (0, xn_s.at[k, mine], xn_s.at[k, mine], over),
            "n_side": (1, xn_s.at[k, mine], xn_s.at[k, mine], side),
            "n_far": (2, xn_s.at[k, theirs], xn_s.at[k, theirs], side),
            "m_over": (6, moe_s.at[k], moe_out.at[k, 3], over),
            "m_side": (7, moe_s.at[k], moe_out.at[k, 0], side),
            "m_far": (8, moe_out.at[k, 3], moe_out.at[k, 1], side),
            "a_far": (9, part_s.at[k, 3], side_s.at[k, 0], side),
            "a_own": (10, part_s.at[k, 1], side_s.at[k, 1], side),
            "b_over": (11, part_s.at[k, 2], over_s.at[k], over),
        }
        at, source, target, peer = table[name]
        return remote(source, target, sems, 12 * k + at, peer)

    def keep(at, k):
        source, target = ((cot_ref.at[k], cot_out.at[k]), (moe_s.at[k], moe_out.at[k, 2]), (xn_s.at[k], xn_out.at[k]))[at]
        return pltpu.make_async_copy(source, target, local_sem.at[3 * k + at])

    if ring:
        here = lax.axis_index("fsdp").astype(I32)
        ahead, behind = next_on_cycle(here), before_on_cycle(here)
        rows = cat_ref.shape[0]

        def hop(k, source, peer):
            at = pl.ds(pl.multiple_of(source * rows, rows), rows)
            return remote(wcat_ref.at[at], wcat_ref.at[at], sems, 24 + k, peer)

        far_rows = far_ref.shape[2]

        chains = far_ref.shape[0]
        onward = (chains + 1) // 2

        def far_hop(c, k, source, peer):
            at = pl.ds(pl.multiple_of(source * far_rows, far_rows), far_rows)
            held = far_ref.at[c] if k < 2 else far_out.at[c, :, at]
            return remote(held, far_out.at[c, :, at], sems, 31 + 7 * c + k, peer)

        def far_last(c, one, two):
            return far_hop(c, 6, one, {"fsdp": ahead}) if c < onward else far_hop(c, 6, two, {"fsdp": behind})

        def far_own():
            at = pl.ds(pl.multiple_of(here * far_rows, far_rows), far_rows)
            return pltpu.make_async_copy(far_ref, far_out.at[:, :, at], local_sem.at[7])

        def along(k):
            one, two = here, here
            for _ in range(k):
                one, two = before_on_cycle(one), next_on_cycle(two)
            return one, two

    tiles = part // 128

    @pl.when(step == 0)
    def _():
        peers = [side, over]
        if ring:
            peers += [{"fsdp": ahead}, {"fsdp": behind}]
        greet(peers)
        if ring:
            wcat_ref[pl.ds(pl.multiple_of(here * rows, rows), rows), :] = cat_ref[...]
            hop(0, here, {"fsdp": ahead}).start()
            hop(1, here, {"fsdp": behind}).start()
            far_own().start()
            for c in range(chains):
                far_hop(c, 0, here, {"fsdp": ahead}).start()
                far_hop(c, 1, here, {"fsdp": behind}).start()
        else:
            wcat_ref[...] = cat_ref[...]
        for k in range(micro):
            def body(i, _, k=k):
                at = pl.ds(pl.multiple_of(i * 128, 128), 128)
                x = tok_ref[k, at, :].astype(F32)
                r = lax.rsqrt(jnp.mean(x * x, axis=1, keepdims=True) + EPS)
                xn_s[k, pl.ds(pl.multiple_of(me * part + i * 128, 128), 128), :] = (x * r * gain1_ref[...]).astype(BF16)
                return 0

            lax.fori_loop(0, tiles, body, 0)
            if k == 0:
                c = 0
                copy("n_over", c).start()
                copy("n_side", c).start()
        if ring:
            one, two = here, here
            for k in range(1, 4):
                one, two = before_on_cycle(one), next_on_cycle(two)
                hop(2 * k - 2, one, {"fsdp": ahead}).wait_recv()
                hop(2 * k, one, {"fsdp": ahead}).start()
                hop(2 * k - 1, two, {"fsdp": behind}).wait_recv()
                if k < 3:
                    hop(2 * k + 1, two, {"fsdp": behind}).start()
        copy("n_over", 0).wait_recv()
        copy("n_far", 0).start()
        copy("n_over", 1).start()
        copy("n_side", 1).start()
        if ring:
            hop(6, before_on_cycle(one), {"fsdp": ahead}).wait_recv()
        copy("n_side", 0).wait_recv()
        copy("n_far", 0).wait_recv()
        for k in range(micro):
            keep(0, k).start()

    if ring:
        for turn in range(3 * chains):
            k, c = turn // chains + 1, turn % chains

            @pl.when(step == 2 + turn * 16 // (3 * chains))
            def _(k=k, c=c):
                one, two = along(k)
                far_hop(c, 2 * k - 2, one, {"fsdp": ahead}).wait_recv()
                far_hop(c, 2 * k - 1, two, {"fsdp": behind}).wait_recv()
                if k < 3:
                    far_hop(c, 2 * k, one, {"fsdp": ahead}).start()
                    far_hop(c, 2 * k + 1, two, {"fsdp": behind}).start()
                else:
                    far_last(c, one, two).start()

    @pl.when(step == STEPS)
    def _():
        c = 1
        copy("n_side", c).wait_recv()
        copy("n_far", c).wait_recv()

    @pl.when((t == 0) & (m < micro))
    def _():
        def body(i, _):
            at = pl.ds(pl.multiple_of(i * QB, QB), QB)
            proj = dot_nn(xn_s[m, at, :], wcat_ref[:, :cols]).astype(BF16)
            for h in range(heads):
                base = h * 3 * HEAD_DIM
                q_s[h, at, :] = proj[:, base : base + HEAD_DIM] * 0.125
                k_s[h, at, :] = proj[:, base + HEAD_DIM : base + 2 * HEAD_DIM]
                vt_s[h, :, at] = proj[:, base + 2 * HEAD_DIM : base + 3 * HEAD_DIM].T
            return 0

        lax.fori_loop(0, nq, body, 0)

    @pl.when((t > 0) & (m < micro))
    def _():
        at = t - 1
        slot = 3 - at // per
        blk = (me ^ slot) * per + at % per

        def finish(mixed_t):
            rows = pl.ds(pl.multiple_of(at % per * QB, QB), QB)
            part_s[m, slot, rows, :] = dot_nt(mixed_t.T, wcat_ref[:, cols:]).astype(BF16)

        attend_rows(blk, lo_ref.at[m], q_s, k_s, vt_s, mixed_ref.at[m], lse_ref.at[m], finish)

    for k in range(micro):
        first = k * STEPS
        c = k

        @pl.when(step == first + per)
        def _(c=c):
            copy("a_far", c).start()

        @pl.when(step == first + 2 * per)
        def _(c=c, k=k):
            copy("a_far", c).wait_recv()
            part_s[k, 2] = (part_s[k, 2].astype(F32) + side_s[k, 0].astype(F32)).astype(BF16)
            copy("b_over", c).start()
            if k == 0:
                copy("n_over", 1).wait_recv()
                copy("n_far", 1).start()
            else:
                copy("m_over", 0).wait_recv()
                copy("m_far", 0).start()

        @pl.when(step == first + 3 * per)
        def _(c=c, k=k):
            copy("a_own", c).start()
        @pl.when(step == first + 4 * per)
        def _(c=c, k=k):
            copy("a_own", c).wait_recv()
            copy("b_over", c).wait_recv()

            def body(i, _):
                at = pl.ds(pl.multiple_of(i * 128, 128), 128)
                hid = (
                    tok_ref[k, at, :].astype(F32) + part_s[k, 0, at, :].astype(F32)
                    + side_s[k, 1, at, :].astype(F32) + over_s[k, at, :].astype(F32)
                )
                hid_ref[k, at, :] = hid
                r = lax.rsqrt(jnp.mean(hid * hid, axis=1, keepdims=True) + EPS)
                moe_s[k, at, :] = (hid * r * gain2_ref[...]).astype(BF16)
                return 0

            lax.fori_loop(0, tiles, body, 0)
            copy("m_over", c).start()
            copy("m_side", c).start()
            keep(1, c).start()
            keep(2, c).start()

    def keep_near():
        return pltpu.make_async_copy(near_ref, near_out, local_sem.at[8])

    def keep_w():
        return pltpu.make_async_copy(wcat_ref, wcat_out, local_sem.at[6])

    @pl.when(step == STEPS)
    def _():
        keep_w().start()
        keep_near().start()

    @pl.when(step == 2 * STEPS)
    def _():
        c, d = 0, 1
        keep_w().wait()
        keep_near().wait()
        copy("m_over", d).wait_recv()
        copy("m_far", d).start()
        for e in (c, d):
            copy("m_side", e).wait_recv()
            copy("m_far", e).wait_recv()
            for name in NAMES:
                copy(name, e).wait_send()
            for at in range(3):
                keep(at, e).wait()
        if ring:
            one, two = here, here
            for k in range(4):
                hop(2 * k, one, {"fsdp": ahead}).wait_send()
                for c in range(chains):
                    if k < 3:
                        far_hop(c, 2 * k, one, {"fsdp": ahead}).wait_send()
                        far_hop(c, 2 * k + 1, two, {"fsdp": behind}).wait_send()
                    else:
                        far_last(c, one, two).wait_send()
                if k < 3:
                    hop(2 * k + 1, two, {"fsdp": behind}).wait_send()
                one, two = before_on_cycle(one), next_on_cycle(two)
            far_own().wait()
            for c in range(chains):
                far_last(c, one, two).wait_recv()


def forward_half(tokens, cotangent, gain1, gain2, cat, low, far, near, ring):
    micro, part, width = tokens.shape
    seq = part * 4
    wide = cat.shape[1]
    heads = wide // (4 * HEAD_DIM)
    hc = heads * HEAD_DIM
    anywhere = pl.BlockSpec(memory_space=pl.ANY)
    return pl.pallas_call(
        lambda *refs: forward_kernel(heads, ring, *refs),
        grid=(2 * STEPS + 1,),
        in_specs=[whole(tokens.shape), anywhere, whole((1, width)), whole((1, width)), whole(cat.shape), whole(low.shape), anywhere, anywhere],
        out_specs=[anywhere, anywhere, anywhere, whole((micro, hc, seq)), whole((micro, 8, seq)),
                   whole((micro, part, width)), anywhere, anywhere, anywhere],
        out_shape=[
            jax.ShapeDtypeStruct((micro, seq, width), BF16),
            jax.ShapeDtypeStruct((micro, 4, part, width), BF16),
            jax.ShapeDtypeStruct((micro, part, width), BF16),
            jax.ShapeDtypeStruct((micro, hc, seq), BF16),
            jax.ShapeDtypeStruct((micro, 8, seq), F32),
            jax.ShapeDtypeStruct((micro, part, width), F32),
            jax.ShapeDtypeStruct((width, wide), BF16),
            jax.ShapeDtypeStruct(far.shape[:2] + (width, far.shape[3]) if ring else (8, 128), BF16),
            jax.ShapeDtypeStruct(near.shape, BF16),
        ],
        scratch_shapes=[
            pltpu.VMEM((micro, seq, width), BF16),
            pltpu.VMEM((heads, seq, HEAD_DIM), BF16),
            pltpu.VMEM((heads, seq, HEAD_DIM), BF16),
            pltpu.VMEM((heads, HEAD_DIM, seq), BF16),
            pltpu.VMEM((micro, 4, part, width), BF16),
            pltpu.VMEM((micro, 2, part, width), BF16),
            pltpu.VMEM((micro, part, width), BF16),
            pltpu.VMEM((micro, part, width), BF16),
            pltpu.VMEM((width, wide), BF16),
            pltpu.SemaphoreType.DMA((31 + 7 * far.shape[0],)),
            pltpu.SemaphoreType.DMA((31 + 7 * far.shape[0],)),
            pltpu.SemaphoreType.DMA((9,)),
        ],
        compiler_params=pltpu.CompilerParams(
            dimension_semantics=("arbitrary",), vmem_limit_bytes=VMEM_LIMIT, collective_id=1, has_side_effects=True
        ),
        cost_estimate=pl.CostEstimate(flops=100_000_000_000, bytes_accessed=100_000_000, transcendentals=0),
        name="forward_half",
    )(tokens, cotangent, gain1, gain2, cat, low, far, near)


def run_copy(n, src, src_at, dst, dst_at, sem, act):
    n = pl.multiple_of(n, ROW_TILE)

    @pl.when(n > 0)
    def _():
        copy = pltpu.make_async_copy(
            src.at[pl.ds(pl.multiple_of(src_at, ROW_TILE), n), :],
            dst.at[pl.ds(pl.multiple_of(dst_at, ROW_TILE), n), :],
            sem,
        )
        if act == "start":
            copy.start()
        else:
            copy.wait()


def sort_rows(experts, tables, xs_ref, xl, sems, values):
    n_ref, lo_ref, off_ref = tables
    step = pl.program_id(0)
    slot = step % 2

    def moves(at, slot, act):
        for e in range(experts):
            run_copy(n_ref[at, e], xl.at[slot], lo_ref[at, e], xs_ref.at[e], off_ref[at, e], sems.at[slot, e], act)

    @pl.when(step >= 2)
    def _():
        moves(step - 2, slot, "wait")

    xl[slot] = values()
    moves(step, slot, "start")

    @pl.when(step == pl.num_programs(0) - 1)
    def _():
        moves(step - 1, 1 - slot, "wait")
        moves(step, slot, "wait")


def dispatch_kernel(experts, n_ref, lo_ref, off_ref, x_ref, rt_ref, pos_ref, xs_ref, meta_ref, xl, sems):
    rows = xl.shape[1]
    part = x_ref.shape[1]
    x = x_ref[0]
    logits = dot_nt(rt_ref[...], x)
    spots = pos_ref[0]
    p0, p1, r0, r1 = spots[0:1], spots[1:2], spots[2:3], spots[3:4]
    names = lax.broadcasted_iota(I32, logits.shape, 0)
    first = jnp.sum(jnp.where(names == r0, logits, 0.0), axis=0, keepdims=True)
    second = jnp.sum(jnp.where(names == r1, logits, 0.0), axis=0, keepdims=True)
    g0 = 1.0 / (1.0 + jnp.exp(second - first))
    g1 = 1.0 / (1.0 + jnp.exp(first - second))
    pick = lax.broadcasted_iota(I32, (8, part), 0)
    meta_ref[0] = jnp.where(
        pick == 0, p0.astype(F32), jnp.where(pick == 1, p1.astype(F32), jnp.where(pick == 2, g0, g1))
    )
    spot = lax.broadcasted_iota(I32, (rows, part), 0)
    plain = jnp.where((spot == p0) | (spot == p1), 1.0, 0.0).astype(BF16)
    sort_rows(experts, (n_ref, lo_ref, off_ref), xs_ref, xl, sems, lambda: dot_nn(plain, x).astype(BF16))


def gated_kernel(experts, n_ref, lo_ref, off_ref, side_ref, far_ref, own_ref, over_ref, meta_ref, gs_ref, c_s, xl, in_sems,
                 sems):
    step = pl.program_id(0)
    slot = step % 2
    rows = xl.shape[1]
    part = c_s.shape[1]

    def load(s):
        for t, ref in enumerate((side_ref, far_ref, own_ref, over_ref)):
            @pl.when(s % 4 == t)
            def _(ref=ref):
                pltpu.make_async_copy(ref.at[s // 4], c_s.at[s % 2], in_sems.at[s % 2]).start()

    @pl.when(step == 0)
    def _():
        load(step)

    @pl.when(step < pl.num_programs(0) - 1)
    def _():
        load(step + 1)

    meta = meta_ref[0]
    spot = lax.broadcasted_iota(I32, (rows, part), 0).astype(F32)
    gated = jnp.where(
        spot == meta[0:1], meta[2:3], jnp.where(spot == meta[1:2], meta[3:4], 0.0)
    ).astype(BF16)
    pltpu.make_async_copy(own_ref.at[0], c_s.at[slot], in_sems.at[slot]).wait()
    sort_rows(experts, (n_ref, lo_ref, off_ref), gs_ref, xl, sems, lambda: dot_nn(gated, c_s[slot]).astype(BF16))


def local_rows(part, experts):
    return -(-(2 * part + experts * (ROW_TILE - 1)) // 128) * 128


def dispatch(tables, xs, router_t, spots, most):
    count, part, width = xs.shape
    experts = router_t.shape[0]
    rows = local_rows(part, experts)
    spec = pltpu.PrefetchScalarGridSpec(
        num_scalar_prefetch=3,
        grid=(count,),
        in_specs=[
            pl.BlockSpec((1, part, width), lambda i, *_: (i, 0, 0)),
            whole(router_t.shape),
            pl.BlockSpec((1, 8, part), lambda i, *_: (i, 0, 0)),
        ],
        out_specs=[pl.BlockSpec(memory_space=pl.ANY), pl.BlockSpec((1, 8, part), lambda i, *_: (i, 0, 0))],
        scratch_shapes=[pltpu.VMEM((2, rows, width), BF16), pltpu.SemaphoreType.DMA((2, experts))],
    )
    return pl.pallas_call(
        lambda *refs: dispatch_kernel(experts, *refs),
        grid_spec=spec,
        out_shape=[
            jax.ShapeDtypeStruct((experts, most, width), BF16),
            jax.ShapeDtypeStruct((count, 8, part), F32),
        ],
        compiler_params=params("arbitrary"),
        cost_estimate=pl.CostEstimate(flops=20_000_000_000, bytes_accessed=20_000_000, transcendentals=0),
        name="dispatch",
    )(*tables, xs, router_t, spots)


def dispatch_gated(tables, parts, meta, experts, most, deps):
    _, part, width = parts[0].shape
    count = meta.shape[0]
    rows = local_rows(part, experts)
    anywhere = pl.BlockSpec(memory_space=pl.ANY)
    spec = pltpu.PrefetchScalarGridSpec(
        num_scalar_prefetch=3,
        grid=(count,),
        in_specs=[anywhere] * 4 + [pl.BlockSpec((1, 8, part), lambda i, *_: (i, 0, 0))] + [anywhere] * len(deps),
        out_specs=anywhere,
        scratch_shapes=[
            pltpu.VMEM((2, part, width), BF16),
            pltpu.VMEM((2, rows, width), BF16),
            pltpu.SemaphoreType.DMA((2,)),
            pltpu.SemaphoreType.DMA((2, experts)),
        ],
    )
    return pl.pallas_call(
        lambda *refs: gated_kernel(experts, *refs[:8], *refs[8 + len(deps) :]),
        grid_spec=spec,
        out_shape=jax.ShapeDtypeStruct((experts, most, width), BF16),
        compiler_params=params("arbitrary"),
        cost_estimate=pl.CostEstimate(flops=20_000_000_000, bytes_accessed=20_000_000, transcendentals=0),
        name="dispatch_gated",
    )(*tables, *parts, meta, *deps)


def live_rows(ref, c, tot):
    live = c * CHUNK + lax.broadcasted_iota(I32, ref.shape[1:], 0) < tot
    return jnp.where(live, ref[0], jnp.zeros((), BF16))


def expert_forward_kernel(e_ref, c_ref, tot_ref, steps_ref, xs_ref, w_ref, od_ref, pre_ref):
    i = pl.program_id(0)

    @pl.when(i < steps_ref[0])
    def _():
        x = live_rows(xs_ref, c_ref[i], tot_ref[e_ref[i]])
        pre = dot_nn(x, w_ref[0, 0])
        pre_ref[0] = pre
        t = jnp.tanh(GELU_A * pre * (1.0 + GELU_B * (pre * pre)))
        act = (0.5 * pre * (1.0 + t)).astype(BF16)
        od_ref[0] = dot_nt(act, w_ref[0, 1]).astype(BF16)


def expert_backward_kernel(split, e_ref, c_ref, tot_ref, steps_ref, out_ref, xs_ref, gs_ref, pre_ref, w_ref, od_ref, *refs):
    dw_refs, (din_s, dout_s) = refs[:-2], refs[-2:]
    i = pl.program_id(0)

    @pl.when(i < steps_ref[0])
    def _():
        e = e_ref[i]
        c = c_ref[i]
        tot = tot_ref[e]
        width = xs_ref.shape[2]
        x = live_rows(xs_ref, c, tot)
        g = live_rows(gs_ref, c, tot)
        pre = pre_ref[0]
        dact = dot_nn(g, w_ref[0, 1])
        square = pre * pre
        t = jnp.tanh(GELU_A * pre * (1.0 + GELU_B * square))
        half = 0.5 * (1.0 + t)
        act = pre * half
        slope = half + (0.5 * GELU_A) * pre * (1.0 - t * t) * (1.0 + (3.0 * GELU_B) * square)
        act_low = act.astype(BF16)
        dpre = (slope * dact).astype(BF16)
        od_ref[0, :, :width] = dot_nt(dpre, w_ref[0, 0]).astype(BF16)
        dot_row = jnp.sum(act * dact, axis=1, keepdims=True)
        lane = lax.broadcasted_iota(I32, (CHUNK, 128), 1)
        od_ref[0, :, width:] = jnp.where(lane == e, dot_row, 0.0).astype(BF16)
        last = (c + 1) * CHUNK >= tot

        @pl.when(c == 0)
        def _():
            din_s[...] = dot_tn(x, dpre)
            dout_s[...] = dot_tn(g, act_low)

        if split:
            @pl.when(c > 0)
            def _():
                din_s[...] += dot_tn(x, dpre)
                dout_s[...] += dot_tn(g, act_low)

            @pl.when(last)
            def _():
                count, rows = dw_refs[0].shape[2:4]
                for which, ref in enumerate(dw_refs):
                    for k in range(count):
                        at = pl.ds(pl.multiple_of(out_ref[which * count + k] * rows, rows), rows)
                        ref[0, 0, k] = din_s[at, :].astype(BF16)
                        ref[0, 1, k] = dout_s[at, :].astype(BF16)
        else:
            @pl.when((c > 0) & jnp.logical_not(last))
            def _():
                din_s[...] += dot_tn(x, dpre)
                dout_s[...] += dot_tn(g, act_low)

            @pl.when((c > 0) & last)
            def _():
                dw_refs[0][0, 0] = (din_s[...] + dot_tn(x, dpre)).astype(BF16)
                dw_refs[0][0, 1] = (dout_s[...] + dot_tn(g, act_low)).astype(BF16)

            @pl.when((c == 0) & last)
            def _():
                dw_refs[0][0, 0] = din_s[...].astype(BF16)
                dw_refs[0][0, 1] = dout_s[...].astype(BF16)


def chunk_list(first, group, totals, chunks):
    need = jnp.maximum((totals[first : first + group] + CHUNK - 1) // CHUNK, 1)
    ends = jnp.cumsum(need)
    at = jnp.minimum(jnp.arange(group * chunks, dtype=I32), ends[-1] - 1)
    which = jnp.sum((at[:, None] >= ends[None, :]).astype(I32), axis=1)
    begin = jnp.sum(jnp.where(which[:, None] == jnp.arange(group), (ends - need)[None, :], 0), axis=1)
    return which + first, at - begin, totals, ends[-1:]


def experts_forward(first, listed, xs, weights, deps=()):
    group, _, width, hidden = weights.shape
    most = xs.shape[1]
    spec = pltpu.PrefetchScalarGridSpec(
        num_scalar_prefetch=4,
        grid=(group * (most // CHUNK),),
        in_specs=[
            pl.BlockSpec((1, CHUNK, width), lambda i, e, c, *_: (e[i], c[i], 0)),
            pl.BlockSpec((1, 2, width, hidden), lambda i, e, c, *_: (e[i] - first, 0, 0, 0)),
        ] + [pl.BlockSpec(memory_space=pl.ANY)] * len(deps),
        out_specs=[
            pl.BlockSpec((1, CHUNK, width), lambda i, e, c, *_: (e[i] - first, c[i], 0)),
            pl.BlockSpec((1, CHUNK, hidden), lambda i, e, c, *_: (e[i] - first, c[i], 0)),
        ],
    )
    return pl.pallas_call(
        lambda *refs: expert_forward_kernel(*refs[:6], *refs[6 + len(deps) :]),
        grid_spec=spec,
        out_shape=[
            jax.ShapeDtypeStruct((group, most, width), BF16),
            jax.ShapeDtypeStruct((group, most, hidden), F32),
        ],
        compiler_params=params("arbitrary"),
        cost_estimate=pl.CostEstimate(flops=group * 6_000_000_000, bytes_accessed=group * 10_000_000, transcendentals=0),
        name="experts_forward",
    )(*listed, xs, weights, *deps)


def experts_backward(first, listed, xs, gs, pre, weights, out_order, split, deps=()):
    group, _, width, hidden = weights.shape
    most = xs.shape[1]
    if split:
        half = (group, 2, out_order.shape[0] // 2, width // out_order.shape[0], hidden)
        dw_shapes = [half, half]
        dw_specs = [pl.BlockSpec((1,) + half[1:], lambda i, e, c, *_: (e[i] - first, 0, 0, 0, 0))] * 2
    else:
        dw_shapes = [weights.shape]
        dw_specs = [pl.BlockSpec((1, 2, width, hidden), lambda i, e, c, *_: (e[i] - first, 0, 0, 0))]
    spec = pltpu.PrefetchScalarGridSpec(
        num_scalar_prefetch=5,
        grid=(group * (most // CHUNK),),
        in_specs=[
            pl.BlockSpec((1, CHUNK, width), lambda i, e, c, *_: (e[i], c[i], 0)),
            pl.BlockSpec((1, CHUNK, width), lambda i, e, c, *_: (e[i], c[i], 0)),
            pl.BlockSpec((1, CHUNK, hidden), lambda i, e, c, *_: (e[i] - first, c[i], 0)),
            pl.BlockSpec((1, 2, width, hidden), lambda i, e, c, *_: (e[i] - first, 0, 0, 0)),
        ] + [pl.BlockSpec(memory_space=pl.ANY)] * len(deps),
        out_specs=[pl.BlockSpec((1, CHUNK, width + 128), lambda i, e, c, *_: (e[i] - first, c[i], 0))] + dw_specs,
        scratch_shapes=[pltpu.VMEM((width, hidden), F32), pltpu.VMEM((width, hidden), F32)],
    )
    return pl.pallas_call(
        lambda *refs: expert_backward_kernel(split, *refs[:9], *refs[9 + len(deps) :]),
        grid_spec=spec,
        out_shape=[jax.ShapeDtypeStruct((group, most, width + 128), BF16)]
        + [jax.ShapeDtypeStruct(shape, BF16) for shape in dw_shapes],
        compiler_params=params("arbitrary"),
        cost_estimate=pl.CostEstimate(flops=group * 10_000_000_000, bytes_accessed=group * 10_000_000, transcendentals=0),
        name="experts_backward",
    )(*listed, out_order, xs, gs, pre, weights, *deps)


def combine_kernel(starts, gated, n_ref, lo_ref, off_ref, *refs):
    od_refs = refs[: len(starts) - 1]
    meta_ref, send_ref, keep_ref, od_l, sems = refs[-5:]
    step = pl.program_id(0)
    slot = step % 2
    rows = od_l.shape[1]
    part = meta_ref.shape[2]

    def moves(at, slot, act):
        for e in range(starts[-1]):
            group = max(i for i, s in enumerate(starts[:-1]) if s <= e)
            n, dst, src = n_ref[at, e], lo_ref[at, e], off_ref[at, e]
            run_copy(n, od_refs[group].at[e - starts[group]], src, od_l.at[slot], dst, sems.at[slot, e], act)

    @pl.when(step == 0)
    def _():
        od_l[...] = jnp.zeros_like(od_l)
        moves(0, 0, "start")

    @pl.when(step < pl.num_programs(0) - 1)
    def _():
        moves(step + 1, 1 - slot, "start")

    meta = meta_ref[0].T
    p0, p1, g0, g1 = (meta[:, i : i + 1] for i in range(4))
    spot = lax.broadcasted_iota(I32, (part, rows), 1).astype(F32)
    is0 = spot == p0
    is1 = spot == p1
    if gated:
        pick = jnp.where(is0, g0, jnp.where(is1, g1, 0.0)).astype(BF16)
    else:
        pick = jnp.where(is0 | is1, 1.0, 0.0).astype(BF16)
    moves(step, slot, "wait")
    out = dot_nn(pick, od_l[slot]).astype(BF16)

    @pl.when(step % 4 < 2)
    def _():
        send_ref[0] = out

    @pl.when(step % 4 >= 2)
    def _():
        keep_ref[0] = out


def combine(tables, ods, meta, gated, deps=()):
    starts = [0]
    for od in ods:
        starts.append(starts[-1] + od.shape[0])
    experts = starts[-1]
    wide = ods[0].shape[2]
    count, _, part = meta.shape
    rows = local_rows(part, experts)
    anywhere = pl.BlockSpec(memory_space=pl.ANY)
    spec = pltpu.PrefetchScalarGridSpec(
        num_scalar_prefetch=3,
        grid=(count,),
        in_specs=[anywhere] * (len(ods) + len(deps)) + [pl.BlockSpec((1, 8, part), lambda i, *_: (i, 0, 0))],
        out_specs=[
            pl.BlockSpec((1, part, wide), lambda i, *_: (i // 4, jnp.minimum(i % 4, 1), 0)),
            pl.BlockSpec((1, part, wide), lambda i, *_: (i // 4, jnp.maximum(i % 4 - 2, 0), 0)),
        ],
        scratch_shapes=[pltpu.VMEM((2, rows, wide), BF16), pltpu.SemaphoreType.DMA((2, experts))],
    )
    return pl.pallas_call(
        lambda *refs: combine_kernel(starts, gated, *refs),
        grid_spec=spec,
        out_shape=[jax.ShapeDtypeStruct((count // 4, 2 * part, wide), BF16)] * 2,
        compiler_params=params("arbitrary"),
        cost_estimate=pl.CostEstimate(flops=20_000_000_000, bytes_accessed=20_000_000, transcendentals=0),
        name="combine",
    )(*tables, *ods, *deps, meta)


def routing(routes, capacity, me, part):
    micro = routes.shape[0]
    experts = capacity.shape[0]
    picks = routes.reshape(micro, 4, part, 2).transpose(0, 1, 3, 2)
    names = jnp.arange(experts, dtype=I32)[:, None]
    named = picks[:, :, :, None, :] == names
    either = named[:, :, 0] | named[:, :, 1]
    earlier = jnp.arange(part)[:, None] < jnp.arange(part)[None, :]
    before = jnp.einsum("mbet,ts->mbes", either.astype(BF16), earlier.astype(BF16), preferred_element_type=F32)
    before = before.astype(I32)
    count = jnp.sum(either.astype(I32), axis=3)
    carry = jnp.cumsum(count, axis=1) - count
    kept = jnp.clip(capacity[None, None, :] - carry, 0, count)
    n = (kept + ROW_TILE - 1) // ROW_TILE * ROW_TILE
    lo = jnp.cumsum(n, axis=2) - n
    place = jnp.where(before < kept[..., None], lo[..., None] + before, -1)
    pos = jnp.max(jnp.where(named, place[:, :, None], -1), axis=3)
    order = me ^ jnp.array([1, 3, 0, 2], I32)
    spots = jnp.concatenate([pos, picks, jnp.zeros_like(pos), jnp.zeros_like(pos)], axis=2)
    spots = jnp.take(spots, order, axis=1)
    n = jnp.take(n, order, axis=1)
    lo = jnp.take(lo, order, axis=1)
    flat = n.reshape(micro * 4, experts)
    off = (jnp.cumsum(flat, axis=0) - flat).reshape(n.shape)
    return n, lo, off, jnp.sum(flat, axis=0), spots


def split_low(v):
    high = v.astype(BF16)
    return high, (v - high.astype(F32)).astype(BF16)


BACK = 34
FAR_STEPS = (3, 6, 10, 17, 20, 23, 28, 32)
BACK_NAMES = (
    "a_dx", "b_dx", "g_over", "g_side", "g_far", "p_far", "p_own", "p_over"
)


def backward_kernel(heads, ring, dxs, dxk, hid_ref, cot_ref, tok_ref, moe_ref, xn_ref,
                    gain1_ref, gain2_ref, router_ref, full_ref, w_ref, lo_ref, mixed_ref, lse_ref, wsend_ref, wkeep_ref,
                    gt_ref, cat_out, small_out, wy_ref, wz_ref, wl_ref, adx_s, bdx_s, kp_s, hid_s, cot_s, moe_s, g_s,
                    part_s, xn_s, k_s, kt_s, v_s, dqt_s, dkt_s, dvt_s, dcat_s, small_s, cat_s, caty_s, catz_s, sm_s,
                    stage_s, send_sem, recv_sem, load_sem):
    micro, part, width = tok_ref.shape
    seq = part * 4
    cols = heads * 3 * HEAD_DIM
    per = part // QB
    nq = seq // QB
    step = pl.program_id(0)
    me = lax.axis_index("tp").astype(I32)
    side = {"tp": me ^ 1}
    over = {"tp": me ^ 2}
    sems = (send_sem, recv_sem)
    mine = pl.ds(pl.multiple_of(me * part, part), part)
    theirs = pl.ds(pl.multiple_of((me ^ 2) * part, part), part)
    top, low = pl.ds(0, part), pl.ds(part, part)
    flat = pl.ds(0, width)

    def copy(name, k):
        table = {
            "a_dx": (0, dxs.at[k], adx_s.at[k], side),
            "b_dx": (1, adx_s.at[k, low], bdx_s.at[k], over),
            "g_over": (4, g_s.at[k, mine], g_s.at[k, mine], over),
            "g_side": (5, g_s.at[k, mine], g_s.at[k, mine], side),
            "g_far": (6, g_s.at[k, theirs], g_s.at[k, theirs], side),
            "p_far": (7, part_s.at[3], adx_s.at[k, top, flat], side),
            "p_own": (8, part_s.at[1], adx_s.at[k, low, flat], side),
            "p_over": (9, part_s.at[2], bdx_s.at[k, :, flat], over),
        }
        at, source, target, peer = table[name]
        return remote(source, target, sems, 10 * k + at, peer)

    def load(name, k):
        table = {
            "keep": (0, dxk.at[k], kp_s),
            "hid": (1, hid_ref.at[k], hid_s),
            "cot": (2, cot_ref.at[k], cot_s),
            "moe": (3, moe_ref.at[k, 2], moe_s),
            "xn": (4, xn_ref.at[k], xn_s),
            "tok": (2, tok_ref.at[k], cot_s),
        }
        at, source, target = table[name]
        return pltpu.make_async_copy(source, target, load_sem.at[at])

    def start(names, k):
        for name in names:
            load(name, k).start()

    def wait(names, k):
        for name in names:
            load(name, k).wait()

    def rows_of(i):
        return pl.ds(pl.multiple_of(i * 128, 128), 128)

    def half_sum(k):
        copy("a_dx", k).wait_recv()
        wait(("keep",), k)

        def body(i, _):
            at = pl.ds(pl.multiple_of(part + i * 128, 128), 128)
            adx_s[k, at, :] = (adx_s[k, at, :].astype(F32) + kp_s[at, :].astype(F32)).astype(BF16)
            return 0

        lax.fori_loop(0, part // 128, body, 0)
        copy("b_dx", k).start()

    def hidden_grad(k):
        copy("b_dx", k).wait_recv()
        wait(("hid", "cot", "moe"), k)

        def body(i, _):
            at = rows_of(i)
            total = adx_s[k, at, :].astype(F32) + kp_s[at, :].astype(F32) + bdx_s[k, at, :].astype(F32)
            products = total[:, width:]
            glog = products - full_ref[k, at, :] * jnp.sum(products, axis=1, keepdims=True)
            high, rest = split_low(glog)
            moe = moe_s[at, :]
            small_s[0:8, :] += (dot_tn(high, moe) + dot_tn(rest, moe))[0:8]
            gm = total[:, :width] + dot_nt(high, router_ref[...]) + dot_nt(rest, router_ref[...])
            hid = hid_s[at, :]
            r = lax.rsqrt(jnp.mean(hid * hid, axis=1, keepdims=True) + EPS)
            u = gm * gain2_ref[...]
            grad = cot_s[at, :].astype(F32) + r * u - hid * (r * r * r * jnp.mean(u * hid, axis=1, keepdims=True))
            small_s[16:24, :] += jnp.sum((gm * hid * r).reshape(16, 8, width), axis=0)
            g_s[k, pl.ds(pl.multiple_of(me * part + i * 128, 128), 128), :] = grad.astype(BF16)
            return 0

        lax.fori_loop(0, part // 128, body, 0)
        copy("b_dx", k).wait_send()
        copy("g_over", k).start()
        copy("g_side", k).start()

    def token_grad(k):
        copy("p_own", k).wait_recv()
        copy("p_over", k).wait_recv()
        wait(("tok",), k)

        def body(i, _):
            at = rows_of(i)
            gn = (
                part_s[0, at, :].astype(F32)
                + adx_s[k, pl.ds(pl.multiple_of(part + i * 128, 128), 128), flat].astype(F32)
                + bdx_s[k, at, flat].astype(F32)
            )
            x = cot_s[at, :].astype(F32)
            r = lax.rsqrt(jnp.mean(x * x, axis=1, keepdims=True) + EPS)
            w = gn * gain1_ref[...]
            back = r * w - x * (r * r * r * jnp.mean(w * x, axis=1, keepdims=True))
            mine_at = pl.ds(pl.multiple_of(me * part + i * 128, 128), 128)
            gt_ref[k, at, :] = (g_s[k, mine_at, :].astype(F32) + back).astype(BF16)
            return 0

        lax.fori_loop(0, part // 128, body, 0)

    if ring:
        here = lax.axis_index("fsdp").astype(I32)
        pair = {"fsdp": here ^ 1}
        line = [{"fsdp": here ^ (2 * k)} for k in range(1, 4)]
        tp_peers = [{"tp": me ^ k} for k in range(1, 4)]

        def extra(name, k=0):
            table = {
                "cat_y": (20, lambda: (cat_s, caty_s, pair)),
                "cat_z": (21 + k, lambda: (cat_s.at[k + 1], catz_s.at[k], line[k])),
                "sm_tp": (24 + k, lambda: (small_s, sm_s.at[k], tp_peers[k])),
                "sm_y": (27, lambda: (small_s, sm_s.at[3], pair)),
                "sm_z": (28 + k, lambda: (small_s, sm_s.at[4 + k], line[k])),
            }
            at, parts = table[name]
            return remote(*parts()[:2], sems, at, parts()[2])

        pieces_w = wy_ref.shape[0]

        def far_y(i):
            return remote(wsend_ref.at[i], wy_ref.at[i], sems, 31 + i, pair)

        def far_z(i, k):
            return remote(wz_ref.at[i, k + 1], wl_ref.at[k, i], sems, 31 + pieces_w + 3 * i + k, line[k])

        def far_load(i, which):
            source = wkeep_ref.at[i] if which == 0 else wy_ref.at[i]
            return pltpu.make_async_copy(source, stage_s.at[which], load_sem.at[8 + which])

        def far_store(i):
            return pltpu.make_async_copy(stage_s.at[2], wz_ref.at[i], load_sem.at[10])

        def far_first(i):
            far_y(i).wait_recv()
            if i + 4 < pieces_w:
                far_y(i + 4).start()
            far_load(i, 0).start()
            far_load(i, 1).start()

        def far_second(i):
            far_load(i, 0).wait()
            far_load(i, 1).wait()
            for k in range(4):
                stage_s[2, k] = (stage_s[0, k].astype(F32) + stage_s[1, k].astype(F32)).astype(BF16)
            far_store(i).start()

        def far_third(i):
            far_store(i).wait()
            for k in range(3):
                far_z(i, k).start()

    def far_piece(i):
        if ring and i < wy_ref.shape[0]:
            far_first(i)
            far_second(i)
            far_third(i)

    @pl.when(step == 0)
    def _():
        peers = [side, over]
        if ring:
            peers += [pair] + line + [tp_peers[2]]
        greet(peers)
        copy("a_dx", 0).start()
        start(("keep", "hid", "cot", "moe", "xn"), 0)
        dcat_s[...] = jnp.zeros_like(dcat_s)
        small_s[...] = jnp.zeros_like(small_s)
        dkt_s[...] = jnp.zeros_like(dkt_s)
        dvt_s[...] = jnp.zeros_like(dvt_s)
        half_sum(0)
        copy("a_dx", 1).start()
        if ring:
            for i in range(min(4, pieces_w)):
                far_y(i).start()
        far_piece(0)
        hidden_grad(0)
        start(("keep", "hid", "cot", "moe"), 1)
        far_piece(1)
        far_piece(2)
        copy("g_over", 0).wait_recv()
        copy("g_far", 0).start()
        half_sum(1)
        far_piece(3)
        copy("g_side", 0).wait_recv()
        copy("g_far", 0).wait_recv()
        wait(("xn",), 0)

    def attend(m, blk):
        rows = pl.ds(pl.multiple_of(blk * QB, QB), QB)
        most = WINDOW // QB + 1

        def window(nk):
            begin = pl.multiple_of((blk - (nk - 1)) * QB, QB)
            keys = pl.ds(begin, nk * QB)
            proj = dot_nn(xn_s[rows, :], w_ref[:, :cols]).astype(BF16)
            g = g_s[m, rows, :]
            gm_t = dot_nn(g, w_ref[:, cols:]).astype(BF16).T
            mixed_t = mixed_ref[m, :, rows]
            dcat_s[cols:, :] += dot_nn(mixed_t, g)
            prod = gm_t.astype(F32) * mixed_t.astype(F32)
            lo = lo_ref[m, :, rows]
            kpos = begin + lax.broadcasted_iota(I32, (nk * QB, QB), 0)
            qpos = blk * QB + lax.broadcasted_iota(I32, (QB, QB), 1)
            for h in range(heads):
                base = h * 3 * HEAD_DIM
                at = slice(h * HEAD_DIM, (h + 1) * HEAD_DIM)
                q = proj[:, base : base + HEAD_DIM] * 0.125
                k_new = proj[:, base + HEAD_DIM : base + 2 * HEAD_DIM]
                k_s[h, rows, :] = k_new
                kt_s[h, :, rows] = k_new.T
                v_s[h, rows, :] = proj[:, base + 2 * HEAD_DIM : base + 3 * HEAD_DIM]
                drow = jnp.sum(prod[at], axis=0, keepdims=True)
                s = dot_nt(k_s[h, keys, :], q)
                s = jnp.where(kpos >= lo, s, NEG)
                last = jnp.where(kpos[(nk - 1) * QB :] <= qpos, s[(nk - 1) * QB :], NEG)
                s = last if nk == 1 else jnp.concatenate([s[: (nk - 1) * QB], last], axis=0)
                p = jnp.exp(s - lse_ref[m, h : h + 1, rows])
                dp = dot_nn(v_s[h, keys, :], gm_t[at])
                ds = (p * (dp - drow)).astype(BF16)
                dvt_s[h, :, keys] += dot_nt(gm_t[at], p.astype(BF16))
                dkt_s[h, :, keys] += dot_nt(q.T, ds)
                dqt_s[h, :, rows] = (dot_nn(kt_s[h, :, keys], ds) * 0.125).astype(BF16)

        for nk in range(1, most + 1):
            cond = (blk == nk - 1) if nk < most else (blk >= most - 1)

            @pl.when(cond)
            def _(nk=nk):
                window(nk)

    def finalize(m, at):
        slot = 3 - at // per
        blk = (me ^ slot) * per + at % per
        rows = pl.ds(pl.multiple_of(blk * QB, QB), QB)
        pieces = []
        for h in range(heads):
            pieces += [dqt_s[h, :, rows], dkt_s[h, :, rows].astype(BF16), dvt_s[h, :, rows].astype(BF16)]
            dkt_s[h, :, rows] = jnp.zeros((HEAD_DIM, QB), F32)
            dvt_s[h, :, rows] = jnp.zeros((HEAD_DIM, QB), F32)
        dproj_t = jnp.concatenate(pieces, axis=0)
        x = xn_s[rows, :]
        dcat_s[:cols, :] += dot_nn(dproj_t, x)
        gn = dot_nt(dproj_t.T, w_ref[:, :cols])
        small_s[8:16, :] += jnp.sum((gn * x.astype(F32)).reshape(QB // 8, 8, width), axis=0)
        part_s[slot, pl.ds(pl.multiple_of(at % per * QB, QB), QB), :] = gn.astype(BF16)

    phase = (step - 1) // nq
    m_now = phase // 2

    @pl.when((step > 0) & (step < BACK - 1) & (phase % 2 == 0))
    def _():
        attend(m_now, (step - 1) % nq)

    @pl.when((step > 0) & (step < BACK - 1) & (phase % 2 == 1))
    def _():
        finalize(m_now, (step - 1) % nq)

    def event(at):
        return pl.when(step == at)

    if ring:
        for i, first in zip(range(4, pieces_w), FAR_STEPS):
            @event(first)
            def _(i=i):
                far_first(i)

            @event(first + 1)
            def _(i=i):
                far_second(i)

            @event(min(first + 2, BACK - 1))
            def _(i=i):
                far_third(i)

    @event(5)
    def _():
        hidden_grad(1)

    @event(10)
    def _():
        copy("g_over", 1).wait_recv()
        copy("g_far", 1).start()

    for k in range(micro):
        first = 16 * k + nq

        @event(first + per)
        def _(k=k):
            copy("p_far", k).start()

        @event(first + 2 * per)
        def _(k=k):
            copy("p_far", k).wait_recv()

            def body(i, _):
                at = rows_of(i)
                part_s[2, at, :] = (part_s[2, at, :].astype(F32) + adx_s[k, at, flat].astype(F32)).astype(BF16)
                return 0

            lax.fori_loop(0, part // 128, body, 0)
            copy("p_over", k).start()

        @event(first + 3 * per)
        def _(k=k):
            copy("p_own", k).start()

    @event(16)
    def _():
        start(("xn",), 1)
        copy("g_side", 1).wait_recv()
        copy("g_far", 1).wait_recv()
        start(("tok",), 0)
        wait(("xn",), 1)

    @event(20)
    def _():
        token_grad(0)
        start(("tok",), 1)
        for name in ("p_far", "p_own", "p_over"):
            copy(name, 0).wait_send()

    @event(BACK - 1)
    def _():
        if ring:
            dcat = dcat_s[...].T
            dcat_s[...] = dcat
            rows = width // 8
            y, z = here % 2, here // 2

            def block(k, parity):
                at = pl.multiple_of((2 * (z ^ k) + parity) * rows, rows)
                return dcat_s[pl.ds(at, rows), :]

            for k in range(4):
                cat_s[k] = block(k, 1 - y).astype(BF16)
            extra("cat_y").start()
            for k in range(3):
                extra("sm_tp", k).start()
            extra("cat_y").wait()
            for k in range(4):
                cat_s[k] = (block(k, y) + caty_s[k].astype(F32)).astype(BF16)
            for k in range(3):
                extra("cat_z", k).start()
            for k in range(3):
                extra("sm_tp", k).wait()
            small_s[...] = (small_s[...] + sm_s[0]) + (sm_s[1] + sm_s[2])
            extra("sm_y").start()
            extra("sm_y").wait()
            small_s[...] += sm_s[3]
            for k in range(3):
                extra("sm_z", k).start()
            for k in range(3):
                extra("sm_z", k).wait()
            small_out[...] = (small_s[...] + sm_s[4]) + (sm_s[5] + sm_s[6])
            for k in range(3):
                extra("cat_z", k).wait()
            token_grad(1)
            cat_out[...] = (
                cat_s[0].astype(F32) + catz_s[0].astype(F32) + catz_s[1].astype(F32) + catz_s[2].astype(F32)
            )
        else:
            token_grad(1)
            small_out[...] = small_s[...]
            cat_out[...] = dcat_s[...].T
        if ring:
            for i in range(pieces_w):
                far_y(i).wait_send()
                for k in range(3):
                    far_z(i, k).wait()
        for k in range(micro):
            for name in BACK_NAMES:
                if name != "b_dx" and not (k == 0 and name in ("p_far", "p_own", "p_over")):
                    copy(name, k).wait_send()


def backward_half(dxs, dxk, hidden, cotangent, tokens, moe, xn, gain1, gain2, router, full, w_cat, low, mixed_t,
                  lse, wsend, wkeep, ring, deps=()):
    micro, part, width = tokens.shape
    seq = part * 4
    wide = w_cat.shape[1]
    heads = wide // (4 * HEAD_DIM)
    hc = heads * HEAD_DIM
    dxw = dxs.shape[2]
    pieces, block = (wsend.shape[0], wsend.shape[1:]) if ring else (1, (8, 128))
    anywhere = pl.BlockSpec(memory_space=pl.ANY)

    def once(shape):
        zeros = (0,) * len(shape)
        return pl.BlockSpec(shape, lambda *_: zeros, pipeline_mode=pl.Buffered(1))

    cat_shape = (width // 8, wide) if ring else (width, wide)
    return pl.pallas_call(
        lambda *refs: backward_kernel(heads, ring, *refs[:17], *refs[17 + len(deps) :]),
        grid=(BACK,),
        in_specs=[anywhere] * 7 + [
            once((1, width)), once((1, width)), once(router.shape), once(full.shape), once(w_cat.shape), once(low.shape),
            once(mixed_t.shape), once(lse.shape),
        ] + [anywhere] * (2 + len(deps)),
        out_specs=[once((micro, part, width)), once(cat_shape), once((24, width))] + [anywhere] * 3,
        out_shape=[
            jax.ShapeDtypeStruct((micro, part, width), BF16),
            jax.ShapeDtypeStruct(cat_shape, F32),
            jax.ShapeDtypeStruct((24, width), F32),
            jax.ShapeDtypeStruct((pieces,) + block, BF16),
            jax.ShapeDtypeStruct((pieces,) + block, BF16),
            jax.ShapeDtypeStruct((3, pieces) + block[1:], BF16),
        ],
        scratch_shapes=[
            pltpu.VMEM((micro, 2 * part, dxw), BF16),
            pltpu.VMEM((micro, part, dxw), BF16),
            pltpu.VMEM((2 * part, dxw), BF16),
            pltpu.VMEM((part, width), F32),
            pltpu.VMEM((part, width), BF16),
            pltpu.VMEM((part, width), BF16),
            pltpu.VMEM((micro, seq, width), BF16),
            pltpu.VMEM((4, part, width), BF16),
            pltpu.VMEM((seq, width), BF16),
            pltpu.VMEM((heads, seq, HEAD_DIM), BF16),
            pltpu.VMEM((heads, HEAD_DIM, seq), BF16),
            pltpu.VMEM((heads, seq, HEAD_DIM), BF16),
            pltpu.VMEM((heads, HEAD_DIM, seq), BF16),
            pltpu.VMEM((heads, HEAD_DIM, seq), F32),
            pltpu.VMEM((heads, HEAD_DIM, seq), F32),
            pltpu.VMEM((wide, width), F32),
            pltpu.VMEM((24, width), F32),
            pltpu.VMEM((4, width // 8, wide), BF16),
            pltpu.VMEM((4, width // 8, wide), BF16),
            pltpu.VMEM((3, width // 8, wide), BF16),
            pltpu.VMEM((7, 24, width), F32),
            pltpu.VMEM((3,) + block, BF16),
            pltpu.SemaphoreType.DMA((31 + 4 * pieces,)),
            pltpu.SemaphoreType.DMA((31 + 4 * pieces,)),
            pltpu.SemaphoreType.DMA((11,)),
        ],
        compiler_params=pltpu.CompilerParams(
            dimension_semantics=("arbitrary",), vmem_limit_bytes=60 * 1024 * 1024, collective_id=2, has_side_effects=True
        ),
        cost_estimate=pl.CostEstimate(flops=150_000_000_000, bytes_accessed=100_000_000, transcendentals=0),
        name="backward_half",
    )(dxs, dxk, hidden, cotangent, tokens, moe, xn, gain1, gain2, router, full, w_cat, low, mixed_t, lse, wsend, wkeep, *deps)


def local(tokens, cotangent, gain_attn, gain_moe, qkv_weight, out_weight, router, w_in, w_out, doc_lengths, routes,
          capacity):
    micro, part, width = tokens.shape
    seq = part * 4
    experts = w_in.shape[0]
    n_fsdp = lax.axis_size("fsdp")
    ring = n_fsdp == 8
    me = lax.axis_index("tp").astype(I32)
    most = -(-micro * (CAP + 4 * ROW_TILE) // CHUNK) * CHUNK
    cat = jnp.concatenate([qkv_weight, out_weight.T], axis=1)
    w_pair = jnp.stack([w_in, w_out.transpose(0, 2, 1)], axis=1)
    if ring:
        row_index = lax.axis_index("fsdp").astype(I32)
        near = 2 * ((row_index // 2) ^ jnp.arange(4, dtype=I32))
        out_order = jnp.concatenate([near + row_index % 2, near + (1 - row_index % 2)])
    else:
        cat = lax.all_gather(cat, "fsdp", axis=0, tiled=True)
        out_order = jnp.zeros((1,), I32)
    near, far = w_pair[:NEAR], w_pair[NEAR:]

    n, lo_at, off, totals, spots = routing(routes, capacity, me, part)
    places = jnp.arange(seq, dtype=I32)
    ends = jnp.cumsum(doc_lengths.reshape(micro, -1), axis=1)
    begins = ends - doc_lengths.reshape(micro, -1)
    doc_start = jnp.max(jnp.where(places >= begins[:, :, None], begins[:, :, None], 0), axis=1)
    low = jnp.maximum(doc_start, places - (WINDOW - 1)).astype(I32)
    router_t = router.T

    low = low[:, None, :]
    xn, moe, cot, mixed_t, lse, hidden, w_cat, w_far, near = forward_half(
        tokens, cotangent, gain_attn[None], gain_moe[None], cat, low, far, near, ring
    )
    w_near = lax.all_gather(near, "fsdp", axis=2, tiled=True)
    if not ring:
        w_far = lax.all_gather(far, "fsdp", axis=2, tiled=True)
    core, chip = [(i, i ^ 1) for i in range(4)], [(i, i ^ 2) for i in range(4)]
    cot_over = lax.ppermute(cot, "tp", chip)
    cot_side = lax.ppermute(cot, "tp", core)
    cot_far = lax.ppermute(cot_over, "tp", core)
    blocks = micro * 4
    tables = tuple(table.reshape(blocks, experts) for table in (n, lo_at, off))
    xs, meta = dispatch(tables, moe.reshape(blocks, part, width), router_t, spots.reshape(blocks, 8, part), most)
    list_near = chunk_list(0, NEAR, totals, most // CHUNK)
    list_far = chunk_list(NEAR, experts - NEAR, totals, most // CHUNK)
    fwd_far, pre_far = experts_forward(NEAR, list_far, xs, w_far)
    fwd_near, pre_near = experts_forward(0, list_near, xs, w_near, (fwd_far,))
    out_send, out_keep = combine(tables, (fwd_near, fwd_far), meta, True)
    gs = dispatch_gated(tables, (cot_side, cot_far, cot, cot_over), meta, experts, most, (out_keep,))
    out_got = lax.ppermute(out_send, "tp", core)
    out_both = out_keep.astype(F32) + out_got.astype(F32)
    out_away = lax.ppermute(out_both[:, part:].astype(BF16), "tp", chip)
    output = (hidden + out_both[:, :part] + out_away.astype(F32)).astype(BF16)
    back_near, dw_near = experts_backward(0, list_near, xs, gs, pre_near, w_near, out_order, False)
    dw_near = lax.psum_scatter(dw_near, "fsdp", scatter_dimension=2, tiled=True).astype(F32)
    back_far, *dw_far = experts_backward(NEAR, list_far, xs, gs, pre_far, w_far, out_order, ring, (back_near, out_both))
    if ring:
        wkeep, wsend = (d.reshape((-1,) + d.shape[2:]) for d in dw_far)
    else:
        dw_far = lax.psum_scatter(dw_far[0], "fsdp", scatter_dimension=2, tiled=True).astype(F32)
        wkeep = wsend = jnp.zeros((8, 128), BF16)

    lanes = jnp.arange(128, dtype=I32)
    mine = lax.dynamic_slice_in_dim(routes, me * part, part, 1)
    gates = meta.reshape(micro, 4, 8, part)[:, 2, 2:4]
    full = jnp.sum(jnp.where(mine[..., None] == lanes, gates.transpose(0, 2, 1)[..., None], 0.0), axis=2)
    router_wide = jnp.pad(router, ((0, 0), (0, 128 - experts)))
    dxs, dxk = combine(tables, (back_near, back_far), meta, False)
    grad_tokens, grad_cat, small, _, wz, wl = backward_half(
        dxs, dxk, hidden, cotangent, tokens, moe, xn, gain_attn[None], gain_moe[None], router_wide, full, w_cat, low, mixed_t,
        lse, wsend, wkeep, ring, (output,)
    )
    cols = qkv_weight.shape[1]
    if not ring:
        grad_cat = lax.psum_scatter(grad_cat.astype(BF16), "fsdp", scatter_dimension=0, tiled=True).astype(F32)
        small = lax.psum(small, ("fsdp", "tp"))
    if ring:
        dw_far = (wz[:, 0].astype(F32) + wl[0].astype(F32)) + (wl[1].astype(F32) + wl[2].astype(F32))
        dw_far = dw_far.reshape((experts - NEAR, 2) + dw_far.shape[1:])
    dw = jnp.concatenate([dw_near, dw_far], axis=0)
    return (
        output,
        grad_tokens,
        jnp.sum(small[8:16], axis=0) / gain_attn,
        jnp.sum(small[16:24], axis=0),
        grad_cat[:, :cols],
        grad_cat[:, cols:].T,
        small[:8].T,
        dw[:, 0],
        dw[:, 1].transpose(0, 2, 1),
    )


def solution(mesh):
    rows = P(None, ("fsdp", "tp"), None)
    in_specs = (
        rows,
        rows,
        P(),
        P(),
        P("fsdp", "tp"),
        P("tp", "fsdp"),
        P(),
        P(None, "fsdp", "tp"),
        P(None, "tp", "fsdp"),
        P(None, "fsdp", None),
        P(None, "fsdp", None),
        P(),
    )
    out_specs = (
        rows,
        rows,
        P(),
        P(),
        P("fsdp", "tp"),
        P("tp", "fsdp"),
        P(),
        P(None, "fsdp", "tp"),
        P(None, "tp", "fsdp"),
    )
    return jax.shard_map(local, mesh=mesh, in_specs=in_specs, out_specs=out_specs, check_vma=False)
```

```python
import math

import jax
import jax.numpy as jnp
from jax import lax
from jax.experimental import pallas as pl
from jax.experimental.pallas import tpu as pltpu
from jax.sharding import PartitionSpec as P

HEAD_DIM = 64
WINDOW = 1024
CAP = 768
ROW_TILE = 16
QB = 256
CHUNK = 256
EPS = 1e-06
NEG = -1e30
F32 = jnp.float32
BF16 = jnp.bfloat16
I32 = jnp.int32
VMEM_LIMIT = 56 * 1024 * 1024
GELU_A = math.sqrt(2.0 / math.pi)
GELU_B = 0.044715
NEAR = 2


def dot_nn(a, b):
    return lax.dot_general(a, b, (((1,), (0,)), ((), ())), preferred_element_type=F32)


def dot_nt(a, b):
    return lax.dot_general(a, b, (((1,), (1,)), ((), ())), preferred_element_type=F32)


def dot_tn(a, b):
    return lax.dot_general(a, b, (((0,), (0,)), ((), ())), preferred_element_type=F32)


def params(*semantics):
    return pltpu.CompilerParams(dimension_semantics=semantics, vmem_limit_bytes=VMEM_LIMIT)


def whole(shape):
    zeros = (0,) * len(shape)
    return pl.BlockSpec(shape, lambda *_: zeros)


def next_on_cycle(i):
    y, z = i % 2, i // 2
    return jnp.where(y == 0, jnp.where(z < 3, i + 2, i + 1), jnp.where(z > 0, i - 2, i - 1))


def before_on_cycle(i):
    y, z = i % 2, i // 2
    return jnp.where(y == 0, jnp.where(z > 0, i - 2, i + 1), jnp.where(z < 3, i + 2, i - 1))


def remote(src, dst, sems, k, peer):
    send, recv = sems
    return pltpu.make_async_remote_copy(
        src_ref=src, dst_ref=dst, send_sem=send.at[k], recv_sem=recv.at[k], device_id=peer,
        device_id_type=pl.DeviceIdType.MESH,
    )


def greet(peers):
    barrier = pltpu.get_barrier_semaphore()
    for peer in peers:
        pl.semaphore_signal(barrier, inc=1, device_id=peer, device_id_type=pl.DeviceIdType.MESH)
    pl.semaphore_wait(barrier, len(peers))


def attend_rows(blk, lo_ref, q_s, k_s, vt_s, mixed_ref, lse_ref, finish):
    heads = q_s.shape[0]
    most = WINDOW // QB + 1

    def window(nk):
        start = pl.multiple_of((blk - (nk - 1)) * QB, QB)
        rows = pl.ds(pl.multiple_of(blk * QB, QB), QB)
        keys = pl.ds(start, nk * QB)
        lo = lo_ref[:, rows]
        kpos = start + lax.broadcasted_iota(I32, (nk * QB, QB), 0)
        qpos = blk * QB + lax.broadcasted_iota(I32, (QB, QB), 1)
        outs = []
        for h in range(heads):
            s = dot_nt(k_s[h, keys, :], q_s[h, rows, :])
            s = jnp.where(kpos >= lo, s, NEG)
            last = jnp.where(kpos[(nk - 1) * QB :] <= qpos, s[(nk - 1) * QB :], NEG)
            s = last if nk == 1 else jnp.concatenate([s[: (nk - 1) * QB], last], axis=0)
            top = jnp.max(s, axis=0, keepdims=True)
            p = jnp.exp(s - top)
            total = jnp.sum(p, axis=0, keepdims=True)
            outs.append(dot_nn(vt_s[h, :, keys], p.astype(BF16)) / total)
            lse_ref[h : h + 1, rows] = top + jnp.log(total)
        mixed_t = jnp.concatenate(outs, axis=0).astype(BF16)
        mixed_ref[:, rows] = mixed_t
        finish(mixed_t)

    for nk in range(1, most + 1):
        cond = (blk == nk - 1) if nk < most else (blk >= most - 1)

        @pl.when(cond)
        def _(nk=nk):
            window(nk)


SLOT_ORDER = (3, 2, 1, 0)
STEPS = 9
NAMES = (
    "n_over", "n_side", "n_far", "m_over", "m_side", "m_far", "a_far", "a_own", "b_over"
)


def forward_kernel(heads, ring, tok_ref, cot_ref, gain1_ref, gain2_ref, cat_ref, lo_ref, far_ref, near_ref, xn_out, moe_out, cot_out,
                   mixed_ref, lse_ref, hid_ref, wcat_out, far_out, near_out, xn_s, q_s, k_s, vt_s, part_s, side_s, over_s, moe_s, wcat_ref, send_sem,
                   recv_sem, local_sem):
    micro, part, width = tok_ref.shape
    seq = part * 4
    cols = heads * 3 * HEAD_DIM
    per = part // QB
    nq = seq // QB
    step = pl.program_id(0)
    m = step // STEPS
    t = step % STEPS
    me = lax.axis_index("tp").astype(I32)
    side = {"tp": me ^ 1}
    over = {"tp": me ^ 2}
    sems = (send_sem, recv_sem)
    mine = pl.ds(pl.multiple_of(me * part, part), part)
    theirs = pl.ds(pl.multiple_of((me ^ 2) * part, part), part)

    def copy(name, k):
        table = {
            "n_over": (0, xn_s.at[k, mine], xn_s.at[k, mine], over),
            "n_side": (1, xn_s.at[k, mine], xn_s.at[k, mine], side),
            "n_far": (2, xn_s.at[k, theirs], xn_s.at[k, theirs], side),
            "m_over": (6, moe_s.at[k], moe_out.at[k, 3], over),
            "m_side": (7, moe_s.at[k], moe_out.at[k, 0], side),
            "m_far": (8, moe_out.at[k, 3], moe_out.at[k, 1], side),
            "a_far": (9, part_s.at[k, 3], side_s.at[k, 0], side),
            "a_own": (10, part_s.at[k, 1], side_s.at[k, 1], side),
            "b_over": (11, part_s.at[k, 2], over_s.at[k], over),
        }
        at, source, target, peer = table[name]
        return remote(source, target, sems, 12 * k + at, peer)

    def keep(at, k):
        source, target = ((cot_ref.at[k], cot_out.at[k]), (moe_s.at[k], moe_out.at[k, 2]), (xn_s.at[k], xn_out.at[k]))[at]
        return pltpu.make_async_copy(source, target, local_sem.at[3 * k + at])

    if ring:
        here = lax.axis_index("fsdp").astype(I32)
        ahead, behind = next_on_cycle(here), before_on_cycle(here)
        rows = cat_ref.shape[0]

        def hop(k, source, peer):
            at = pl.ds(pl.multiple_of(source * rows, rows), rows)
            return remote(wcat_ref.at[at], wcat_ref.at[at], sems, 24 + k, peer)

        far_rows = far_ref.shape[2]

        chains = far_ref.shape[0]
        onward = (chains + 1) // 2

        def far_hop(c, k, source, peer):
            at = pl.ds(pl.multiple_of(source * far_rows, far_rows), far_rows)
            held = far_ref.at[c] if k < 2 else far_out.at[c, :, at]
            return remote(held, far_out.at[c, :, at], sems, 31 + 7 * c + k, peer)

        def chain_starts(first, last):
            for c in range(min(first, chains), min(last, chains)):
                far_hop(c, 0, here, {"fsdp": ahead}).start()
                far_hop(c, 1, here, {"fsdp": behind}).start()

        def far_last(c, one, two):
            return far_hop(c, 6, one, {"fsdp": ahead}) if c < onward else far_hop(c, 6, two, {"fsdp": behind})

        def far_own():
            at = pl.ds(pl.multiple_of(here * far_rows, far_rows), far_rows)
            return pltpu.make_async_copy(far_ref, far_out.at[:, :, at], local_sem.at[7])

        def along(k):
            one, two = here, here
            for _ in range(k):
                one, two = before_on_cycle(one), next_on_cycle(two)
            return one, two

    tiles = part // 128

    @pl.when(step == 0)
    def _():
        peers = [side, over]
        if ring:
            peers += [{"fsdp": ahead}, {"fsdp": behind}]
        greet(peers)
        if ring:
            wcat_ref[pl.ds(pl.multiple_of(here * rows, rows), rows), :] = cat_ref[...]
            hop(0, here, {"fsdp": ahead}).start()
            hop(1, here, {"fsdp": behind}).start()
            far_own().start()
            chain_starts(0, 1)
        else:
            wcat_ref[...] = cat_ref[...]
        for k in range(micro):
            def body(i, _, k=k):
                at = pl.ds(pl.multiple_of(i * 128, 128), 128)
                x = tok_ref[k, at, :].astype(F32)
                r = lax.rsqrt(jnp.mean(x * x, axis=1, keepdims=True) + EPS)
                xn_s[k, pl.ds(pl.multiple_of(me * part + i * 128, 128), 128), :] = (x * r * gain1_ref[...]).astype(BF16)
                return 0

            lax.fori_loop(0, tiles, body, 0)
            if k == 0:
                c = 0
                copy("n_over", c).start()
                copy("n_side", c).start()
        if ring:
            one, two = here, here
            for k in range(1, 4):
                one, two = before_on_cycle(one), next_on_cycle(two)
                hop(2 * k - 2, one, {"fsdp": ahead}).wait_recv()
                hop(2 * k, one, {"fsdp": ahead}).start()
                hop(2 * k - 1, two, {"fsdp": behind}).wait_recv()
                if k < 3:
                    hop(2 * k + 1, two, {"fsdp": behind}).start()
                chain_starts(k, k + 1)
        copy("n_over", 0).wait_recv()
        copy("n_far", 0).start()
        copy("n_over", 1).start()
        copy("n_side", 1).start()
        if ring:
            hop(6, before_on_cycle(one), {"fsdp": ahead}).wait_recv()
            chain_starts(4, chains)
        copy("n_side", 0).wait_recv()
        copy("n_far", 0).wait_recv()
        for k in range(micro):
            keep(0, k).start()

    @pl.when(step == STEPS)
    def _():
        c = 1
        copy("n_side", c).wait_recv()
        copy("n_far", c).wait_recv()

    @pl.when((t == 0) & (m < micro))
    def _():
        def body(i, _):
            at = pl.ds(pl.multiple_of(i * QB, QB), QB)
            proj = dot_nn(xn_s[m, at, :], wcat_ref[:, :cols]).astype(BF16)
            for h in range(heads):
                base = h * 3 * HEAD_DIM
                q_s[h, at, :] = proj[:, base : base + HEAD_DIM] * 0.125
                k_s[h, at, :] = proj[:, base + HEAD_DIM : base + 2 * HEAD_DIM]
                vt_s[h, :, at] = proj[:, base + 2 * HEAD_DIM : base + 3 * HEAD_DIM].T
            return 0

        lax.fori_loop(0, nq, body, 0)

    @pl.when((t > 0) & (m < micro))
    def _():
        at = t - 1
        slot = 3 - at // per
        blk = (me ^ slot) * per + at % per

        def finish(mixed_t):
            rows = pl.ds(pl.multiple_of(at % per * QB, QB), QB)
            part_s[m, slot, rows, :] = dot_nt(mixed_t.T, wcat_ref[:, cols:]).astype(BF16)

        attend_rows(blk, lo_ref.at[m], q_s, k_s, vt_s, mixed_ref.at[m], lse_ref.at[m], finish)

    for k in range(micro):
        first = k * STEPS
        c = k

        @pl.when(step == first + per)
        def _(c=c):
            copy("a_far", c).start()

        @pl.when(step == first + 2 * per)
        def _(c=c, k=k):
            copy("a_far", c).wait_recv()
            part_s[k, 2] = (part_s[k, 2].astype(F32) + side_s[k, 0].astype(F32)).astype(BF16)
            copy("b_over", c).start()
            if k == 0:
                copy("n_over", 1).wait_recv()
                copy("n_far", 1).start()
            else:
                copy("m_over", 0).wait_recv()
                copy("m_far", 0).start()

        @pl.when(step == first + 3 * per)
        def _(c=c, k=k):
            copy("a_own", c).start()
        @pl.when(step == first + 4 * per)
        def _(c=c, k=k):
            copy("a_own", c).wait_recv()
            copy("b_over", c).wait_recv()

            def body(i, _):
                at = pl.ds(pl.multiple_of(i * 128, 128), 128)
                hid = (
                    tok_ref[k, at, :].astype(F32) + part_s[k, 0, at, :].astype(F32)
                    + side_s[k, 1, at, :].astype(F32) + over_s[k, at, :].astype(F32)
                )
                hid_ref[k, at, :] = hid
                r = lax.rsqrt(jnp.mean(hid * hid, axis=1, keepdims=True) + EPS)
                moe_s[k, at, :] = (hid * r * gain2_ref[...]).astype(BF16)
                return 0

            lax.fori_loop(0, tiles, body, 0)
            copy("m_over", c).start()
            copy("m_side", c).start()
            keep(1, c).start()
            keep(2, c).start()

    if ring:
        for turn in range(3 * chains):
            k, c = turn // chains + 1, turn % chains

            @pl.when(step == 2 + turn * 16 // (3 * chains))
            def _(k=k, c=c):
                one, two = along(k)
                far_hop(c, 2 * k - 2, one, {"fsdp": ahead}).wait_recv()
                far_hop(c, 2 * k - 1, two, {"fsdp": behind}).wait_recv()
                if k < 3:
                    far_hop(c, 2 * k, one, {"fsdp": ahead}).start()
                    far_hop(c, 2 * k + 1, two, {"fsdp": behind}).start()
                else:
                    far_last(c, one, two).start()

    def keep_near():
        return pltpu.make_async_copy(near_ref, near_out, local_sem.at[8])

    def keep_w():
        return pltpu.make_async_copy(wcat_ref, wcat_out, local_sem.at[6])

    @pl.when(step == STEPS)
    def _():
        keep_w().start()
        keep_near().start()

    @pl.when(step == 2 * STEPS)
    def _():
        c, d = 0, 1
        keep_w().wait()
        keep_near().wait()
        copy("m_over", d).wait_recv()
        copy("m_far", d).start()
        for e in (c, d):
            copy("m_side", e).wait_recv()
            copy("m_far", e).wait_recv()
            for name in NAMES:
                copy(name, e).wait_send()
            for at in range(3):
                keep(at, e).wait()
        if ring:
            one, two = here, here
            for k in range(4):
                hop(2 * k, one, {"fsdp": ahead}).wait_send()
                for c in range(chains):
                    if k < 3:
                        far_hop(c, 2 * k, one, {"fsdp": ahead}).wait_send()
                        far_hop(c, 2 * k + 1, two, {"fsdp": behind}).wait_send()
                    else:
                        far_last(c, one, two).wait_send()
                if k < 3:
                    hop(2 * k + 1, two, {"fsdp": behind}).wait_send()
                one, two = before_on_cycle(one), next_on_cycle(two)
            far_own().wait()
            for c in range(chains):
                far_last(c, one, two).wait_recv()


def forward_half(tokens, cotangent, gain1, gain2, cat, low, far, near, ring):
    micro, part, width = tokens.shape
    seq = part * 4
    wide = cat.shape[1]
    heads = wide // (4 * HEAD_DIM)
    hc = heads * HEAD_DIM
    anywhere = pl.BlockSpec(memory_space=pl.ANY)
    return pl.pallas_call(
        lambda *refs: forward_kernel(heads, ring, *refs),
        grid=(2 * STEPS + 1,),
        in_specs=[whole(tokens.shape), anywhere, whole((1, width)), whole((1, width)), whole(cat.shape), whole(low.shape), anywhere, anywhere],
        out_specs=[anywhere, anywhere, anywhere, whole((micro, hc, seq)), whole((micro, 8, seq)),
                   whole((micro, part, width)), anywhere, anywhere, anywhere],
        out_shape=[
            jax.ShapeDtypeStruct((micro, seq, width), BF16),
            jax.ShapeDtypeStruct((micro, 4, part, width), BF16),
            jax.ShapeDtypeStruct((micro, part, width), BF16),
            jax.ShapeDtypeStruct((micro, hc, seq), BF16),
            jax.ShapeDtypeStruct((micro, 8, seq), F32),
            jax.ShapeDtypeStruct((micro, part, width), F32),
            jax.ShapeDtypeStruct((width, wide), BF16),
            jax.ShapeDtypeStruct(far.shape[:2] + (width, far.shape[3]) if ring else (8, 128), BF16),
            jax.ShapeDtypeStruct(near.shape, BF16),
        ],
        scratch_shapes=[
            pltpu.VMEM((micro, seq, width), BF16),
            pltpu.VMEM((heads, seq, HEAD_DIM), BF16),
            pltpu.VMEM((heads, seq, HEAD_DIM), BF16),
            pltpu.VMEM((heads, HEAD_DIM, seq), BF16),
            pltpu.VMEM((micro, 4, part, width), BF16),
            pltpu.VMEM((micro, 2, part, width), BF16),
            pltpu.VMEM((micro, part, width), BF16),
            pltpu.VMEM((micro, part, width), BF16),
            pltpu.VMEM((width, wide), BF16),
            pltpu.SemaphoreType.DMA((31 + 7 * far.shape[0],)),
            pltpu.SemaphoreType.DMA((31 + 7 * far.shape[0],)),
            pltpu.SemaphoreType.DMA((9,)),
        ],
        compiler_params=pltpu.CompilerParams(
            dimension_semantics=("arbitrary",), vmem_limit_bytes=VMEM_LIMIT, collective_id=1, has_side_effects=True
        ),
        cost_estimate=pl.CostEstimate(flops=100_000_000_000, bytes_accessed=100_000_000, transcendentals=0),
        name="forward_half",
    )(tokens, cotangent, gain1, gain2, cat, low, far, near)


def run_copy(n, src, src_at, dst, dst_at, sem, act):
    n = pl.multiple_of(n, ROW_TILE)

    @pl.when(n > 0)
    def _():
        copy = pltpu.make_async_copy(
            src.at[pl.ds(pl.multiple_of(src_at, ROW_TILE), n), :],
            dst.at[pl.ds(pl.multiple_of(dst_at, ROW_TILE), n), :],
            sem,
        )
        if act == "start":
            copy.start()
        else:
            copy.wait()


def sort_rows(experts, tables, xs_ref, xl, sems, values):
    n_ref, lo_ref, off_ref = tables
    step = pl.program_id(0)
    slot = step % 2

    def moves(at, slot, act):
        for e in range(experts):
            run_copy(n_ref[at, e], xl.at[slot], lo_ref[at, e], xs_ref.at[e], off_ref[at, e], sems.at[slot, e], act)

    @pl.when(step >= 2)
    def _():
        moves(step - 2, slot, "wait")

    xl[slot] = values()
    moves(step, slot, "start")

    @pl.when(step == pl.num_programs(0) - 1)
    def _():
        moves(step - 1, 1 - slot, "wait")
        moves(step, slot, "wait")


def dispatch_kernel(experts, n_ref, lo_ref, off_ref, x_ref, rt_ref, pos_ref, xs_ref, meta_ref, xl, sems):
    rows = xl.shape[1]
    part = x_ref.shape[1]
    x = x_ref[0]
    logits = dot_nt(rt_ref[...], x)
    spots = pos_ref[0]
    p0, p1, r0, r1 = spots[0:1], spots[1:2], spots[2:3], spots[3:4]
    names = lax.broadcasted_iota(I32, logits.shape, 0)
    first = jnp.sum(jnp.where(names == r0, logits, 0.0), axis=0, keepdims=True)
    second = jnp.sum(jnp.where(names == r1, logits, 0.0), axis=0, keepdims=True)
    g0 = 1.0 / (1.0 + jnp.exp(second - first))
    g1 = 1.0 / (1.0 + jnp.exp(first - second))
    pick = lax.broadcasted_iota(I32, (8, part), 0)
    meta_ref[0] = jnp.where(
        pick == 0, p0.astype(F32), jnp.where(pick == 1, p1.astype(F32), jnp.where(pick == 2, g0, g1))
    )
    spot = lax.broadcasted_iota(I32, (rows, part), 0)
    plain = jnp.where((spot == p0) | (spot == p1), 1.0, 0.0).astype(BF16)
    sort_rows(experts, (n_ref, lo_ref, off_ref), xs_ref, xl, sems, lambda: dot_nn(plain, x).astype(BF16))


def gated_kernel(experts, n_ref, lo_ref, off_ref, side_ref, far_ref, own_ref, over_ref, meta_ref, gs_ref, c_s, xl, in_sems,
                 sems):
    step = pl.program_id(0)
    slot = step % 2
    rows = xl.shape[1]
    part = c_s.shape[1]

    def load(s):
        for t, ref in enumerate((side_ref, far_ref, own_ref, over_ref)):
            @pl.when(s % 4 == t)
            def _(ref=ref):
                pltpu.make_async_copy(ref.at[s // 4], c_s.at[s % 2], in_sems.at[s % 2]).start()

    @pl.when(step == 0)
    def _():
        load(step)

    @pl.when(step < pl.num_programs(0) - 1)
    def _():
        load(step + 1)

    meta = meta_ref[0]
    spot = lax.broadcasted_iota(I32, (rows, part), 0).astype(F32)
    gated = jnp.where(
        spot == meta[0:1], meta[2:3], jnp.where(spot == meta[1:2], meta[3:4], 0.0)
    ).astype(BF16)
    pltpu.make_async_copy(own_ref.at[0], c_s.at[slot], in_sems.at[slot]).wait()
    sort_rows(experts, (n_ref, lo_ref, off_ref), gs_ref, xl, sems, lambda: dot_nn(gated, c_s[slot]).astype(BF16))


def local_rows(part, experts):
    return -(-(2 * part + experts * (ROW_TILE - 1)) // 128) * 128


def dispatch(tables, xs, router_t, spots, most):
    count, part, width = xs.shape
    experts = router_t.shape[0]
    rows = local_rows(part, experts)
    spec = pltpu.PrefetchScalarGridSpec(
        num_scalar_prefetch=3,
        grid=(count,),
        in_specs=[
            pl.BlockSpec((1, part, width), lambda i, *_: (i, 0, 0)),
            whole(router_t.shape),
            pl.BlockSpec((1, 8, part), lambda i, *_: (i, 0, 0)),
        ],
        out_specs=[pl.BlockSpec(memory_space=pl.ANY), pl.BlockSpec((1, 8, part), lambda i, *_: (i, 0, 0))],
        scratch_shapes=[pltpu.VMEM((2, rows, width), BF16), pltpu.SemaphoreType.DMA((2, experts))],
    )
    return pl.pallas_call(
        lambda *refs: dispatch_kernel(experts, *refs),
        grid_spec=spec,
        out_shape=[
            jax.ShapeDtypeStruct((experts, most, width), BF16),
            jax.ShapeDtypeStruct((count, 8, part), F32),
        ],
        compiler_params=params("arbitrary"),
        cost_estimate=pl.CostEstimate(flops=20_000_000_000, bytes_accessed=20_000_000, transcendentals=0),
        name="dispatch",
    )(*tables, xs, router_t, spots)


def dispatch_gated(tables, parts, meta, experts, most, deps):
    _, part, width = parts[0].shape
    count = meta.shape[0]
    rows = local_rows(part, experts)
    anywhere = pl.BlockSpec(memory_space=pl.ANY)
    spec = pltpu.PrefetchScalarGridSpec(
        num_scalar_prefetch=3,
        grid=(count,),
        in_specs=[anywhere] * 4 + [pl.BlockSpec((1, 8, part), lambda i, *_: (i, 0, 0))] + [anywhere] * len(deps),
        out_specs=anywhere,
        scratch_shapes=[
            pltpu.VMEM((2, part, width), BF16),
            pltpu.VMEM((2, rows, width), BF16),
            pltpu.SemaphoreType.DMA((2,)),
            pltpu.SemaphoreType.DMA((2, experts)),
        ],
    )
    return pl.pallas_call(
        lambda *refs: gated_kernel(experts, *refs[:8], *refs[8 + len(deps) :]),
        grid_spec=spec,
        out_shape=jax.ShapeDtypeStruct((experts, most, width), BF16),
        compiler_params=params("arbitrary"),
        cost_estimate=pl.CostEstimate(flops=20_000_000_000, bytes_accessed=20_000_000, transcendentals=0),
        name="dispatch_gated",
    )(*tables, *parts, meta, *deps)


def live_rows(ref, c, tot):
    live = c * CHUNK + lax.broadcasted_iota(I32, ref.shape[1:], 0) < tot
    return jnp.where(live, ref[0], jnp.zeros((), BF16))


def expert_forward_kernel(e_ref, c_ref, tot_ref, steps_ref, xs_ref, w_ref, od_ref, pre_ref):
    i = pl.program_id(0)

    @pl.when(i < steps_ref[0])
    def _():
        x = live_rows(xs_ref, c_ref[i], tot_ref[e_ref[i]])
        pre = dot_nn(x, w_ref[0, 0])
        pre_ref[0] = pre
        t = jnp.tanh(GELU_A * pre * (1.0 + GELU_B * (pre * pre)))
        act = (0.5 * pre * (1.0 + t)).astype(BF16)
        od_ref[0] = dot_nt(act, w_ref[0, 1]).astype(BF16)


def expert_backward_kernel(split, e_ref, c_ref, tot_ref, steps_ref, out_ref, xs_ref, gs_ref, pre_ref, w_ref, od_ref, *refs):
    dw_refs, (din_s, dout_s) = refs[:-2], refs[-2:]
    i = pl.program_id(0)

    @pl.when(i < steps_ref[0])
    def _():
        e = e_ref[i]
        c = c_ref[i]
        tot = tot_ref[e]
        width = xs_ref.shape[2]
        x = live_rows(xs_ref, c, tot)
        g = live_rows(gs_ref, c, tot)
        pre = pre_ref[0]
        dact = dot_nn(g, w_ref[0, 1])
        square = pre * pre
        t = jnp.tanh(GELU_A * pre * (1.0 + GELU_B * square))
        half = 0.5 * (1.0 + t)
        act = pre * half
        slope = half + (0.5 * GELU_A) * pre * (1.0 - t * t) * (1.0 + (3.0 * GELU_B) * square)
        act_low = act.astype(BF16)
        dpre = (slope * dact).astype(BF16)
        od_ref[0, :, :width] = dot_nt(dpre, w_ref[0, 0]).astype(BF16)
        dot_row = jnp.sum(act * dact, axis=1, keepdims=True)
        lane = lax.broadcasted_iota(I32, (CHUNK, 128), 1)
        od_ref[0, :, width:] = jnp.where(lane == e, dot_row, 0.0).astype(BF16)
        last = (c + 1) * CHUNK >= tot

        @pl.when(c == 0)
        def _():
            din_s[...] = dot_tn(x, dpre)
            dout_s[...] = dot_tn(g, act_low)

        if split:
            @pl.when(c > 0)
            def _():
                din_s[...] += dot_tn(x, dpre)
                dout_s[...] += dot_tn(g, act_low)

            @pl.when(last)
            def _():
                count, rows = dw_refs[0].shape[2:4]
                for which, ref in enumerate(dw_refs):
                    for k in range(count):
                        at = pl.ds(pl.multiple_of(out_ref[which * count + k] * rows, rows), rows)
                        ref[0, 0, k] = din_s[at, :].astype(BF16)
                        ref[0, 1, k] = dout_s[at, :].astype(BF16)
        else:
            @pl.when((c > 0) & jnp.logical_not(last))
            def _():
                din_s[...] += dot_tn(x, dpre)
                dout_s[...] += dot_tn(g, act_low)

            @pl.when((c > 0) & last)
            def _():
                dw_refs[0][0, 0] = (din_s[...] + dot_tn(x, dpre)).astype(BF16)
                dw_refs[0][0, 1] = (dout_s[...] + dot_tn(g, act_low)).astype(BF16)

            @pl.when((c == 0) & last)
            def _():
                dw_refs[0][0, 0] = din_s[...].astype(BF16)
                dw_refs[0][0, 1] = dout_s[...].astype(BF16)


def chunk_list(first, group, totals, chunks):
    need = jnp.maximum((totals[first : first + group] + CHUNK - 1) // CHUNK, 1)
    ends = jnp.cumsum(need)
    at = jnp.minimum(jnp.arange(group * chunks, dtype=I32), ends[-1] - 1)
    which = jnp.sum((at[:, None] >= ends[None, :]).astype(I32), axis=1)
    begin = jnp.sum(jnp.where(which[:, None] == jnp.arange(group), (ends - need)[None, :], 0), axis=1)
    return which + first, at - begin, totals, ends[-1:]


def experts_forward(first, listed, xs, weights, deps=()):
    group, _, width, hidden = weights.shape
    most = xs.shape[1]
    spec = pltpu.PrefetchScalarGridSpec(
        num_scalar_prefetch=4,
        grid=(group * (most // CHUNK),),
        in_specs=[
            pl.BlockSpec((1, CHUNK, width), lambda i, e, c, *_: (e[i], c[i], 0)),
            pl.BlockSpec((1, 2, width, hidden), lambda i, e, c, *_: (e[i] - first, 0, 0, 0)),
        ] + [pl.BlockSpec(memory_space=pl.ANY)] * len(deps),
        out_specs=[
            pl.BlockSpec((1, CHUNK, width), lambda i, e, c, *_: (e[i] - first, c[i], 0)),
            pl.BlockSpec((1, CHUNK, hidden), lambda i, e, c, *_: (e[i] - first, c[i], 0)),
        ],
    )
    return pl.pallas_call(
        lambda *refs: expert_forward_kernel(*refs[:6], *refs[6 + len(deps) :]),
        grid_spec=spec,
        out_shape=[
            jax.ShapeDtypeStruct((group, most, width), BF16),
            jax.ShapeDtypeStruct((group, most, hidden), F32),
        ],
        compiler_params=params("arbitrary"),
        cost_estimate=pl.CostEstimate(flops=group * 6_000_000_000, bytes_accessed=group * 10_000_000, transcendentals=0),
        name="experts_forward",
    )(*listed, xs, weights, *deps)


def experts_backward(first, listed, xs, gs, pre, weights, out_order, split, deps=()):
    group, _, width, hidden = weights.shape
    most = xs.shape[1]
    if split:
        half = (group, 2, out_order.shape[0] // 2, width // out_order.shape[0], hidden)
        dw_shapes = [half, half]
        dw_specs = [pl.BlockSpec((1,) + half[1:], lambda i, e, c, *_: (e[i] - first, 0, 0, 0, 0))] * 2
    else:
        dw_shapes = [weights.shape]
        dw_specs = [pl.BlockSpec((1, 2, width, hidden), lambda i, e, c, *_: (e[i] - first, 0, 0, 0))]
    spec = pltpu.PrefetchScalarGridSpec(
        num_scalar_prefetch=5,
        grid=(group * (most // CHUNK),),
        in_specs=[
            pl.BlockSpec((1, CHUNK, width), lambda i, e, c, *_: (e[i], c[i], 0)),
            pl.BlockSpec((1, CHUNK, width), lambda i, e, c, *_: (e[i], c[i], 0)),
            pl.BlockSpec((1, CHUNK, hidden), lambda i, e, c, *_: (e[i] - first, c[i], 0)),
            pl.BlockSpec((1, 2, width, hidden), lambda i, e, c, *_: (e[i] - first, 0, 0, 0)),
        ] + [pl.BlockSpec(memory_space=pl.ANY)] * len(deps),
        out_specs=[pl.BlockSpec((1, CHUNK, width + 128), lambda i, e, c, *_: (e[i] - first, c[i], 0))] + dw_specs,
        scratch_shapes=[pltpu.VMEM((width, hidden), F32), pltpu.VMEM((width, hidden), F32)],
    )
    return pl.pallas_call(
        lambda *refs: expert_backward_kernel(split, *refs[:9], *refs[9 + len(deps) :]),
        grid_spec=spec,
        out_shape=[jax.ShapeDtypeStruct((group, most, width + 128), BF16)]
        + [jax.ShapeDtypeStruct(shape, BF16) for shape in dw_shapes],
        compiler_params=params("arbitrary"),
        cost_estimate=pl.CostEstimate(flops=group * 10_000_000_000, bytes_accessed=group * 10_000_000, transcendentals=0),
        name="experts_backward",
    )(*listed, out_order, xs, gs, pre, weights, *deps)


def combine_kernel(starts, gated, n_ref, lo_ref, off_ref, *refs):
    od_refs = refs[: len(starts) - 1]
    meta_ref, send_ref, keep_ref, od_l, sems = refs[-5:]
    step = pl.program_id(0)
    slot = step % 2
    rows = od_l.shape[1]
    part = meta_ref.shape[2]

    def moves(at, slot, act):
        for e in range(starts[-1]):
            group = max(i for i, s in enumerate(starts[:-1]) if s <= e)
            n, dst, src = n_ref[at, e], lo_ref[at, e], off_ref[at, e]
            run_copy(n, od_refs[group].at[e - starts[group]], src, od_l.at[slot], dst, sems.at[slot, e], act)

    @pl.when(step == 0)
    def _():
        od_l[...] = jnp.zeros_like(od_l)
        moves(0, 0, "start")

    @pl.when(step < pl.num_programs(0) - 1)
    def _():
        moves(step + 1, 1 - slot, "start")

    meta = meta_ref[0].T
    p0, p1, g0, g1 = (meta[:, i : i + 1] for i in range(4))
    spot = lax.broadcasted_iota(I32, (part, rows), 1).astype(F32)
    is0 = spot == p0
    is1 = spot == p1
    if gated:
        pick = jnp.where(is0, g0, jnp.where(is1, g1, 0.0)).astype(BF16)
    else:
        pick = jnp.where(is0 | is1, 1.0, 0.0).astype(BF16)
    moves(step, slot, "wait")
    out = dot_nn(pick, od_l[slot]).astype(BF16)

    @pl.when(step % 4 < 2)
    def _():
        send_ref[0] = out

    @pl.when(step % 4 >= 2)
    def _():
        keep_ref[0] = out


def combine(tables, ods, meta, gated, deps=()):
    starts = [0]
    for od in ods:
        starts.append(starts[-1] + od.shape[0])
    experts = starts[-1]
    wide = ods[0].shape[2]
    count, _, part = meta.shape
    rows = local_rows(part, experts)
    anywhere = pl.BlockSpec(memory_space=pl.ANY)
    spec = pltpu.PrefetchScalarGridSpec(
        num_scalar_prefetch=3,
        grid=(count,),
        in_specs=[anywhere] * (len(ods) + len(deps)) + [pl.BlockSpec((1, 8, part), lambda i, *_: (i, 0, 0))],
        out_specs=[
            pl.BlockSpec((1, part, wide), lambda i, *_: (i // 4, jnp.minimum(i % 4, 1), 0)),
            pl.BlockSpec((1, part, wide), lambda i, *_: (i // 4, jnp.maximum(i % 4 - 2, 0), 0)),
        ],
        scratch_shapes=[pltpu.VMEM((2, rows, wide), BF16), pltpu.SemaphoreType.DMA((2, experts))],
    )
    return pl.pallas_call(
        lambda *refs: combine_kernel(starts, gated, *refs),
        grid_spec=spec,
        out_shape=[jax.ShapeDtypeStruct((count // 4, 2 * part, wide), BF16)] * 2,
        compiler_params=params("arbitrary"),
        cost_estimate=pl.CostEstimate(flops=20_000_000_000, bytes_accessed=20_000_000, transcendentals=0),
        name="combine",
    )(*tables, *ods, *deps, meta)


def routing(routes, capacity, me, part):
    micro = routes.shape[0]
    experts = capacity.shape[0]
    picks = routes.reshape(micro, 4, part, 2).transpose(0, 1, 3, 2)
    names = jnp.arange(experts, dtype=I32)[:, None]
    named = picks[:, :, :, None, :] == names
    either = named[:, :, 0] | named[:, :, 1]
    earlier = jnp.arange(part)[:, None] < jnp.arange(part)[None, :]
    before = jnp.einsum("mbet,ts->mbes", either.astype(BF16), earlier.astype(BF16), preferred_element_type=F32)
    before = before.astype(I32)
    count = jnp.sum(either.astype(I32), axis=3)
    carry = jnp.cumsum(count, axis=1) - count
    kept = jnp.clip(capacity[None, None, :] - carry, 0, count)
    n = (kept + ROW_TILE - 1) // ROW_TILE * ROW_TILE
    lo = jnp.cumsum(n, axis=2) - n
    place = jnp.where(before < kept[..., None], lo[..., None] + before, -1)
    pos = jnp.max(jnp.where(named, place[:, :, None], -1), axis=3)
    order = me ^ jnp.array([1, 3, 0, 2], I32)
    spots = jnp.concatenate([pos, picks, jnp.zeros_like(pos), jnp.zeros_like(pos)], axis=2)
    spots = jnp.take(spots, order, axis=1)
    n = jnp.take(n, order, axis=1)
    lo = jnp.take(lo, order, axis=1)
    flat = n.reshape(micro * 4, experts)
    off = (jnp.cumsum(flat, axis=0) - flat).reshape(n.shape)
    return n, lo, off, jnp.sum(flat, axis=0), spots


def split_low(v):
    high = v.astype(BF16)
    return high, (v - high.astype(F32)).astype(BF16)


BACK = 34
FAR_STEPS = (3, 6, 10, 17, 20, 23, 28, 32)
BACK_NAMES = (
    "a_dx", "a_own", "b_dx", "g_over", "g_side", "g_far", "p_far", "p_own", "p_over"
)


def backward_kernel(heads, ring, dxs, dxk, hid_ref, cot_ref, tok_ref, moe_ref, xn_ref,
                    gain1_ref, gain2_ref, router_ref, full_ref, w_ref, lo_ref, mixed_ref, lse_ref, wsend_ref, wkeep_ref,
                    gt_ref, cat_out, small_out, wy_ref, wz_ref, wo_ref, wl0_ref, wl1_ref, wl2_ref, adx_s, bdx_s, kp_s, hid_s, cot_s, moe_s, g_s,
                    part_s, xn_s, q_s, k_s, kt_s, v_s, dqt_s, dkt_s, dvt_s, dcat_s, small_s, cat_s, caty_s, catz_s, sm_s,
                    stage_s, send_sem, recv_sem, load_sem):
    micro, part, width = tok_ref.shape
    seq = part * 4
    cols = heads * 3 * HEAD_DIM
    per = part // QB
    nq = seq // QB
    step = pl.program_id(0)
    me = lax.axis_index("tp").astype(I32)
    side = {"tp": me ^ 1}
    over = {"tp": me ^ 2}
    sems = (send_sem, recv_sem)
    wl_refs = (wl0_ref, wl1_ref, wl2_ref)
    mine = pl.ds(pl.multiple_of(me * part, part), part)
    theirs = pl.ds(pl.multiple_of((me ^ 2) * part, part), part)
    top, low = pl.ds(0, part), pl.ds(part, part)
    flat = pl.ds(0, width)

    def copy(name, k):
        table = {
            "a_dx": (0, dxs.at[k, low], adx_s.at[k, low], side),
            "a_own": (2, dxs.at[k, top], adx_s.at[k, top], side),
            "b_dx": (1, adx_s.at[k, low], bdx_s.at[k], over),
            "g_over": (4, g_s.at[k, mine], g_s.at[k, mine], over),
            "g_side": (5, g_s.at[k, mine], g_s.at[k, mine], side),
            "g_far": (6, g_s.at[k, theirs], g_s.at[k, theirs], side),
            "p_far": (7, part_s.at[3], adx_s.at[k, top, flat], side),
            "p_own": (8, part_s.at[1], adx_s.at[k, low, flat], side),
            "p_over": (9, part_s.at[2], bdx_s.at[k, :, flat], over),
        }
        at, source, target, peer = table[name]
        return remote(source, target, sems, 10 * k + at, peer)

    def load(name, k):
        table = {
            "keep": (0, dxk.at[k], kp_s),
            "hid": (1, hid_ref.at[k], hid_s),
            "cot": (2, cot_ref.at[k], cot_s),
            "moe": (3, moe_ref.at[k, 2], moe_s),
            "xn": (4, xn_ref.at[k], xn_s),
            "tok": (2, tok_ref.at[k], cot_s),
        }
        at, source, target = table[name]
        return pltpu.make_async_copy(source, target, load_sem.at[at])

    def start(names, k):
        for name in names:
            load(name, k).start()

    def wait(names, k):
        for name in names:
            load(name, k).wait()

    def rows_of(i):
        return pl.ds(pl.multiple_of(i * 128, 128), 128)

    def half_sum(k):
        copy("a_dx", k).wait_recv()
        wait(("keep",), k)

        def body(i, _):
            at = pl.ds(pl.multiple_of(part + i * 128, 128), 128)
            adx_s[k, at, :] = (adx_s[k, at, :].astype(F32) + kp_s[at, :].astype(F32)).astype(BF16)
            return 0

        lax.fori_loop(0, part // 128, body, 0)
        copy("b_dx", k).start()

    def hidden_grad(k):
        copy("a_own", k).wait_recv()
        copy("b_dx", k).wait_recv()
        wait(("hid", "cot", "moe"), k)

        def body(i, _):
            at = rows_of(i)
            total = adx_s[k, at, :].astype(F32) + kp_s[at, :].astype(F32) + bdx_s[k, at, :].astype(F32)
            products = total[:, width:]
            glog = products - full_ref[k, at, :] * jnp.sum(products, axis=1, keepdims=True)
            high, rest = split_low(glog)
            moe = moe_s[at, :]
            small_s[0:8, :] += (dot_tn(high, moe) + dot_tn(rest, moe))[0:8]
            gm = total[:, :width] + dot_nt(high, router_ref[...]) + dot_nt(rest, router_ref[...])
            hid = hid_s[at, :]
            r = lax.rsqrt(jnp.mean(hid * hid, axis=1, keepdims=True) + EPS)
            u = gm * gain2_ref[...]
            grad = cot_s[at, :].astype(F32) + r * u - hid * (r * r * r * jnp.mean(u * hid, axis=1, keepdims=True))
            small_s[16:24, :] += jnp.sum((gm * hid * r).reshape(16, 8, width), axis=0)
            g_s[k, pl.ds(pl.multiple_of(me * part + i * 128, 128), 128), :] = grad.astype(BF16)
            return 0

        lax.fori_loop(0, part // 128, body, 0)
        copy("b_dx", k).wait_send()
        copy("g_over", k).start()
        copy("g_side", k).start()

    def token_grad(k):
        copy("p_own", k).wait_recv()
        copy("p_over", k).wait_recv()
        wait(("tok",), k)

        def body(i, _):
            at = rows_of(i)
            gn = (
                part_s[0, at, :].astype(F32)
                + adx_s[k, pl.ds(pl.multiple_of(part + i * 128, 128), 128), flat].astype(F32)
                + bdx_s[k, at, flat].astype(F32)
            )
            x = cot_s[at, :].astype(F32)
            r = lax.rsqrt(jnp.mean(x * x, axis=1, keepdims=True) + EPS)
            w = gn * gain1_ref[...]
            back = r * w - x * (r * r * r * jnp.mean(w * x, axis=1, keepdims=True))
            mine_at = pl.ds(pl.multiple_of(me * part + i * 128, 128), 128)
            gt_ref[k, at, :] = (g_s[k, mine_at, :].astype(F32) + back).astype(BF16)
            return 0

        lax.fori_loop(0, part // 128, body, 0)

    if ring:
        here = lax.axis_index("fsdp").astype(I32)
        pair = {"fsdp": here ^ 1}
        line = [{"fsdp": here ^ (2 * k)} for k in range(1, 4)]
        tp_peers = [{"tp": me ^ k} for k in range(1, 4)]

        def extra(name, k=0):
            table = {
                "cat_y": (20, lambda: (cat_s, caty_s, pair)),
                "cat_z": (21 + k, lambda: (cat_s.at[k + 1], catz_s.at[k], line[k])),
                "sm_tp": (24 + k, lambda: (small_s, sm_s.at[k], tp_peers[k])),
                "sm_y": (27, lambda: (small_s, sm_s.at[3], pair)),
                "sm_z": (28 + k, lambda: (small_s, sm_s.at[4 + k], line[k])),
            }
            at, parts = table[name]
            return remote(*parts()[:2], sems, at, parts()[2])

        pieces_w = wy_ref.shape[0]

        def far_y(i):
            return remote(wsend_ref.at[i], wy_ref.at[i], sems, 31 + i, pair)

        def far_z(i, k):
            return remote(wz_ref.at[i, k], wl_refs[k].at[i], sems, 31 + pieces_w + 3 * i + k, line[k])

        def far_load(i, which):
            source = wkeep_ref.at[i] if which == 0 else wy_ref.at[i]
            return pltpu.make_async_copy(source, stage_s.at[which], load_sem.at[8 + which])

        def far_store(i):
            return (
                pltpu.make_async_copy(stage_s.at[2, 1:4], wz_ref.at[i], load_sem.at[10]),
                pltpu.make_async_copy(stage_s.at[2, 0], wo_ref.at[i], load_sem.at[11]),
            )

        def far_first(i):
            far_y(i).wait_recv()
            if i + 4 < pieces_w:
                far_y(i + 4).start()
            far_load(i, 0).start()
            far_load(i, 1).start()

        def far_second(i):
            far_load(i, 0).wait()
            far_load(i, 1).wait()
            for k in range(4):
                stage_s[2, k] = (stage_s[0, k].astype(F32) + stage_s[1, k].astype(F32)).astype(BF16)
            for store in far_store(i):
                store.start()

        def far_third(i):
            for store in far_store(i):
                store.wait()
            for k in range(3):
                far_z(i, k).start()

    def project():
        def body(i, _):
            rows = pl.ds(pl.multiple_of(i * QB, QB), QB)
            proj = dot_nn(xn_s[rows, :], w_ref[:, :cols]).astype(BF16)
            for h in range(heads):
                base = h * 3 * HEAD_DIM
                q_s[h, rows, :] = proj[:, base : base + HEAD_DIM] * 0.125
                k_new = proj[:, base + HEAD_DIM : base + 2 * HEAD_DIM]
                k_s[h, rows, :] = k_new
                kt_s[h, :, rows] = k_new.T
                v_s[h, rows, :] = proj[:, base + 2 * HEAD_DIM : base + 3 * HEAD_DIM]
            return 0

        lax.fori_loop(0, nq, body, 0)

    def far_piece(i):
        if ring and i < wy_ref.shape[0]:
            far_first(i)
            far_second(i)
            far_third(i)

    @pl.when(step == 0)
    def _():
        peers = [side, over]
        if ring:
            peers += [pair] + line + [tp_peers[2]]
        greet(peers)
        copy("a_dx", 0).start()
        copy("a_own", 0).start()
        start(("keep", "hid", "cot", "moe", "xn"), 0)
        dcat_s[...] = jnp.zeros_like(dcat_s)
        small_s[...] = jnp.zeros_like(small_s)
        dkt_s[...] = jnp.zeros_like(dkt_s)
        dvt_s[...] = jnp.zeros_like(dvt_s)
        half_sum(0)
        copy("a_dx", 1).start()
        copy("a_own", 1).start()
        if ring:
            for i in range(min(4, pieces_w)):
                far_y(i).start()
        wait(("xn",), 0)
        project()
        far_piece(0)
        hidden_grad(0)
        start(("keep", "hid", "cot", "moe"), 1)
        far_piece(1)
        far_piece(2)
        copy("g_over", 0).wait_recv()
        copy("g_far", 0).start()
        half_sum(1)
        far_piece(3)
        copy("g_side", 0).wait_recv()
        copy("g_far", 0).wait_recv()

    def attend(m, blk):
        rows = pl.ds(pl.multiple_of(blk * QB, QB), QB)
        most = WINDOW // QB + 1

        def window(nk):
            begin = pl.multiple_of((blk - (nk - 1)) * QB, QB)
            keys = pl.ds(begin, nk * QB)
            g = g_s[m, rows, :]
            gm_t = dot_nn(g, w_ref[:, cols:]).astype(BF16).T
            mixed_t = mixed_ref[m, :, rows]
            dcat_s[cols:, :] += dot_nn(mixed_t, g)
            prod = gm_t.astype(F32) * mixed_t.astype(F32)
            lo = lo_ref[m, :, rows]
            kpos = begin + lax.broadcasted_iota(I32, (nk * QB, QB), 0)
            qpos = blk * QB + lax.broadcasted_iota(I32, (QB, QB), 1)
            for h in range(heads):
                at = slice(h * HEAD_DIM, (h + 1) * HEAD_DIM)
                q = q_s[h, rows, :]
                drow = jnp.sum(prod[at], axis=0, keepdims=True)
                s = dot_nt(k_s[h, keys, :], q)
                s = jnp.where(kpos >= lo, s, NEG)
                last = jnp.where(kpos[(nk - 1) * QB :] <= qpos, s[(nk - 1) * QB :], NEG)
                s = last if nk == 1 else jnp.concatenate([s[: (nk - 1) * QB], last], axis=0)
                p = jnp.exp(s - lse_ref[m, h : h + 1, rows])
                dp = dot_nn(v_s[h, keys, :], gm_t[at])
                ds = (p * (dp - drow)).astype(BF16)
                dvt_s[h, :, keys] += dot_nt(gm_t[at], p.astype(BF16))
                dkt_s[h, :, keys] += dot_nt(q.T, ds)
                dqt_s[h, :, rows] = (dot_nn(kt_s[h, :, keys], ds) * 0.125).astype(BF16)

        for nk in range(1, most + 1):
            cond = (blk == nk - 1) if nk < most else (blk >= most - 1)

            @pl.when(cond)
            def _(nk=nk):
                window(nk)

    def finalize(m, at):
        slot = 3 - at // per
        blk = (me ^ slot) * per + at % per
        rows = pl.ds(pl.multiple_of(blk * QB, QB), QB)
        pieces = []
        for h in range(heads):
            pieces += [dqt_s[h, :, rows], dkt_s[h, :, rows].astype(BF16), dvt_s[h, :, rows].astype(BF16)]
            dkt_s[h, :, rows] = jnp.zeros((HEAD_DIM, QB), F32)
            dvt_s[h, :, rows] = jnp.zeros((HEAD_DIM, QB), F32)
        dproj_t = jnp.concatenate(pieces, axis=0)
        x = xn_s[rows, :]
        dcat_s[:cols, :] += dot_nn(dproj_t, x)
        gn = dot_nt(dproj_t.T, w_ref[:, :cols])
        small_s[8:16, :] += jnp.sum((gn * x.astype(F32)).reshape(QB // 8, 8, width), axis=0)
        part_s[slot, pl.ds(pl.multiple_of(at % per * QB, QB), QB), :] = gn.astype(BF16)

    phase = (step - 1) // nq
    m_now = phase // 2

    @pl.when((step > 0) & (step < BACK - 1) & (phase % 2 == 0))
    def _():
        attend(m_now, (step - 1) % nq)

    @pl.when((step > 0) & (step < BACK - 1) & (phase % 2 == 1))
    def _():
        finalize(m_now, (step - 1) % nq)

    def event(at):
        return pl.when(step == at)

    if ring:
        for i, first in zip(range(4, pieces_w), FAR_STEPS):
            @event(first)
            def _(i=i):
                far_first(i)

            @event(first + 1)
            def _(i=i):
                far_second(i)

            @event(min(first + 2, BACK - 1))
            def _(i=i):
                far_third(i)

    @event(5)
    def _():
        hidden_grad(1)

    @event(10)
    def _():
        copy("g_over", 1).wait_recv()
        copy("g_far", 1).start()

    for k in range(micro):
        first = 16 * k + nq

        @event(first + per)
        def _(k=k):
            copy("p_far", k).start()

        @event(first + 2 * per)
        def _(k=k):
            copy("p_far", k).wait_recv()

            def body(i, _):
                at = rows_of(i)
                part_s[2, at, :] = (part_s[2, at, :].astype(F32) + adx_s[k, at, flat].astype(F32)).astype(BF16)
                return 0

            lax.fori_loop(0, part // 128, body, 0)
            copy("p_over", k).start()

        @event(first + 3 * per)
        def _(k=k):
            copy("p_own", k).start()

    @event(16)
    def _():
        start(("xn",), 1)
        copy("g_side", 1).wait_recv()
        copy("g_far", 1).wait_recv()
        start(("tok",), 0)
        wait(("xn",), 1)
        project()

    @event(20)
    def _():
        token_grad(0)
        start(("tok",), 1)
        for name in ("p_far", "p_own", "p_over"):
            copy(name, 0).wait_send()

    @event(BACK - 1)
    def _():
        if ring:
            dcat = dcat_s[...].T
            dcat_s[...] = dcat
            rows = width // 8
            y, z = here % 2, here // 2

            def block(k, parity):
                at = pl.multiple_of((2 * (z ^ k) + parity) * rows, rows)
                return dcat_s[pl.ds(at, rows), :]

            for k in range(4):
                cat_s[k] = block(k, 1 - y).astype(BF16)
            extra("cat_y").start()
            for k in range(3):
                extra("sm_tp", k).start()
            extra("cat_y").wait()
            for k in range(4):
                cat_s[k] = (block(k, y) + caty_s[k].astype(F32)).astype(BF16)
            for k in range(3):
                extra("cat_z", k).start()
            for k in range(3):
                extra("sm_tp", k).wait()
            small_s[...] = (small_s[...] + sm_s[0]) + (sm_s[1] + sm_s[2])
            extra("sm_y").start()
            extra("sm_y").wait()
            small_s[...] += sm_s[3]
            for k in range(3):
                extra("sm_z", k).start()
            for k in range(3):
                extra("sm_z", k).wait()
            small_out[...] = (small_s[...] + sm_s[4]) + (sm_s[5] + sm_s[6])
            for k in range(3):
                extra("cat_z", k).wait()
            token_grad(1)
            cat_out[...] = (
                cat_s[0].astype(F32) + catz_s[0].astype(F32) + catz_s[1].astype(F32) + catz_s[2].astype(F32)
            )
        else:
            token_grad(1)
            small_out[...] = small_s[...]
            cat_out[...] = dcat_s[...].T
        if ring:
            for i in range(pieces_w):
                far_y(i).wait_send()
                for k in range(3):
                    far_z(i, k).wait()
        for k in range(micro):
            for name in BACK_NAMES:
                if name != "b_dx" and not (k == 0 and name in ("p_far", "p_own", "p_over")):
                    copy(name, k).wait_send()


def backward_half(dxs, dxk, hidden, cotangent, tokens, moe, xn, gain1, gain2, router, full, w_cat, low, mixed_t,
                  lse, wsend, wkeep, ring, deps=()):
    micro, part, width = tokens.shape
    seq = part * 4
    wide = w_cat.shape[1]
    heads = wide // (4 * HEAD_DIM)
    hc = heads * HEAD_DIM
    dxw = dxs.shape[2]
    pieces, block = (wsend.shape[0], wsend.shape[1:]) if ring else (1, (8, 128))
    anywhere = pl.BlockSpec(memory_space=pl.ANY)

    def once(shape):
        zeros = (0,) * len(shape)
        return pl.BlockSpec(shape, lambda *_: zeros, pipeline_mode=pl.Buffered(1))

    cat_shape = (width // 8, wide) if ring else (width, wide)
    return pl.pallas_call(
        lambda *refs: backward_kernel(heads, ring, *refs[:17], *refs[17 + len(deps) :]),
        grid=(BACK,),
        in_specs=[anywhere] * 7 + [
            once((1, width)), once((1, width)), once(router.shape), once(full.shape), once(w_cat.shape), once(low.shape),
            once(mixed_t.shape), once(lse.shape),
        ] + [anywhere] * (2 + len(deps)),
        out_specs=[once((micro, part, width)), once(cat_shape), once((24, width))] + [anywhere] * 6,
        out_shape=[
            jax.ShapeDtypeStruct((micro, part, width), BF16),
            jax.ShapeDtypeStruct(cat_shape, F32),
            jax.ShapeDtypeStruct((24, width), F32),
            jax.ShapeDtypeStruct((pieces,) + block, BF16),
            jax.ShapeDtypeStruct((pieces, 3) + block[1:], BF16),
        ] + [jax.ShapeDtypeStruct((pieces,) + block[1:], BF16)] * 4,
        scratch_shapes=[
            pltpu.VMEM((micro, 2 * part, dxw), BF16),
            pltpu.VMEM((micro, part, dxw), BF16),
            pltpu.VMEM((2 * part, dxw), BF16),
            pltpu.VMEM((part, width), F32),
            pltpu.VMEM((part, width), BF16),
            pltpu.VMEM((part, width), BF16),
            pltpu.VMEM((micro, seq, width), BF16),
            pltpu.VMEM((4, part, width), BF16),
            pltpu.VMEM((seq, width), BF16),
            pltpu.VMEM((heads, seq, HEAD_DIM), BF16),
            pltpu.VMEM((heads, seq, HEAD_DIM), BF16),
            pltpu.VMEM((heads, HEAD_DIM, seq), BF16),
            pltpu.VMEM((heads, seq, HEAD_DIM), BF16),
            pltpu.VMEM((heads, HEAD_DIM, seq), BF16),
            pltpu.VMEM((heads, HEAD_DIM, seq), F32),
            pltpu.VMEM((heads, HEAD_DIM, seq), F32),
            pltpu.VMEM((wide, width), F32),
            pltpu.VMEM((24, width), F32),
            pltpu.VMEM((4, width // 8, wide), BF16),
            pltpu.VMEM((4, width // 8, wide), BF16),
            pltpu.VMEM((3, width // 8, wide), BF16),
            pltpu.VMEM((7, 24, width), F32),
            pltpu.VMEM((3,) + block, BF16),
            pltpu.SemaphoreType.DMA((31 + 4 * pieces,)),
            pltpu.SemaphoreType.DMA((31 + 4 * pieces,)),
            pltpu.SemaphoreType.DMA((12,)),
        ],
        compiler_params=pltpu.CompilerParams(
            dimension_semantics=("arbitrary",), vmem_limit_bytes=60 * 1024 * 1024, collective_id=2, has_side_effects=True
        ),
        cost_estimate=pl.CostEstimate(flops=150_000_000_000, bytes_accessed=100_000_000, transcendentals=0),
        name="backward_half",
    )(dxs, dxk, hidden, cotangent, tokens, moe, xn, gain1, gain2, router, full, w_cat, low, mixed_t, lse, wsend, wkeep, *deps)


def local(tokens, cotangent, gain_attn, gain_moe, qkv_weight, out_weight, router, w_in, w_out, doc_lengths, routes,
          capacity):
    micro, part, width = tokens.shape
    seq = part * 4
    experts = w_in.shape[0]
    n_fsdp = lax.axis_size("fsdp")
    ring = n_fsdp == 8
    me = lax.axis_index("tp").astype(I32)
    most = -(-micro * (CAP + 4 * ROW_TILE) // CHUNK) * CHUNK
    cat = jnp.concatenate([qkv_weight, out_weight.T], axis=1)
    w_pair = jnp.stack([w_in, w_out.transpose(0, 2, 1)], axis=1)
    if ring:
        row_index = lax.axis_index("fsdp").astype(I32)
        near = 2 * ((row_index // 2) ^ jnp.arange(4, dtype=I32))
        out_order = jnp.concatenate([near + row_index % 2, near + (1 - row_index % 2)])
    else:
        cat = lax.all_gather(cat, "fsdp", axis=0, tiled=True)
        out_order = jnp.zeros((1,), I32)
    near, far = w_pair[:NEAR], w_pair[NEAR:]

    n, lo_at, off, totals, spots = routing(routes, capacity, me, part)
    places = jnp.arange(seq, dtype=I32)
    ends = jnp.cumsum(doc_lengths.reshape(micro, -1), axis=1)
    begins = ends - doc_lengths.reshape(micro, -1)
    doc_start = jnp.max(jnp.where(places >= begins[:, :, None], begins[:, :, None], 0), axis=1)
    low = jnp.maximum(doc_start, places - (WINDOW - 1)).astype(I32)
    router_t = router.T

    low = low[:, None, :]
    xn, moe, cot, mixed_t, lse, hidden, w_cat, w_far, near = forward_half(
        tokens, cotangent, gain_attn[None], gain_moe[None], cat, low, far, near, ring
    )
    w_near = lax.all_gather(near, "fsdp", axis=2, tiled=True)
    if not ring:
        w_far = lax.all_gather(far, "fsdp", axis=2, tiled=True)
    core, chip = [(i, i ^ 1) for i in range(4)], [(i, i ^ 2) for i in range(4)]
    cot_over = lax.ppermute(cot, "tp", chip)
    cot_side = lax.ppermute(cot, "tp", core)
    cot_far = lax.ppermute(cot_over, "tp", core)
    blocks = micro * 4
    tables = tuple(table.reshape(blocks, experts) for table in (n, lo_at, off))
    xs, meta = dispatch(tables, moe.reshape(blocks, part, width), router_t, spots.reshape(blocks, 8, part), most)
    list_near = chunk_list(0, NEAR, totals, most // CHUNK)
    list_far = chunk_list(NEAR, experts - NEAR, totals, most // CHUNK)
    fwd_far, pre_far = experts_forward(NEAR, list_far, xs, w_far)
    fwd_near, pre_near = experts_forward(0, list_near, xs, w_near, (fwd_far,))
    out_send, out_keep = combine(tables, (fwd_near, fwd_far), meta, True)
    gs = dispatch_gated(tables, (cot_side, cot_far, cot, cot_over), meta, experts, most, (out_keep,))
    out_got = lax.ppermute(out_send, "tp", core)
    out_both = out_keep.astype(F32) + out_got.astype(F32)
    out_away = lax.ppermute(out_both[:, part:].astype(BF16), "tp", chip)
    output = (hidden + out_both[:, :part] + out_away.astype(F32)).astype(BF16)
    back_near, dw_near = experts_backward(0, list_near, xs, gs, pre_near, w_near, out_order, False)
    dw_near = lax.psum_scatter(dw_near, "fsdp", scatter_dimension=2, tiled=True).astype(F32)
    back_far, *dw_far = experts_backward(NEAR, list_far, xs, gs, pre_far, w_far, out_order, ring, (back_near, out_both))
    if ring:
        wkeep, wsend = (d.reshape((-1,) + d.shape[2:]) for d in dw_far)
    else:
        dw_far = lax.psum_scatter(dw_far[0], "fsdp", scatter_dimension=2, tiled=True).astype(F32)
        wkeep = wsend = jnp.zeros((8, 128), BF16)

    lanes = jnp.arange(128, dtype=I32)
    mine = lax.dynamic_slice_in_dim(routes, me * part, part, 1)
    gates = meta.reshape(micro, 4, 8, part)[:, 2, 2:4]
    full = jnp.sum(jnp.where(mine[..., None] == lanes, gates.transpose(0, 2, 1)[..., None], 0.0), axis=2)
    router_wide = jnp.pad(router, ((0, 0), (0, 128 - experts)))
    dxs, dxk = combine(tables, (back_near, back_far), meta, False)
    grad_tokens, grad_cat, small, _, _, *shares = backward_half(
        dxs, dxk, hidden, cotangent, tokens, moe, xn, gain_attn[None], gain_moe[None], router_wide, full, w_cat, low, mixed_t,
        lse, wsend, wkeep, ring, (output,)
    )
    cols = qkv_weight.shape[1]
    if not ring:
        grad_cat = lax.psum_scatter(grad_cat.astype(BF16), "fsdp", scatter_dimension=0, tiled=True).astype(F32)
        small = lax.psum(small, ("fsdp", "tp"))
    if ring:
        dw_far = sum(share.astype(F32) for share in shares)
        dw_far = dw_far.reshape((experts - NEAR, 2) + dw_far.shape[1:])
    dw = jnp.concatenate([dw_near, dw_far], axis=0)
    return (
        output,
        grad_tokens,
        jnp.sum(small[8:16], axis=0) / gain_attn,
        jnp.sum(small[16:24], axis=0),
        grad_cat[:, :cols],
        grad_cat[:, cols:].T,
        small[:8].T,
        dw[:, 0],
        dw[:, 1].transpose(0, 2, 1),
    )


def solution(mesh):
    rows = P(None, ("fsdp", "tp"), None)
    in_specs = (
        rows,
        rows,
        P(),
        P(),
        P("fsdp", "tp"),
        P("tp", "fsdp"),
        P(),
        P(None, "fsdp", "tp"),
        P(None, "tp", "fsdp"),
        P(None, "fsdp", None),
        P(None, "fsdp", None),
        P(),
    )
    out_specs = (
        rows,
        rows,
        P(),
        P(),
        P("fsdp", "tp"),
        P("tp", "fsdp"),
        P(),
        P(None, "fsdp", "tp"),
        P(None, "tp", "fsdp"),
    )
    return jax.shard_map(local, mesh=mesh, in_specs=in_specs, out_specs=out_specs, check_vma=False)
```

```python
import math

import jax
import jax.numpy as jnp
from jax import lax
from jax.experimental import pallas as pl
from jax.experimental.pallas import tpu as pltpu
from jax.sharding import PartitionSpec as P

HEAD_DIM = 64
WINDOW = 1024
CAP = 768
ROW_TILE = 16
QB = 256
CHUNK = 256
EPS = 1e-06
NEG = -1e30
F32 = jnp.float32
BF16 = jnp.bfloat16
I32 = jnp.int32
VMEM_LIMIT = 56 * 1024 * 1024
GELU_A = math.sqrt(2.0 / math.pi)
GELU_B = 0.044715
NEAR = 3


def dot_nn(a, b):
    return lax.dot_general(a, b, (((1,), (0,)), ((), ())), preferred_element_type=F32)


def dot_nt(a, b):
    return lax.dot_general(a, b, (((1,), (1,)), ((), ())), preferred_element_type=F32)


def dot_tn(a, b):
    return lax.dot_general(a, b, (((0,), (0,)), ((), ())), preferred_element_type=F32)


def params(*semantics):
    return pltpu.CompilerParams(dimension_semantics=semantics, vmem_limit_bytes=VMEM_LIMIT)


def whole(shape):
    zeros = (0,) * len(shape)
    return pl.BlockSpec(shape, lambda *_: zeros)


def next_on_cycle(i):
    y, z = i % 2, i // 2
    return jnp.where(y == 0, jnp.where(z < 3, i + 2, i + 1), jnp.where(z > 0, i - 2, i - 1))


def before_on_cycle(i):
    y, z = i % 2, i // 2
    return jnp.where(y == 0, jnp.where(z > 0, i - 2, i + 1), jnp.where(z < 3, i + 2, i - 1))


def remote(src, dst, sems, k, peer):
    send, recv = sems
    return pltpu.make_async_remote_copy(
        src_ref=src, dst_ref=dst, send_sem=send.at[k], recv_sem=recv.at[k], device_id=peer,
        device_id_type=pl.DeviceIdType.MESH,
    )


def greet(peers):
    barrier = pltpu.get_barrier_semaphore()
    for peer in peers:
        pl.semaphore_signal(barrier, inc=1, device_id=peer, device_id_type=pl.DeviceIdType.MESH)
    pl.semaphore_wait(barrier, len(peers))


def attend_rows(blk, lo_ref, q_s, k_s, vt_s, mixed_ref, lse_ref, finish):
    heads = q_s.shape[0]
    most = WINDOW // QB + 1

    def window(nk):
        start = pl.multiple_of((blk - (nk - 1)) * QB, QB)
        rows = pl.ds(pl.multiple_of(blk * QB, QB), QB)
        keys = pl.ds(start, nk * QB)
        lo = lo_ref[:, rows]
        kpos = start + lax.broadcasted_iota(I32, (nk * QB, QB), 0)
        qpos = blk * QB + lax.broadcasted_iota(I32, (QB, QB), 1)
        outs = []
        for h in range(heads):
            s = dot_nt(k_s[h, keys, :], q_s[h, rows, :])
            s = jnp.where(kpos >= lo, s, NEG)
            last = jnp.where(kpos[(nk - 1) * QB :] <= qpos, s[(nk - 1) * QB :], NEG)
            s = last if nk == 1 else jnp.concatenate([s[: (nk - 1) * QB], last], axis=0)
            top = jnp.max(s, axis=0, keepdims=True)
            p = jnp.exp(s - top)
            total = jnp.sum(p, axis=0, keepdims=True)
            outs.append(dot_nn(vt_s[h, :, keys], p.astype(BF16)) / total)
            lse_ref[h : h + 1, rows] = top + jnp.log(total)
        mixed_t = jnp.concatenate(outs, axis=0).astype(BF16)
        mixed_ref[:, rows] = mixed_t
        finish(mixed_t)

    for nk in range(1, most + 1):
        cond = (blk == nk - 1) if nk < most else (blk >= most - 1)

        @pl.when(cond)
        def _(nk=nk):
            window(nk)


SLOT_ORDER = (3, 2, 1, 0)
STEPS = 9
NAMES = (
    "n_over", "n_side", "n_far", "m_over", "m_side", "m_far", "a_far", "a_own", "b_over"
)


def forward_kernel(heads, ring, tok_ref, cot_ref, gain1_ref, gain2_ref, cat_ref, lo_ref, far_ref, near_ref, xn_out, moe_out, cot_out,
                   mixed_ref, lse_ref, hid_ref, wcat_out, far_out, near_out, xn_s, q_s, k_s, vt_s, part_s, side_s, over_s, moe_s, wcat_ref, send_sem,
                   recv_sem, local_sem):
    micro, part, width = tok_ref.shape
    seq = part * 4
    cols = heads * 3 * HEAD_DIM
    per = part // QB
    nq = seq // QB
    step = pl.program_id(0)
    m = step // STEPS
    t = step % STEPS
    me = lax.axis_index("tp").astype(I32)
    side = {"tp": me ^ 1}
    over = {"tp": me ^ 2}
    sems = (send_sem, recv_sem)
    mine = pl.ds(pl.multiple_of(me * part, part), part)
    theirs = pl.ds(pl.multiple_of((me ^ 2) * part, part), part)

    def copy(name, k):
        table = {
            "n_over": (0, xn_s.at[k, mine], xn_s.at[k, mine], over),
            "n_side": (1, xn_s.at[k, mine], xn_s.at[k, mine], side),
            "n_far": (2, xn_s.at[k, theirs], xn_s.at[k, theirs], side),
            "m_over": (6, moe_s.at[k], moe_out.at[k, 3], over),
            "m_side": (7, moe_s.at[k], moe_out.at[k, 0], side),
            "m_far": (8, moe_out.at[k, 3], moe_out.at[k, 1], side),
            "a_far": (9, part_s.at[k, 3], side_s.at[k, 0], side),
            "a_own": (10, part_s.at[k, 1], side_s.at[k, 1], side),
            "b_over": (11, part_s.at[k, 2], over_s.at[k], over),
        }
        at, source, target, peer = table[name]
        return remote(source, target, sems, 12 * k + at, peer)

    def keep(at, k):
        source, target = ((cot_ref.at[k], cot_out.at[k]), (moe_s.at[k], moe_out.at[k, 2]), (xn_s.at[k], xn_out.at[k]))[at]
        return pltpu.make_async_copy(source, target, local_sem.at[3 * k + at])

    if ring:
        here = lax.axis_index("fsdp").astype(I32)
        ahead, behind = next_on_cycle(here), before_on_cycle(here)
        rows = cat_ref.shape[0]

        def hop(k, source, peer):
            at = pl.ds(pl.multiple_of(source * rows, rows), rows)
            return remote(wcat_ref.at[at], wcat_ref.at[at], sems, 24 + k, peer)

        far_rows = far_ref.shape[2]

        chains = far_ref.shape[0]
        onward = (chains + 1) // 2

        def far_hop(c, k, source, peer):
            at = pl.ds(pl.multiple_of(source * far_rows, far_rows), far_rows)
            held = far_ref.at[c] if k < 2 else far_out.at[c, :, at]
            return remote(held, far_out.at[c, :, at], sems, 31 + 7 * c + k, peer)

        def chain_starts(first, last):
            for c in range(min(first, chains), min(last, chains)):
                far_hop(c, 0, here, {"fsdp": ahead}).start()
                far_hop(c, 1, here, {"fsdp": behind}).start()

        def far_last(c, one, two):
            return far_hop(c, 6, one, {"fsdp": ahead}) if c < onward else far_hop(c, 6, two, {"fsdp": behind})

        def far_own():
            at = pl.ds(pl.multiple_of(here * far_rows, far_rows), far_rows)
            return pltpu.make_async_copy(far_ref, far_out.at[:, :, at], local_sem.at[7])

        def along(k):
            one, two = here, here
            for _ in range(k):
                one, two = before_on_cycle(one), next_on_cycle(two)
            return one, two

    tiles = part // 128

    @pl.when(step == 0)
    def _():
        peers = [side, over]
        if ring:
            peers += [{"fsdp": ahead}, {"fsdp": behind}]
        greet(peers)
        if ring:
            wcat_ref[pl.ds(pl.multiple_of(here * rows, rows), rows), :] = cat_ref[...]
            hop(0, here, {"fsdp": ahead}).start()
            hop(1, here, {"fsdp": behind}).start()
            far_own().start()
            chain_starts(0, 1)
        else:
            wcat_ref[...] = cat_ref[...]
        for k in range(micro):
            def body(i, _, k=k):
                at = pl.ds(pl.multiple_of(i * 128, 128), 128)
                x = tok_ref[k, at, :].astype(F32)
                r = lax.rsqrt(jnp.mean(x * x, axis=1, keepdims=True) + EPS)
                xn_s[k, pl.ds(pl.multiple_of(me * part + i * 128, 128), 128), :] = (x * r * gain1_ref[...]).astype(BF16)
                return 0

            lax.fori_loop(0, tiles, body, 0)
            if k == 0:
                c = 0
                copy("n_over", c).start()
                copy("n_side", c).start()
        if ring:
            one, two = here, here
            for k in range(1, 4):
                one, two = before_on_cycle(one), next_on_cycle(two)
                hop(2 * k - 2, one, {"fsdp": ahead}).wait_recv()
                hop(2 * k, one, {"fsdp": ahead}).start()
                hop(2 * k - 1, two, {"fsdp": behind}).wait_recv()
                if k < 3:
                    hop(2 * k + 1, two, {"fsdp": behind}).start()
                chain_starts(k, k + 1)
        copy("n_over", 0).wait_recv()
        copy("n_far", 0).start()
        copy("n_over", 1).start()
        copy("n_side", 1).start()
        if ring:
            hop(6, before_on_cycle(one), {"fsdp": ahead}).wait_recv()
            chain_starts(4, chains)
        copy("n_side", 0).wait_recv()
        copy("n_far", 0).wait_recv()
        for k in range(micro):
            keep(0, k).start()

    @pl.when(step == STEPS)
    def _():
        c = 1
        copy("n_side", c).wait_recv()
        copy("n_far", c).wait_recv()

    @pl.when((t == 0) & (m < micro))
    def _():
        def body(i, _):
            at = pl.ds(pl.multiple_of(i * QB, QB), QB)
            proj = dot_nn(xn_s[m, at, :], wcat_ref[:, :cols]).astype(BF16)
            for h in range(heads):
                base = h * 3 * HEAD_DIM
                q_s[h, at, :] = proj[:, base : base + HEAD_DIM] * 0.125
                k_s[h, at, :] = proj[:, base + HEAD_DIM : base + 2 * HEAD_DIM]
                vt_s[h, :, at] = proj[:, base + 2 * HEAD_DIM : base + 3 * HEAD_DIM].T
            return 0

        lax.fori_loop(0, nq, body, 0)

    @pl.when((t > 0) & (m < micro))
    def _():
        at = t - 1
        slot = 3 - at // per
        blk = (me ^ slot) * per + at % per

        def finish(mixed_t):
            rows = pl.ds(pl.multiple_of(at % per * QB, QB), QB)
            part_s[m, slot, rows, :] = dot_nt(mixed_t.T, wcat_ref[:, cols:]).astype(BF16)

        attend_rows(blk, lo_ref.at[m], q_s, k_s, vt_s, mixed_ref.at[m], lse_ref.at[m], finish)

    for k in range(micro):
        first = k * STEPS
        c = k

        @pl.when(step == first + per)
        def _(c=c):
            copy("a_far", c).start()

        @pl.when(step == first + 2 * per)
        def _(c=c, k=k):
            copy("a_far", c).wait_recv()
            part_s[k, 2] = (part_s[k, 2].astype(F32) + side_s[k, 0].astype(F32)).astype(BF16)
            copy("b_over", c).start()
            if k == 0:
                copy("n_over", 1).wait_recv()
                copy("n_far", 1).start()
            else:
                copy("m_over", 0).wait_recv()
                copy("m_far", 0).start()

        @pl.when(step == first + 3 * per)
        def _(c=c, k=k):
            copy("a_own", c).start()
        @pl.when(step == first + 4 * per)
        def _(c=c, k=k):
            copy("a_own", c).wait_recv()
            copy("b_over", c).wait_recv()

            def body(i, _):
                at = pl.ds(pl.multiple_of(i * 128, 128), 128)
                hid = (
                    tok_ref[k, at, :].astype(F32) + part_s[k, 0, at, :].astype(F32)
                    + side_s[k, 1, at, :].astype(F32) + over_s[k, at, :].astype(F32)
                )
                hid_ref[k, at, :] = hid
                r = lax.rsqrt(jnp.mean(hid * hid, axis=1, keepdims=True) + EPS)
                moe_s[k, at, :] = (hid * r * gain2_ref[...]).astype(BF16)
                return 0

            lax.fori_loop(0, tiles, body, 0)
            copy("m_over", c).start()
            copy("m_side", c).start()
            keep(1, c).start()
            keep(2, c).start()

    if ring:
        for turn in range(3 * chains):
            k, c = turn // chains + 1, turn % chains

            @pl.when(step == 2 + turn * 16 // (3 * chains))
            def _(k=k, c=c):
                one, two = along(k)
                far_hop(c, 2 * k - 2, one, {"fsdp": ahead}).wait_recv()
                far_hop(c, 2 * k - 1, two, {"fsdp": behind}).wait_recv()
                if k < 3:
                    far_hop(c, 2 * k, one, {"fsdp": ahead}).start()
                    far_hop(c, 2 * k + 1, two, {"fsdp": behind}).start()
                else:
                    far_last(c, one, two).start()

    def keep_near():
        return pltpu.make_async_copy(near_ref, near_out, local_sem.at[8])

    def keep_w():
        return pltpu.make_async_copy(wcat_ref, wcat_out, local_sem.at[6])

    @pl.when(step == STEPS)
    def _():
        keep_w().start()
        keep_near().start()

    @pl.when(step == 2 * STEPS)
    def _():
        c, d = 0, 1
        keep_w().wait()
        keep_near().wait()
        copy("m_over", d).wait_recv()
        copy("m_far", d).start()
        for e in (c, d):
            copy("m_side", e).wait_recv()
            copy("m_far", e).wait_recv()
            for name in NAMES:
                copy(name, e).wait_send()
            for at in range(3):
                keep(at, e).wait()
        if ring:
            one, two = here, here
            for k in range(4):
                hop(2 * k, one, {"fsdp": ahead}).wait_send()
                for c in range(chains):
                    if k < 3:
                        far_hop(c, 2 * k, one, {"fsdp": ahead}).wait_send()
                        far_hop(c, 2 * k + 1, two, {"fsdp": behind}).wait_send()
                    else:
                        far_last(c, one, two).wait_send()
                if k < 3:
                    hop(2 * k + 1, two, {"fsdp": behind}).wait_send()
                one, two = before_on_cycle(one), next_on_cycle(two)
            far_own().wait()
            for c in range(chains):
                far_last(c, one, two).wait_recv()


def forward_half(tokens, cotangent, gain1, gain2, cat, low, far, near, ring):
    micro, part, width = tokens.shape
    seq = part * 4
    wide = cat.shape[1]
    heads = wide // (4 * HEAD_DIM)
    hc = heads * HEAD_DIM
    anywhere = pl.BlockSpec(memory_space=pl.ANY)
    return pl.pallas_call(
        lambda *refs: forward_kernel(heads, ring, *refs),
        grid=(2 * STEPS + 1,),
        in_specs=[whole(tokens.shape), anywhere, whole((1, width)), whole((1, width)), whole(cat.shape), whole(low.shape), anywhere, anywhere],
        out_specs=[anywhere, anywhere, anywhere, whole((micro, hc, seq)), whole((micro, 8, seq)),
                   whole((micro, part, width)), anywhere, anywhere, anywhere],
        out_shape=[
            jax.ShapeDtypeStruct((micro, seq, width), BF16),
            jax.ShapeDtypeStruct((micro, 4, part, width), BF16),
            jax.ShapeDtypeStruct((micro, part, width), BF16),
            jax.ShapeDtypeStruct((micro, hc, seq), BF16),
            jax.ShapeDtypeStruct((micro, 8, seq), F32),
            jax.ShapeDtypeStruct((micro, part, width), F32),
            jax.ShapeDtypeStruct((width, wide), BF16),
            jax.ShapeDtypeStruct(far.shape[:2] + (width, far.shape[3]) if ring else (8, 128), BF16),
            jax.ShapeDtypeStruct(near.shape, BF16),
        ],
        scratch_shapes=[
            pltpu.VMEM((micro, seq, width), BF16),
            pltpu.VMEM((heads, seq, HEAD_DIM), BF16),
            pltpu.VMEM((heads, seq, HEAD_DIM), BF16),
            pltpu.VMEM((heads, HEAD_DIM, seq), BF16),
            pltpu.VMEM((micro, 4, part, width), BF16),
            pltpu.VMEM((micro, 2, part, width), BF16),
            pltpu.VMEM((micro, part, width), BF16),
            pltpu.VMEM((micro, part, width), BF16),
            pltpu.VMEM((width, wide), BF16),
            pltpu.SemaphoreType.DMA((31 + 7 * far.shape[0],)),
            pltpu.SemaphoreType.DMA((31 + 7 * far.shape[0],)),
            pltpu.SemaphoreType.DMA((9,)),
        ],
        compiler_params=pltpu.CompilerParams(
            dimension_semantics=("arbitrary",), vmem_limit_bytes=VMEM_LIMIT, collective_id=1, has_side_effects=True
        ),
        cost_estimate=pl.CostEstimate(flops=100_000_000_000, bytes_accessed=100_000_000, transcendentals=0),
        name="forward_half",
    )(tokens, cotangent, gain1, gain2, cat, low, far, near)


def run_copy(n, src, src_at, dst, dst_at, sem, act):
    n = pl.multiple_of(n, ROW_TILE)

    @pl.when(n > 0)
    def _():
        copy = pltpu.make_async_copy(
            src.at[pl.ds(pl.multiple_of(src_at, ROW_TILE), n), :],
            dst.at[pl.ds(pl.multiple_of(dst_at, ROW_TILE), n), :],
            sem,
        )
        if act == "start":
            copy.start()
        else:
            copy.wait()


def sort_rows(experts, tables, xs_ref, xl, sems, values):
    n_ref, lo_ref, off_ref = tables
    step = pl.program_id(0)
    slot = step % 2

    def moves(at, slot, act):
        for e in range(experts):
            run_copy(n_ref[at, e], xl.at[slot], lo_ref[at, e], xs_ref.at[e], off_ref[at, e], sems.at[slot, e], act)

    @pl.when(step >= 2)
    def _():
        moves(step - 2, slot, "wait")

    xl[slot] = values()
    moves(step, slot, "start")

    @pl.when(step == pl.num_programs(0) - 1)
    def _():
        moves(step - 1, 1 - slot, "wait")
        moves(step, slot, "wait")


def dispatch_kernel(experts, n_ref, lo_ref, off_ref, x_ref, rt_ref, pos_ref, xs_ref, meta_ref, xl, sems):
    rows = xl.shape[1]
    part = x_ref.shape[1]
    x = x_ref[0]
    logits = dot_nt(rt_ref[...], x)
    spots = pos_ref[0]
    p0, p1, r0, r1 = spots[0:1], spots[1:2], spots[2:3], spots[3:4]
    names = lax.broadcasted_iota(I32, logits.shape, 0)
    first = jnp.sum(jnp.where(names == r0, logits, 0.0), axis=0, keepdims=True)
    second = jnp.sum(jnp.where(names == r1, logits, 0.0), axis=0, keepdims=True)
    g0 = 1.0 / (1.0 + jnp.exp(second - first))
    g1 = 1.0 / (1.0 + jnp.exp(first - second))
    pick = lax.broadcasted_iota(I32, (8, part), 0)
    meta_ref[0] = jnp.where(
        pick == 0, p0.astype(F32), jnp.where(pick == 1, p1.astype(F32), jnp.where(pick == 2, g0, g1))
    )
    spot = lax.broadcasted_iota(I32, (rows, part), 0)
    plain = jnp.where((spot == p0) | (spot == p1), 1.0, 0.0).astype(BF16)
    sort_rows(experts, (n_ref, lo_ref, off_ref), xs_ref, xl, sems, lambda: dot_nn(plain, x).astype(BF16))


def gated_kernel(experts, n_ref, lo_ref, off_ref, side_ref, far_ref, own_ref, over_ref, meta_ref, gs_ref, c_s, xl, in_sems,
                 sems):
    step = pl.program_id(0)
    slot = step % 2
    rows = xl.shape[1]
    part = c_s.shape[1]

    def load(s):
        for t, ref in enumerate((side_ref, far_ref, own_ref, over_ref)):
            @pl.when(s % 4 == t)
            def _(ref=ref):
                pltpu.make_async_copy(ref.at[s // 4], c_s.at[s % 2], in_sems.at[s % 2]).start()

    @pl.when(step == 0)
    def _():
        load(step)

    @pl.when(step < pl.num_programs(0) - 1)
    def _():
        load(step + 1)

    meta = meta_ref[0]
    spot = lax.broadcasted_iota(I32, (rows, part), 0).astype(F32)
    gated = jnp.where(
        spot == meta[0:1], meta[2:3], jnp.where(spot == meta[1:2], meta[3:4], 0.0)
    ).astype(BF16)
    pltpu.make_async_copy(own_ref.at[0], c_s.at[slot], in_sems.at[slot]).wait()
    sort_rows(experts, (n_ref, lo_ref, off_ref), gs_ref, xl, sems, lambda: dot_nn(gated, c_s[slot]).astype(BF16))


def local_rows(part, experts):
    return -(-(2 * part + experts * (ROW_TILE - 1)) // 128) * 128


def dispatch(tables, xs, router_t, spots, most):
    count, part, width = xs.shape
    experts = router_t.shape[0]
    rows = local_rows(part, experts)
    spec = pltpu.PrefetchScalarGridSpec(
        num_scalar_prefetch=3,
        grid=(count,),
        in_specs=[
            pl.BlockSpec((1, part, width), lambda i, *_: (i, 0, 0)),
            whole(router_t.shape),
            pl.BlockSpec((1, 8, part), lambda i, *_: (i, 0, 0)),
        ],
        out_specs=[pl.BlockSpec(memory_space=pl.ANY), pl.BlockSpec((1, 8, part), lambda i, *_: (i, 0, 0))],
        scratch_shapes=[pltpu.VMEM((2, rows, width), BF16), pltpu.SemaphoreType.DMA((2, experts))],
    )
    return pl.pallas_call(
        lambda *refs: dispatch_kernel(experts, *refs),
        grid_spec=spec,
        out_shape=[
            jax.ShapeDtypeStruct((experts, most, width), BF16),
            jax.ShapeDtypeStruct((count, 8, part), F32),
        ],
        compiler_params=params("arbitrary"),
        cost_estimate=pl.CostEstimate(flops=20_000_000_000, bytes_accessed=20_000_000, transcendentals=0),
        name="dispatch",
    )(*tables, xs, router_t, spots)


def dispatch_gated(tables, parts, meta, experts, most, deps):
    _, part, width = parts[0].shape
    count = meta.shape[0]
    rows = local_rows(part, experts)
    anywhere = pl.BlockSpec(memory_space=pl.ANY)
    spec = pltpu.PrefetchScalarGridSpec(
        num_scalar_prefetch=3,
        grid=(count,),
        in_specs=[anywhere] * 4 + [pl.BlockSpec((1, 8, part), lambda i, *_: (i, 0, 0))] + [anywhere] * len(deps),
        out_specs=anywhere,
        scratch_shapes=[
            pltpu.VMEM((2, part, width), BF16),
            pltpu.VMEM((2, rows, width), BF16),
            pltpu.SemaphoreType.DMA((2,)),
            pltpu.SemaphoreType.DMA((2, experts)),
        ],
    )
    return pl.pallas_call(
        lambda *refs: gated_kernel(experts, *refs[:8], *refs[8 + len(deps) :]),
        grid_spec=spec,
        out_shape=jax.ShapeDtypeStruct((experts, most, width), BF16),
        compiler_params=params("arbitrary"),
        cost_estimate=pl.CostEstimate(flops=20_000_000_000, bytes_accessed=20_000_000, transcendentals=0),
        name="dispatch_gated",
    )(*tables, *parts, meta, *deps)


def live_rows(ref, c, tot):
    live = c * CHUNK + lax.broadcasted_iota(I32, ref.shape[1:], 0) < tot
    return jnp.where(live, ref[0], jnp.zeros((), BF16))


def expert_forward_kernel(e_ref, c_ref, tot_ref, steps_ref, xs_ref, w_ref, od_ref, pre_ref):
    i = pl.program_id(0)

    @pl.when(i < steps_ref[0])
    def _():
        x = live_rows(xs_ref, c_ref[i], tot_ref[e_ref[i]])
        pre = dot_nn(x, w_ref[0, 0])
        pre_ref[0] = pre
        t = jnp.tanh(GELU_A * pre * (1.0 + GELU_B * (pre * pre)))
        act = (0.5 * pre * (1.0 + t)).astype(BF16)
        od_ref[0] = dot_nt(act, w_ref[0, 1]).astype(BF16)


def expert_backward_kernel(split, e_ref, c_ref, tot_ref, steps_ref, out_ref, xs_ref, gs_ref, pre_ref, w_ref, od_ref, *refs):
    dw_refs, (din_s, dout_s) = refs[:-2], refs[-2:]
    i = pl.program_id(0)

    @pl.when(i < steps_ref[0])
    def _():
        e = e_ref[i]
        c = c_ref[i]
        tot = tot_ref[e]
        width = xs_ref.shape[2]
        x = live_rows(xs_ref, c, tot)
        g = live_rows(gs_ref, c, tot)
        pre = pre_ref[0]
        dact = dot_nn(g, w_ref[0, 1])
        square = pre * pre
        t = jnp.tanh(GELU_A * pre * (1.0 + GELU_B * square))
        half = 0.5 * (1.0 + t)
        act = pre * half
        slope = half + (0.5 * GELU_A) * pre * (1.0 - t * t) * (1.0 + (3.0 * GELU_B) * square)
        act_low = act.astype(BF16)
        dpre = (slope * dact).astype(BF16)
        od_ref[0, :, :width] = dot_nt(dpre, w_ref[0, 0]).astype(BF16)
        dot_row = jnp.sum(act * dact, axis=1, keepdims=True)
        lane = lax.broadcasted_iota(I32, (CHUNK, 128), 1)
        od_ref[0, :, width:] = jnp.where(lane == e, dot_row, 0.0).astype(BF16)
        last = (c + 1) * CHUNK >= tot

        @pl.when(c == 0)
        def _():
            din_s[...] = dot_tn(x, dpre)
            dout_s[...] = dot_tn(g, act_low)

        if split:
            @pl.when(c > 0)
            def _():
                din_s[...] += dot_tn(x, dpre)
                dout_s[...] += dot_tn(g, act_low)

            @pl.when(last)
            def _():
                count, rows = dw_refs[0].shape[2:4]
                for which, ref in enumerate(dw_refs):
                    for k in range(count):
                        at = pl.ds(pl.multiple_of(out_ref[which * count + k] * rows, rows), rows)
                        ref[0, 0, k] = din_s[at, :].astype(BF16)
                        ref[0, 1, k] = dout_s[at, :].astype(BF16)
        else:
            @pl.when((c > 0) & jnp.logical_not(last))
            def _():
                din_s[...] += dot_tn(x, dpre)
                dout_s[...] += dot_tn(g, act_low)

            @pl.when((c > 0) & last)
            def _():
                dw_refs[0][0, 0] = (din_s[...] + dot_tn(x, dpre)).astype(BF16)
                dw_refs[0][0, 1] = (dout_s[...] + dot_tn(g, act_low)).astype(BF16)

            @pl.when((c == 0) & last)
            def _():
                dw_refs[0][0, 0] = din_s[...].astype(BF16)
                dw_refs[0][0, 1] = dout_s[...].astype(BF16)


def chunk_list(first, group, totals, chunks):
    need = jnp.maximum((totals[first : first + group] + CHUNK - 1) // CHUNK, 1)
    ends = jnp.cumsum(need)
    at = jnp.minimum(jnp.arange(group * chunks, dtype=I32), ends[-1] - 1)
    which = jnp.sum((at[:, None] >= ends[None, :]).astype(I32), axis=1)
    begin = jnp.sum(jnp.where(which[:, None] == jnp.arange(group), (ends - need)[None, :], 0), axis=1)
    return which + first, at - begin, totals, ends[-1:]


def experts_forward(first, listed, xs, weights, deps=()):
    group, _, width, hidden = weights.shape
    most = xs.shape[1]
    spec = pltpu.PrefetchScalarGridSpec(
        num_scalar_prefetch=4,
        grid=(group * (most // CHUNK),),
        in_specs=[
            pl.BlockSpec((1, CHUNK, width), lambda i, e, c, *_: (e[i], c[i], 0)),
            pl.BlockSpec((1, 2, width, hidden), lambda i, e, c, *_: (e[i] - first, 0, 0, 0)),
        ] + [pl.BlockSpec(memory_space=pl.ANY)] * len(deps),
        out_specs=[
            pl.BlockSpec((1, CHUNK, width), lambda i, e, c, *_: (e[i] - first, c[i], 0)),
            pl.BlockSpec((1, CHUNK, hidden), lambda i, e, c, *_: (e[i] - first, c[i], 0)),
        ],
    )
    return pl.pallas_call(
        lambda *refs: expert_forward_kernel(*refs[:6], *refs[6 + len(deps) :]),
        grid_spec=spec,
        out_shape=[
            jax.ShapeDtypeStruct((group, most, width), BF16),
            jax.ShapeDtypeStruct((group, most, hidden), F32),
        ],
        compiler_params=params("arbitrary"),
        cost_estimate=pl.CostEstimate(flops=group * 6_000_000_000, bytes_accessed=group * 10_000_000, transcendentals=0),
        name="experts_forward",
    )(*listed, xs, weights, *deps)


def experts_backward(first, listed, xs, gs, pre, weights, out_order, split, deps=()):
    group, _, width, hidden = weights.shape
    most = xs.shape[1]
    if split:
        half = (group, 2, out_order.shape[0] // 2, width // out_order.shape[0], hidden)
        dw_shapes = [half, half]
        dw_specs = [pl.BlockSpec((1,) + half[1:], lambda i, e, c, *_: (e[i] - first, 0, 0, 0, 0))] * 2
    else:
        dw_shapes = [weights.shape]
        dw_specs = [pl.BlockSpec((1, 2, width, hidden), lambda i, e, c, *_: (e[i] - first, 0, 0, 0))]
    spec = pltpu.PrefetchScalarGridSpec(
        num_scalar_prefetch=5,
        grid=(group * (most // CHUNK),),
        in_specs=[
            pl.BlockSpec((1, CHUNK, width), lambda i, e, c, *_: (e[i], c[i], 0)),
            pl.BlockSpec((1, CHUNK, width), lambda i, e, c, *_: (e[i], c[i], 0)),
            pl.BlockSpec((1, CHUNK, hidden), lambda i, e, c, *_: (e[i] - first, c[i], 0)),
            pl.BlockSpec((1, 2, width, hidden), lambda i, e, c, *_: (e[i] - first, 0, 0, 0)),
        ] + [pl.BlockSpec(memory_space=pl.ANY)] * len(deps),
        out_specs=[pl.BlockSpec((1, CHUNK, width + 128), lambda i, e, c, *_: (e[i] - first, c[i], 0))] + dw_specs,
        scratch_shapes=[pltpu.VMEM((width, hidden), F32), pltpu.VMEM((width, hidden), F32)],
    )
    return pl.pallas_call(
        lambda *refs: expert_backward_kernel(split, *refs[:9], *refs[9 + len(deps) :]),
        grid_spec=spec,
        out_shape=[jax.ShapeDtypeStruct((group, most, width + 128), BF16)]
        + [jax.ShapeDtypeStruct(shape, BF16) for shape in dw_shapes],
        compiler_params=params("arbitrary"),
        cost_estimate=pl.CostEstimate(flops=group * 10_000_000_000, bytes_accessed=group * 10_000_000, transcendentals=0),
        name="experts_backward",
    )(*listed, out_order, xs, gs, pre, weights, *deps)


def combine_kernel(starts, gated, n_ref, lo_ref, off_ref, *refs):
    od_refs = refs[: len(starts) - 1]
    meta_ref, send_ref, keep_ref, od_l, sems = refs[-5:]
    step = pl.program_id(0)
    slot = step % 2
    rows = od_l.shape[1]
    part = meta_ref.shape[2]

    def moves(at, slot, act):
        for e in range(starts[-1]):
            group = max(i for i, s in enumerate(starts[:-1]) if s <= e)
            n, dst, src = n_ref[at, e], lo_ref[at, e], off_ref[at, e]
            run_copy(n, od_refs[group].at[e - starts[group]], src, od_l.at[slot], dst, sems.at[slot, e], act)

    @pl.when(step == 0)
    def _():
        od_l[...] = jnp.zeros_like(od_l)
        moves(0, 0, "start")

    @pl.when(step < pl.num_programs(0) - 1)
    def _():
        moves(step + 1, 1 - slot, "start")

    meta = meta_ref[0].T
    p0, p1, g0, g1 = (meta[:, i : i + 1] for i in range(4))
    spot = lax.broadcasted_iota(I32, (part, rows), 1).astype(F32)
    is0 = spot == p0
    is1 = spot == p1
    if gated:
        pick = jnp.where(is0, g0, jnp.where(is1, g1, 0.0)).astype(BF16)
    else:
        pick = jnp.where(is0 | is1, 1.0, 0.0).astype(BF16)
    moves(step, slot, "wait")
    out = dot_nn(pick, od_l[slot]).astype(BF16)

    @pl.when(step % 4 < 2)
    def _():
        send_ref[0] = out

    @pl.when(step % 4 >= 2)
    def _():
        keep_ref[0] = out


def combine(tables, ods, meta, gated, deps=()):
    starts = [0]
    for od in ods:
        starts.append(starts[-1] + od.shape[0])
    experts = starts[-1]
    wide = ods[0].shape[2]
    count, _, part = meta.shape
    rows = local_rows(part, experts)
    anywhere = pl.BlockSpec(memory_space=pl.ANY)
    spec = pltpu.PrefetchScalarGridSpec(
        num_scalar_prefetch=3,
        grid=(count,),
        in_specs=[anywhere] * (len(ods) + len(deps)) + [pl.BlockSpec((1, 8, part), lambda i, *_: (i, 0, 0))],
        out_specs=[
            pl.BlockSpec((1, part, wide), lambda i, *_: (i // 4, jnp.minimum(i % 4, 1), 0)),
            pl.BlockSpec((1, part, wide), lambda i, *_: (i // 4, jnp.maximum(i % 4 - 2, 0), 0)),
        ],
        scratch_shapes=[pltpu.VMEM((2, rows, wide), BF16), pltpu.SemaphoreType.DMA((2, experts))],
    )
    return pl.pallas_call(
        lambda *refs: combine_kernel(starts, gated, *refs),
        grid_spec=spec,
        out_shape=[jax.ShapeDtypeStruct((count // 4, 2 * part, wide), BF16)] * 2,
        compiler_params=params("arbitrary"),
        cost_estimate=pl.CostEstimate(flops=20_000_000_000, bytes_accessed=20_000_000, transcendentals=0),
        name="combine",
    )(*tables, *ods, *deps, meta)


def routing(routes, capacity, me, part):
    micro = routes.shape[0]
    experts = capacity.shape[0]
    picks = routes.reshape(micro, 4, part, 2).transpose(0, 1, 3, 2)
    names = jnp.arange(experts, dtype=I32)[:, None]
    named = picks[:, :, :, None, :] == names
    either = named[:, :, 0] | named[:, :, 1]
    earlier = jnp.arange(part)[:, None] < jnp.arange(part)[None, :]
    before = jnp.einsum("mbet,ts->mbes", either.astype(BF16), earlier.astype(BF16), preferred_element_type=F32)
    before = before.astype(I32)
    count = jnp.sum(either.astype(I32), axis=3)
    carry = jnp.cumsum(count, axis=1) - count
    kept = jnp.clip(capacity[None, None, :] - carry, 0, count)
    n = (kept + ROW_TILE - 1) // ROW_TILE * ROW_TILE
    lo = jnp.cumsum(n, axis=2) - n
    place = jnp.where(before < kept[..., None], lo[..., None] + before, -1)
    pos = jnp.max(jnp.where(named, place[:, :, None], -1), axis=3)
    order = me ^ jnp.array([1, 3, 0, 2], I32)
    spots = jnp.concatenate([pos, picks, jnp.zeros_like(pos), jnp.zeros_like(pos)], axis=2)
    spots = jnp.take(spots, order, axis=1)
    n = jnp.take(n, order, axis=1)
    lo = jnp.take(lo, order, axis=1)
    flat = n.reshape(micro * 4, experts)
    off = (jnp.cumsum(flat, axis=0) - flat).reshape(n.shape)
    return n, lo, off, jnp.sum(flat, axis=0), spots


def split_low(v):
    high = v.astype(BF16)
    return high, (v - high.astype(F32)).astype(BF16)


BACK = 34
FAR_STEPS = (3, 6, 10, 17, 20, 23, 28, 32)
BACK_NAMES = (
    "a_dx", "a_own", "b_dx", "g_over", "g_side", "g_far", "p_far", "p_own", "p_over"
)


def backward_kernel(heads, ring, dxs, dxk, hid_ref, cot_ref, tok_ref, moe_ref, xn_ref,
                    gain1_ref, gain2_ref, router_ref, full_ref, w_ref, lo_ref, mixed_ref, lse_ref, wsend_ref, wkeep_ref,
                    gt_ref, cat_out, small_out, wy_ref, wz_ref, wo_ref, wl0_ref, wl1_ref, wl2_ref, adx_s, bdx_s, kp_s, hid_s, cot_s, moe_s, g_s,
                    part_s, xn_s, q_s, k_s, kt_s, v_s, dqt_s, dkt_s, dvt_s, dcat_s, small_s, cat_s, caty_s, catz_s, sm_s,
                    stage_s, send_sem, recv_sem, load_sem):
    micro, part, width = tok_ref.shape
    seq = part * 4
    cols = heads * 3 * HEAD_DIM
    per = part // QB
    nq = seq // QB
    step = pl.program_id(0)
    me = lax.axis_index("tp").astype(I32)
    side = {"tp": me ^ 1}
    over = {"tp": me ^ 2}
    sems = (send_sem, recv_sem)
    wl_refs = (wl0_ref, wl1_ref, wl2_ref)
    mine = pl.ds(pl.multiple_of(me * part, part), part)
    theirs = pl.ds(pl.multiple_of((me ^ 2) * part, part), part)
    top, low = pl.ds(0, part), pl.ds(part, part)
    flat = pl.ds(0, width)

    def copy(name, k):
        table = {
            "a_dx": (0, dxs.at[k, low], adx_s.at[k, low], side),
            "a_own": (2, dxs.at[k, top], adx_s.at[k, top], side),
            "b_dx": (1, adx_s.at[k, low], bdx_s.at[k], over),
            "g_over": (4, g_s.at[k, mine], g_s.at[k, mine], over),
            "g_side": (5, g_s.at[k, mine], g_s.at[k, mine], side),
            "g_far": (6, g_s.at[k, theirs], g_s.at[k, theirs], side),
            "p_far": (7, part_s.at[3], adx_s.at[k, top, flat], side),
            "p_own": (8, part_s.at[1], adx_s.at[k, low, flat], side),
            "p_over": (9, part_s.at[2], bdx_s.at[k, :, flat], over),
        }
        at, source, target, peer = table[name]
        return remote(source, target, sems, 10 * k + at, peer)

    def load(name, k):
        table = {
            "keep": (0, dxk.at[k], kp_s),
            "hid": (1, hid_ref.at[k], hid_s),
            "cot": (2, cot_ref.at[k], cot_s),
            "moe": (3, moe_ref.at[k, 2], moe_s),
            "xn": (4, xn_ref.at[k], xn_s),
            "tok": (2, tok_ref.at[k], cot_s),
        }
        at, source, target = table[name]
        return pltpu.make_async_copy(source, target, load_sem.at[at])

    def start(names, k):
        for name in names:
            load(name, k).start()

    def wait(names, k):
        for name in names:
            load(name, k).wait()

    def rows_of(i):
        return pl.ds(pl.multiple_of(i * 128, 128), 128)

    def half_sum(k):
        copy("a_dx", k).wait_recv()
        wait(("keep",), k)

        def body(i, _):
            at = pl.ds(pl.multiple_of(part + i * 128, 128), 128)
            adx_s[k, at, :] = (adx_s[k, at, :].astype(F32) + kp_s[at, :].astype(F32)).astype(BF16)
            return 0

        lax.fori_loop(0, part // 128, body, 0)
        copy("b_dx", k).start()

    def hidden_grad(k):
        copy("a_own", k).wait_recv()
        copy("b_dx", k).wait_recv()
        wait(("hid", "cot", "moe"), k)

        def body(i, _):
            at = rows_of(i)
            total = adx_s[k, at, :].astype(F32) + kp_s[at, :].astype(F32) + bdx_s[k, at, :].astype(F32)
            products = total[:, width:]
            glog = products - full_ref[k, at, :] * jnp.sum(products, axis=1, keepdims=True)
            high, rest = split_low(glog)
            moe = moe_s[at, :]
            small_s[0:8, :] += (dot_tn(high, moe) + dot_tn(rest, moe))[0:8]
            gm = total[:, :width] + dot_nt(high, router_ref[...]) + dot_nt(rest, router_ref[...])
            hid = hid_s[at, :]
            r = lax.rsqrt(jnp.mean(hid * hid, axis=1, keepdims=True) + EPS)
            u = gm * gain2_ref[...]
            grad = cot_s[at, :].astype(F32) + r * u - hid * (r * r * r * jnp.mean(u * hid, axis=1, keepdims=True))
            small_s[16:24, :] += jnp.sum((gm * hid * r).reshape(16, 8, width), axis=0)
            g_s[k, pl.ds(pl.multiple_of(me * part + i * 128, 128), 128), :] = grad.astype(BF16)
            return 0

        lax.fori_loop(0, part // 128, body, 0)
        copy("b_dx", k).wait_send()
        copy("g_over", k).start()
        copy("g_side", k).start()

    def token_grad(k):
        copy("p_own", k).wait_recv()
        copy("p_over", k).wait_recv()
        wait(("tok",), k)

        def body(i, _):
            at = rows_of(i)
            gn = (
                part_s[0, at, :].astype(F32)
                + adx_s[k, pl.ds(pl.multiple_of(part + i * 128, 128), 128), flat].astype(F32)
                + bdx_s[k, at, flat].astype(F32)
            )
            x = cot_s[at, :].astype(F32)
            r = lax.rsqrt(jnp.mean(x * x, axis=1, keepdims=True) + EPS)
            w = gn * gain1_ref[...]
            back = r * w - x * (r * r * r * jnp.mean(w * x, axis=1, keepdims=True))
            mine_at = pl.ds(pl.multiple_of(me * part + i * 128, 128), 128)
            gt_ref[k, at, :] = (g_s[k, mine_at, :].astype(F32) + back).astype(BF16)
            return 0

        lax.fori_loop(0, part // 128, body, 0)

    if ring:
        here = lax.axis_index("fsdp").astype(I32)
        pair = {"fsdp": here ^ 1}
        line = [{"fsdp": here ^ (2 * k)} for k in range(1, 4)]
        tp_peers = [{"tp": me ^ k} for k in range(1, 4)]

        def extra(name, k=0):
            table = {
                "cat_y": (20, lambda: (cat_s, caty_s, pair)),
                "cat_z": (21 + k, lambda: (cat_s.at[k + 1], catz_s.at[k], line[k])),
                "sm_tp": (24 + k, lambda: (small_s, sm_s.at[k], tp_peers[k])),
                "sm_y": (27, lambda: (small_s, sm_s.at[3], pair)),
                "sm_z": (28 + k, lambda: (small_s, sm_s.at[4 + k], line[k])),
            }
            at, parts = table[name]
            return remote(*parts()[:2], sems, at, parts()[2])

        pieces_w = wy_ref.shape[0]

        def far_y(i):
            return remote(wsend_ref.at[i], wy_ref.at[i], sems, 31 + i, pair)

        def far_z(i, k):
            return remote(wz_ref.at[i, k], wl_refs[k].at[i], sems, 31 + pieces_w + 3 * i + k, line[k])

        def far_load(i, which):
            source = wkeep_ref.at[i] if which == 0 else wy_ref.at[i]
            return pltpu.make_async_copy(source, stage_s.at[which], load_sem.at[8 + which])

        def far_store(i):
            return (
                pltpu.make_async_copy(stage_s.at[2, 1:4], wz_ref.at[i], load_sem.at[10]),
                pltpu.make_async_copy(stage_s.at[2, 0], wo_ref.at[i], load_sem.at[11]),
            )

        def far_first(i):
            far_y(i).wait_recv()
            if i + 4 < pieces_w:
                far_y(i + 4).start()
            far_load(i, 0).start()
            far_load(i, 1).start()

        def far_second(i):
            far_load(i, 0).wait()
            far_load(i, 1).wait()
            for k in range(4):
                stage_s[2, k] = (stage_s[0, k].astype(F32) + stage_s[1, k].astype(F32)).astype(BF16)
            for store in far_store(i):
                store.start()

        def far_third(i):
            for store in far_store(i):
                store.wait()
            for k in range(3):
                far_z(i, k).start()

    def project():
        def body(i, _):
            rows = pl.ds(pl.multiple_of(i * QB, QB), QB)
            proj = dot_nn(xn_s[rows, :], w_ref[:, :cols]).astype(BF16)
            for h in range(heads):
                base = h * 3 * HEAD_DIM
                q_s[h, rows, :] = proj[:, base : base + HEAD_DIM] * 0.125
                k_new = proj[:, base + HEAD_DIM : base + 2 * HEAD_DIM]
                k_s[h, rows, :] = k_new
                kt_s[h, :, rows] = k_new.T
                v_s[h, rows, :] = proj[:, base + 2 * HEAD_DIM : base + 3 * HEAD_DIM]
            return 0

        lax.fori_loop(0, nq, body, 0)

    def far_piece(i):
        if ring and i < wy_ref.shape[0]:
            far_first(i)
            far_second(i)
            far_third(i)

    @pl.when(step == 0)
    def _():
        peers = [side, over]
        if ring:
            peers += [pair] + line + [tp_peers[2]]
        greet(peers)
        copy("a_dx", 0).start()
        copy("a_own", 0).start()
        start(("keep", "hid", "cot", "moe", "xn"), 0)
        dcat_s[...] = jnp.zeros_like(dcat_s)
        small_s[...] = jnp.zeros_like(small_s)
        dkt_s[...] = jnp.zeros_like(dkt_s)
        dvt_s[...] = jnp.zeros_like(dvt_s)
        half_sum(0)
        copy("a_dx", 1).start()
        copy("a_own", 1).start()
        if ring:
            for i in range(min(4, pieces_w)):
                far_y(i).start()
        wait(("xn",), 0)
        project()
        far_piece(0)
        hidden_grad(0)
        start(("keep", "hid", "cot", "moe"), 1)
        far_piece(1)
        far_piece(2)
        copy("g_over", 0).wait_recv()
        copy("g_far", 0).start()
        half_sum(1)
        far_piece(3)
        copy("g_side", 0).wait_recv()
        copy("g_far", 0).wait_recv()

    def attend(m, blk):
        rows = pl.ds(pl.multiple_of(blk * QB, QB), QB)
        most = WINDOW // QB + 1

        def window(nk):
            begin = pl.multiple_of((blk - (nk - 1)) * QB, QB)
            keys = pl.ds(begin, nk * QB)
            g = g_s[m, rows, :]
            gm_t = dot_nn(g, w_ref[:, cols:]).astype(BF16).T
            mixed_t = mixed_ref[m, :, rows]
            dcat_s[cols:, :] += dot_nn(mixed_t, g)
            prod = gm_t.astype(F32) * mixed_t.astype(F32)
            lo = lo_ref[m, :, rows]
            kpos = begin + lax.broadcasted_iota(I32, (nk * QB, QB), 0)
            qpos = blk * QB + lax.broadcasted_iota(I32, (QB, QB), 1)
            for h in range(heads):
                at = slice(h * HEAD_DIM, (h + 1) * HEAD_DIM)
                q = q_s[h, rows, :]
                drow = jnp.sum(prod[at], axis=0, keepdims=True)
                s = dot_nt(k_s[h, keys, :], q)
                s = jnp.where(kpos >= lo, s, NEG)
                last = jnp.where(kpos[(nk - 1) * QB :] <= qpos, s[(nk - 1) * QB :], NEG)
                s = last if nk == 1 else jnp.concatenate([s[: (nk - 1) * QB], last], axis=0)
                p = jnp.exp(s - lse_ref[m, h : h + 1, rows])
                dp = dot_nn(v_s[h, keys, :], gm_t[at])
                ds = (p * (dp - drow)).astype(BF16)
                dvt_s[h, :, keys] += dot_nt(gm_t[at], p.astype(BF16))
                dkt_s[h, :, keys] += dot_nt(q.T, ds)
                dqt_s[h, :, rows] = (dot_nn(kt_s[h, :, keys], ds) * 0.125).astype(BF16)

        for nk in range(1, most + 1):
            cond = (blk == nk - 1) if nk < most else (blk >= most - 1)

            @pl.when(cond)
            def _(nk=nk):
                window(nk)

    def finalize(m, at):
        slot = 3 - at // per
        blk = (me ^ slot) * per + at % per
        rows = pl.ds(pl.multiple_of(blk * QB, QB), QB)
        pieces = []
        for h in range(heads):
            pieces += [dqt_s[h, :, rows], dkt_s[h, :, rows].astype(BF16), dvt_s[h, :, rows].astype(BF16)]
            dkt_s[h, :, rows] = jnp.zeros((HEAD_DIM, QB), F32)
            dvt_s[h, :, rows] = jnp.zeros((HEAD_DIM, QB), F32)
        dproj_t = jnp.concatenate(pieces, axis=0)
        x = xn_s[rows, :]
        dcat_s[:cols, :] += dot_nn(dproj_t, x)
        gn = dot_nt(dproj_t.T, w_ref[:, :cols])
        small_s[8:16, :] += jnp.sum((gn * x.astype(F32)).reshape(QB // 8, 8, width), axis=0)
        part_s[slot, pl.ds(pl.multiple_of(at % per * QB, QB), QB), :] = gn.astype(BF16)

    phase = (step - 1) // nq
    m_now = phase // 2

    @pl.when((step > 0) & (step < BACK - 1) & (phase % 2 == 0))
    def _():
        attend(m_now, (step - 1) % nq)

    @pl.when((step > 0) & (step < BACK - 1) & (phase % 2 == 1))
    def _():
        finalize(m_now, (step - 1) % nq)

    def event(at):
        return pl.when(step == at)

    if ring:
        for i, first in zip(range(4, pieces_w), FAR_STEPS):
            @event(first)
            def _(i=i):
                far_first(i)

            @event(first + 1)
            def _(i=i):
                far_second(i)

            @event(min(first + 2, BACK - 1))
            def _(i=i):
                far_third(i)

    @event(5)
    def _():
        hidden_grad(1)

    @event(10)
    def _():
        copy("g_over", 1).wait_recv()
        copy("g_far", 1).start()

    for k in range(micro):
        first = 16 * k + nq

        @event(first + per)
        def _(k=k):
            copy("p_far", k).start()

        @event(first + 2 * per)
        def _(k=k):
            copy("p_far", k).wait_recv()

            def body(i, _):
                at = rows_of(i)
                part_s[2, at, :] = (part_s[2, at, :].astype(F32) + adx_s[k, at, flat].astype(F32)).astype(BF16)
                return 0

            lax.fori_loop(0, part // 128, body, 0)
            copy("p_over", k).start()

        @event(first + 3 * per)
        def _(k=k):
            copy("p_own", k).start()

    @event(16)
    def _():
        start(("xn",), 1)
        copy("g_side", 1).wait_recv()
        copy("g_far", 1).wait_recv()
        start(("tok",), 0)
        wait(("xn",), 1)
        project()

    @event(20)
    def _():
        token_grad(0)
        start(("tok",), 1)
        for name in ("p_far", "p_own", "p_over"):
            copy(name, 0).wait_send()

    @event(BACK - 1)
    def _():
        if ring:
            dcat = dcat_s[...].T
            dcat_s[...] = dcat
            rows = width // 8
            y, z = here % 2, here // 2

            def block(k, parity):
                at = pl.multiple_of((2 * (z ^ k) + parity) * rows, rows)
                return dcat_s[pl.ds(at, rows), :]

            for k in range(4):
                cat_s[k] = block(k, 1 - y).astype(BF16)
            extra("cat_y").start()
            for k in range(3):
                extra("sm_tp", k).start()
            extra("cat_y").wait()
            for k in range(4):
                cat_s[k] = (block(k, y) + caty_s[k].astype(F32)).astype(BF16)
            for k in range(3):
                extra("cat_z", k).start()
            for k in range(3):
                extra("sm_tp", k).wait()
            small_s[...] = (small_s[...] + sm_s[0]) + (sm_s[1] + sm_s[2])
            extra("sm_y").start()
            extra("sm_y").wait()
            small_s[...] += sm_s[3]
            for k in range(3):
                extra("sm_z", k).start()
            for k in range(3):
                extra("sm_z", k).wait()
            small_out[...] = (small_s[...] + sm_s[4]) + (sm_s[5] + sm_s[6])
            for k in range(3):
                extra("cat_z", k).wait()
            token_grad(1)
            cat_out[...] = (
                cat_s[0].astype(F32) + catz_s[0].astype(F32) + catz_s[1].astype(F32) + catz_s[2].astype(F32)
            )
        else:
            token_grad(1)
            small_out[...] = small_s[...]
            cat_out[...] = dcat_s[...].T
        if ring:
            for i in range(pieces_w):
                far_y(i).wait_send()
                for k in range(3):
                    far_z(i, k).wait()
        for k in range(micro):
            for name in BACK_NAMES:
                if name != "b_dx" and not (k == 0 and name in ("p_far", "p_own", "p_over")):
                    copy(name, k).wait_send()


def backward_half(dxs, dxk, hidden, cotangent, tokens, moe, xn, gain1, gain2, router, full, w_cat, low, mixed_t,
                  lse, wsend, wkeep, ring, deps=()):
    micro, part, width = tokens.shape
    seq = part * 4
    wide = w_cat.shape[1]
    heads = wide // (4 * HEAD_DIM)
    hc = heads * HEAD_DIM
    dxw = dxs.shape[2]
    pieces, block = (wsend.shape[0], wsend.shape[1:]) if ring else (1, (8, 128))
    anywhere = pl.BlockSpec(memory_space=pl.ANY)

    def once(shape):
        zeros = (0,) * len(shape)
        return pl.BlockSpec(shape, lambda *_: zeros, pipeline_mode=pl.Buffered(1))

    cat_shape = (width // 8, wide) if ring else (width, wide)
    return pl.pallas_call(
        lambda *refs: backward_kernel(heads, ring, *refs[:17], *refs[17 + len(deps) :]),
        grid=(BACK,),
        in_specs=[anywhere] * 7 + [
            once((1, width)), once((1, width)), once(router.shape), once(full.shape), once(w_cat.shape), once(low.shape),
            once(mixed_t.shape), once(lse.shape),
        ] + [anywhere] * (2 + len(deps)),
        out_specs=[once((micro, part, width)), once(cat_shape), once((24, width))] + [anywhere] * 6,
        out_shape=[
            jax.ShapeDtypeStruct((micro, part, width), BF16),
            jax.ShapeDtypeStruct(cat_shape, F32),
            jax.ShapeDtypeStruct((24, width), F32),
            jax.ShapeDtypeStruct((pieces,) + block, BF16),
            jax.ShapeDtypeStruct((pieces, 3) + block[1:], BF16),
        ] + [jax.ShapeDtypeStruct((pieces,) + block[1:], BF16)] * 4,
        scratch_shapes=[
            pltpu.VMEM((micro, 2 * part, dxw), BF16),
            pltpu.VMEM((micro, part, dxw), BF16),
            pltpu.VMEM((2 * part, dxw), BF16),
            pltpu.VMEM((part, width), F32),
            pltpu.VMEM((part, width), BF16),
            pltpu.VMEM((part, width), BF16),
            pltpu.VMEM((micro, seq, width), BF16),
            pltpu.VMEM((4, part, width), BF16),
            pltpu.VMEM((seq, width), BF16),
            pltpu.VMEM((heads, seq, HEAD_DIM), BF16),
            pltpu.VMEM((heads, seq, HEAD_DIM), BF16),
            pltpu.VMEM((heads, HEAD_DIM, seq), BF16),
            pltpu.VMEM((heads, seq, HEAD_DIM), BF16),
            pltpu.VMEM((heads, HEAD_DIM, seq), BF16),
            pltpu.VMEM((heads, HEAD_DIM, seq), F32),
            pltpu.VMEM((heads, HEAD_DIM, seq), F32),
            pltpu.VMEM((wide, width), F32),
            pltpu.VMEM((24, width), F32),
            pltpu.VMEM((4, width // 8, wide), BF16),
            pltpu.VMEM((4, width // 8, wide), BF16),
            pltpu.VMEM((3, width // 8, wide), BF16),
            pltpu.VMEM((7, 24, width), F32),
            pltpu.VMEM((3,) + block, BF16),
            pltpu.SemaphoreType.DMA((31 + 4 * pieces,)),
            pltpu.SemaphoreType.DMA((31 + 4 * pieces,)),
            pltpu.SemaphoreType.DMA((12,)),
        ],
        compiler_params=pltpu.CompilerParams(
            dimension_semantics=("arbitrary",), vmem_limit_bytes=60 * 1024 * 1024, collective_id=2, has_side_effects=True
        ),
        cost_estimate=pl.CostEstimate(flops=150_000_000_000, bytes_accessed=100_000_000, transcendentals=0),
        name="backward_half",
    )(dxs, dxk, hidden, cotangent, tokens, moe, xn, gain1, gain2, router, full, w_cat, low, mixed_t, lse, wsend, wkeep, *deps)


def local(tokens, cotangent, gain_attn, gain_moe, qkv_weight, out_weight, router, w_in, w_out, doc_lengths, routes,
          capacity):
    micro, part, width = tokens.shape
    seq = part * 4
    experts = w_in.shape[0]
    n_fsdp = lax.axis_size("fsdp")
    ring = n_fsdp == 8
    me = lax.axis_index("tp").astype(I32)
    most = -(-micro * (CAP + 4 * ROW_TILE) // CHUNK) * CHUNK
    cat = jnp.concatenate([qkv_weight, out_weight.T], axis=1)
    w_pair = jnp.stack([w_in, w_out.transpose(0, 2, 1)], axis=1)
    if ring:
        row_index = lax.axis_index("fsdp").astype(I32)
        near = 2 * ((row_index // 2) ^ jnp.arange(4, dtype=I32))
        out_order = jnp.concatenate([near + row_index % 2, near + (1 - row_index % 2)])
    else:
        cat = lax.all_gather(cat, "fsdp", axis=0, tiled=True)
        out_order = jnp.zeros((1,), I32)
    near, far = w_pair[:NEAR], w_pair[NEAR:]

    n, lo_at, off, totals, spots = routing(routes, capacity, me, part)
    places = jnp.arange(seq, dtype=I32)
    ends = jnp.cumsum(doc_lengths.reshape(micro, -1), axis=1)
    begins = ends - doc_lengths.reshape(micro, -1)
    doc_start = jnp.max(jnp.where(places >= begins[:, :, None], begins[:, :, None], 0), axis=1)
    low = jnp.maximum(doc_start, places - (WINDOW - 1)).astype(I32)
    router_t = router.T

    low = low[:, None, :]
    xn, moe, cot, mixed_t, lse, hidden, w_cat, w_far, near = forward_half(
        tokens, cotangent, gain_attn[None], gain_moe[None], cat, low, far, near, ring
    )
    w_near = lax.all_gather(near, "fsdp", axis=2, tiled=True)
    if not ring:
        w_far = lax.all_gather(far, "fsdp", axis=2, tiled=True)
    core, chip = [(i, i ^ 1) for i in range(4)], [(i, i ^ 2) for i in range(4)]
    cot_over = lax.ppermute(cot, "tp", chip)
    cot_side = lax.ppermute(cot, "tp", core)
    cot_far = lax.ppermute(cot_over, "tp", core)
    blocks = micro * 4
    tables = tuple(table.reshape(blocks, experts) for table in (n, lo_at, off))
    xs, meta = dispatch(tables, moe.reshape(blocks, part, width), router_t, spots.reshape(blocks, 8, part), most)
    list_near = chunk_list(0, NEAR, totals, most // CHUNK)
    list_far = chunk_list(NEAR, experts - NEAR, totals, most // CHUNK)
    fwd_far, pre_far = experts_forward(NEAR, list_far, xs, w_far)
    gs = dispatch_gated(tables, (cot_side, cot_far, cot, cot_over), meta, experts, most, (fwd_far,))
    fwd_near, pre_near = experts_forward(0, list_near, xs, w_near, (gs,))
    out_send, out_keep = combine(tables, (fwd_near, fwd_far), meta, True)
    out_got = lax.ppermute(out_send, "tp", core)
    out_both = out_keep.astype(F32) + out_got.astype(F32)
    out_away = lax.ppermute(out_both[:, part:].astype(BF16), "tp", chip)
    output = (hidden + out_both[:, :part] + out_away.astype(F32)).astype(BF16)
    back_near, dw_near = experts_backward(0, list_near, xs, gs, pre_near, w_near, out_order, False)
    dw_near = lax.psum_scatter(dw_near, "fsdp", scatter_dimension=2, tiled=True).astype(F32)
    back_far, *dw_far = experts_backward(NEAR, list_far, xs, gs, pre_far, w_far, out_order, ring, (back_near, out_both))
    if ring:
        wkeep, wsend = (d.reshape((-1,) + d.shape[2:]) for d in dw_far)
    else:
        dw_far = lax.psum_scatter(dw_far[0], "fsdp", scatter_dimension=2, tiled=True).astype(F32)
        wkeep = wsend = jnp.zeros((8, 128), BF16)

    lanes = jnp.arange(128, dtype=I32)
    mine = lax.dynamic_slice_in_dim(routes, me * part, part, 1)
    gates = meta.reshape(micro, 4, 8, part)[:, 2, 2:4]
    full = jnp.sum(jnp.where(mine[..., None] == lanes, gates.transpose(0, 2, 1)[..., None], 0.0), axis=2)
    router_wide = jnp.pad(router, ((0, 0), (0, 128 - experts)))
    dxs, dxk = combine(tables, (back_near, back_far), meta, False)
    grad_tokens, grad_cat, small, _, _, *shares = backward_half(
        dxs, dxk, hidden, cotangent, tokens, moe, xn, gain_attn[None], gain_moe[None], router_wide, full, w_cat, low, mixed_t,
        lse, wsend, wkeep, ring, (output,)
    )
    cols = qkv_weight.shape[1]
    if not ring:
        grad_cat = lax.psum_scatter(grad_cat.astype(BF16), "fsdp", scatter_dimension=0, tiled=True).astype(F32)
        small = lax.psum(small, ("fsdp", "tp"))
    if ring:
        dw_far = sum(share.astype(F32) for share in shares)
        dw_far = dw_far.reshape((experts - NEAR, 2) + dw_far.shape[1:])
    dw = jnp.concatenate([dw_near, dw_far], axis=0)
    return (
        output,
        grad_tokens,
        jnp.sum(small[8:16], axis=0) / gain_attn,
        jnp.sum(small[16:24], axis=0),
        grad_cat[:, :cols],
        grad_cat[:, cols:].T,
        small[:8].T,
        dw[:, 0],
        dw[:, 1].transpose(0, 2, 1),
    )


def solution(mesh):
    rows = P(None, ("fsdp", "tp"), None)
    in_specs = (
        rows,
        rows,
        P(),
        P(),
        P("fsdp", "tp"),
        P("tp", "fsdp"),
        P(),
        P(None, "fsdp", "tp"),
        P(None, "tp", "fsdp"),
        P(None, "fsdp", None),
        P(None, "fsdp", None),
        P(),
    )
    out_specs = (
        rows,
        rows,
        P(),
        P(),
        P("fsdp", "tp"),
        P("tp", "fsdp"),
        P(),
        P(None, "fsdp", "tp"),
        P(None, "tp", "fsdp"),
    )
    return jax.shard_map(local, mesh=mesh, in_specs=in_specs, out_specs=out_specs, check_vma=False)
```
